32 devices in a mesh: dp: 8 (over y, x, core), tensor: 4 (over z).
Axes of the slice: x: 2, y: 2, z: 4, core: 2. Of those that a mesh axis runs over, the one named last changes fastest.
Arguments:
- layer_input: bfloat16 [2048, 2048], P('dp'), may hold values from -20 to 20
- doc_ids: int32 [2048], P('dp'), may hold values from 0 to 2047, as said below
- expert_ids: int32 [2048, 4], P('dp'), may hold values from 0 to 7, all different within a row; in each aligned block of 256 rows (0 to 255, 256 to 511, ...) at most 192 rows name the same one
- route_weights: float32 [2048, 4], P('dp'), may hold values from 0.05 to 0.6
- attn_gain: bfloat16 [2048], replicated, may hold values from 0.5 to 1.5
- qkv_weight: bfloat16 [2048, 6144], P(None, 'tensor'), may hold values from -0.125 to 0.125
- qkv_bias: bfloat16 [16, 384], P('tensor'), may hold values from -2 to 2
- out_weight: bfloat16 [2048, 2048], P('tensor'), may hold values from -0.5 to 0.5
- mlp_gain: bfloat16 [2048], replicated, may hold values from 0.5 to 1.5
- expert_gate_up: bfloat16 [8, 2048, 2, 1408], P(None, None, None, 'tensor'), may hold values from -0.125 to 0.125
- expert_down: bfloat16 [8, 1408, 2048], P(None, 'tensor'), may hold values from -0.15625 to 0.15625
- shared_gate_up: bfloat16 [2048, 2, 5632], P(None, None, 'tensor'), may hold values from -0.125 to 0.125
- shared_down: bfloat16 [5632, 2048], P('tensor'), may hold values from -0.078125 to 0.078125
- shared_gate: bfloat16 [2048], replicated, may hold values from -0.125 to 0.125
- cotangent: bfloat16 [2048, 2048], P('dp'), may hold values from -6 to 6
Outputs:
- layer_output: bfloat16 [2048, 2048], P('dp')
- input_grad: bfloat16 [2048, 2048], P('dp')
- attn_gain_grad: float32 [2048], P('dp')
- qkv_weight_grad: float32 [2048, 6144], P('dp', 'tensor')
- qkv_bias_grad: float32 [16, 384], P('tensor', 'dp')
- out_weight_grad: float32 [2048, 2048], P('tensor', 'dp')
- mlp_gain_grad: float32 [2048], P('dp')
- expert_gate_up_grad: float32 [8, 2048, 2, 1408], P(None, 'dp', None, 'tensor')
- expert_down_grad: float32 [8, 1408, 2048], P(None, 'tensor', 'dp')
- shared_gate_up_grad: float32 [2048, 2, 5632], P('dp', None, 'tensor')
- shared_down_grad: float32 [5632, 2048], P('tensor', 'dp')
- shared_gate_grad: float32 [2048], P('dp')
The draws below stay inside these ranges and needn't reach their ends.
Inputs may be any that keep to these rules, and one draw needn't show every extreme that they name: `doc_ids`: never falling; a sequence's label is the index of its first token; every block of 256 tokens (one index of dp) begins a new sequence, so no sequence crosses blocks; a sequence has 1 to 256 tokens, one has exactly 256, and the last token forms a sequence of its own. `expert_ids`: each row names 4 different experts; within the rows of one device no expert is named by more than 192 rows, a bound that some block reaches.
All inputs are finite; a program needn't handle non-finite values.
Results may differ from the reference program's by a relative error of at most 0.015.
Values sent between devices are 32-bit elements; how exact they have to be, the bound alone decides.
No kernel may reach another device: no remote copies, remote signals or barrier semaphores. Data moves between devices by JAX's collectives and lax.ppermute only.
A program may use at most 384 MiB of HBM per device.

```python
import math
import jax
import jax.numpy as jnp
import numpy as np
from jax import lax

D = 2048
HEADS = 16
HEAD_DIM = 128
FE = 1408
FS = 5632
TOPK = 4
E = 8
TOK_DEV = 256
TOKENS = 2048
CAP = 192
N_DP = 8


def draw_layer_input(key, part):
    key_rows, key_cols, key_body = jax.random.split(key, 3)
    row_scale = jnp.exp(jax.random.uniform(key_rows, (TOKENS, 1), jnp.float32, math.log(0.3), math.log(3.0)))
    col_scale = jnp.exp(jax.random.uniform(key_cols, (1, D), jnp.float32, math.log(0.3), math.log(3.0)))
    base_draw = jnp.clip(jax.random.normal(key_body, (TOKENS, D), jnp.float32), -6.0, 6.0)
    return jnp.clip(base_draw * row_scale * col_scale, -20.0, 20.0).astype(jnp.bfloat16)


def draw_doc_ids(key, part):
    key_rate, key_full, key_cuts = jax.random.split(key, 3)
    blocks_all = TOKENS // TOK_DEV
    position = jnp.arange(TOKENS, dtype=jnp.int32)
    owner = position // TOK_DEV
    within = position % TOK_DEV
    rate_draw = jax.random.randint(key_rate, (blocks_all,), 0, 6)
    full_block = jax.random.randint(key_full, (), 0, blocks_all - 1)
    rate_draw = jnp.where(jnp.arange(blocks_all, dtype=jnp.int32) == full_block, 0, rate_draw)
    cut_draw = jax.random.randint(key_cuts, (TOKENS,), 0, TOK_DEV)
    begins = (within == 0) | (cut_draw < rate_draw[owner]) | (position == TOKENS - 1)
    first = lax.cummax(jnp.where(begins, position, jnp.zeros_like(position)), axis=0)
    return first.astype(jnp.int32)


def raised(array, stream_key, source, target, parts, factor):
    owner, partner = [(jnp.arange(array.shape[dim]) // (array.shape[dim] // parts)).reshape([-1 if axis == dim else 1 for axis in range(array.ndim)]) for dim in (source, target)]
    chosen = jax.random.permutation(stream_key, parts)[partner]
    strong = (owner == chosen) | (owner == (partner + parts // 2) % parts)
    return jnp.where(strong, factor * array, array)


def block_scale(own_key, extent, cuts, least, largest):
    level, own = 1.0, jax.random.fold_in(own_key, 6)
    for dim, blocks in cuts:
        draws = jnp.exp(jax.random.uniform(jax.random.fold_in(own, dim), (blocks,), jnp.float32, least / len(cuts), largest / len(cuts)))
        level = level * jnp.repeat(draws, extent[dim] // blocks).reshape([-1 if axis == dim else 1 for axis in range(len(extent))])
    return level


def deal_out(rng, own, number, rows, number_of, top, most, slope):
    ranking = jax.random.permutation(rng, number_of)
    packed, common = portions_of(number_of, rows * top, most, slope, True), portions_of(number_of, rows * top, most, slope, False)
    places = jnp.arange(number_of)

    def named(lengths, turn):
        used = int((lengths > 0).sum())
        fixed = max(1, used // 4)
        passed = fixed + (places - fixed + turn * (used - fixed)) % max(1, number_of - fixed)
        return jnp.zeros((number_of,), jnp.int32).at[ranking[jnp.where(places < fixed, places, passed)]].set(jnp.asarray(lengths, jnp.int32))

    lengths = jnp.where(number % 4 == 0, named(packed, number // 4), named(common, number - number // 4 - 1))
    mixed = jax.random.permutation(jax.random.fold_in(own, 3), number_of)
    giver, receiver = mixed[0:number_of // 2 * 2:2], mixed[1:number_of // 2 * 2:2]
    room = jnp.minimum(lengths[giver] - 1, most - lengths[receiver]) // 2
    room = jnp.where((giver == ranking[0]) | (receiver == ranking[0]) | (lengths[receiver] == 0), 0, jnp.maximum(room, 0))
    passed = jax.random.randint(jax.random.fold_in(own, 4), (number_of // 2,), 0, 1 << 20) % (room + 1)
    lengths = lengths.at[giver].add(-passed).at[receiver].add(passed)
    items = jnp.searchsorted(jnp.cumsum(lengths), jnp.arange(rows * top), side="right").astype(jnp.int32)
    grid = items.reshape(top, rows).T
    grid = grid[jax.random.permutation(jax.random.fold_in(own, 1), rows)]
    turn = jax.random.randint(jax.random.fold_in(own, 2), (rows, 1), 0, top)
    return jnp.take_along_axis(grid, (jnp.arange(top)[None, :] + turn) % top, axis=1)


def portions_of(amount, total, reach, lean, full):
    weights = [(1 << 20) // math.isqrt(grade ** lean) + 1 for grade in range(1, amount + 1)]
    largest = reach if full else min(reach, max(-(-total // amount), total * weights[0] // sum(weights)))
    least = 1 if total - largest >= amount - 1 else 0
    given, surplus = [largest] + [least] * (amount - 1), total - largest - least * (amount - 1)
    while surplus > 0:
        free = [i for i in range(1, amount) if given[i] < largest] or [i for i in range(1, amount) if given[i] < reach]
        whole, left = sum([weights[i] for i in free]), surplus
        for i in free:
            more = min(reach - given[i], max(1, left * weights[i] // whole), surplus)
            given[i] = given[i] + more
            surplus = surplus - more
    return np.array(given)


def scatter_about(stream_key, extent, spread, reach, shards=(), held_as=jnp.bfloat16):
    values = spread * jax.random.normal(stream_key, extent, jnp.float32)
    if shards:
        values = values * block_scale(stream_key, extent, shards, -0.22, 0.18)
    return jnp.clip(values, -reach, reach).astype(held_as)


def gaussian_with(key, shape, scale, bound, cuts, heavy, kind=jnp.bfloat16):
    drawn = scale * jax.random.normal(key, shape, jnp.float32)
    if cuts:
        drawn = drawn * block_scale(key, shape, cuts, -0.22, 0.18)
    return jnp.clip(raised(drawn, jax.random.fold_in(key, 3), *heavy), -bound, bound).astype(kind)


def setup_inputs(seed: int = 0) -> dict:
    splits = jax.random.split(jax.random.key(seed), 16)
    layer_input = draw_layer_input(jax.random.fold_in(splits[15], 71), 0)
    doc_ids = draw_doc_ids(jax.random.fold_in(splits[15], 71), 0)
    expert_ids_keys = jax.random.split(jax.random.fold_in(splits[2], 1), TOKENS // TOK_DEV)
    expert_ids_turns = jax.random.permutation(jax.random.fold_in(splits[2], 3), TOKENS // TOK_DEV)
    expert_ids = jax.vmap(lambda own, number: deal_out(jax.random.fold_in(splits[2], 2), own, number, TOK_DEV, E, TOPK, CAP, 2))(expert_ids_keys, expert_ids_turns).reshape((TOKENS, TOPK))
    route_weights = jnp.clip(0.05 + 0.55 * jax.random.uniform(splits[3], (TOKENS, TOPK), jnp.float32) ** block_scale(splits[3], (TOKENS, TOPK), ((0, 8),), -0.2, 0.2), 0.05, 0.6)
    attn_gain = jnp.clip(1.0 + 0.1 * jax.random.normal(splits[4], (D,), jnp.float32), 0.5, 1.5).astype(jnp.bfloat16)
    qkv_weight = scatter_about(splits[5], (D, HEADS * 3 * HEAD_DIM), D ** -0.5, 0.125, ((1, 4),))
    qkv_bias = scatter_about(splits[6], (HEADS, 3 * HEAD_DIM), 0.5, 2.0, ((0, 4),))
    out_weight = scatter_about(splits[7], (HEADS * HEAD_DIM, D), (HEADS * HEAD_DIM // 16) ** -0.5, 0.5, ((0, 4),))
    mlp_gain = jnp.clip(1.0 + 0.1 * jax.random.normal(splits[8], (D,), jnp.float32), 0.5, 1.5).astype(jnp.bfloat16)
    expert_gate_up = scatter_about(splits[9], (E, D, 2, FE), D ** -0.5, 0.125, ((3, 4),))
    expert_down = scatter_about(splits[10], (E, FE, D), FE ** -0.5, 0.15625, ((1, 4),))
    shared_gate_up = scatter_about(splits[11], (D, 2, FS), D ** -0.5, 0.125, ((2, 4),))
    shared_down = scatter_about(splits[12], (FS, D), FS ** -0.5, 0.078125, ((0, 4),))
    shared_gate = scatter_about(splits[13], (D,), D ** -0.5, 0.125)
    cotangent = gaussian_with(splits[14], (TOKENS, D), 1.0, 6.0, ((0, 8),), (0, 1, 8, 2.0))
    return dict(layer_input=layer_input, doc_ids=doc_ids, expert_ids=expert_ids, route_weights=route_weights, attn_gain=attn_gain, qkv_weight=qkv_weight, qkv_bias=qkv_bias, out_weight=out_weight, mlp_gain=mlp_gain, expert_gate_up=expert_gate_up, expert_down=expert_down, shared_gate_up=shared_gate_up, shared_down=shared_down, shared_gate=shared_gate, cotangent=cotangent)


EPS = 1e-06
ROPE_BASE = 1000000.0
NEG = -1e+30

@jax.custom_vjp
def low(v):
    return lax.optimization_barrier(v.astype(jnp.bfloat16)).astype(jnp.float32)

@jax.custom_vjp
def low_back(v):
    return v

def low_keep(v):
    return (low(v), None)

def low_pass(kept, grad):
    return (grad,)

def back_keep(v):
    return (v, None)

def back_low(kept, grad):
    return (low(grad),)
low.defvjp(low_keep, low_pass)
low_back.defvjp(back_keep, back_low)

def matmul(left, right):
    return jnp.dot(left, right, precision=lax.Precision.HIGHEST, preferred_element_type=jnp.float32)

def rms_norm(values_in, gain_vec):
    factor = lax.rsqrt(lax.optimization_barrier(jnp.mean(values_in * values_in, axis=-1, keepdims=True)) + EPS)
    return values_in * factor * gain_vec

def rope_tables(doc_ids):
    index = jnp.arange(TOKENS, dtype=jnp.int32)
    begins = jnp.concatenate([jnp.ones((1,), dtype=bool), doc_ids[1:] != doc_ids[:-1]])
    first = lax.cummax(jnp.where(begins, index, jnp.zeros_like(index)), axis=0)
    place = (index - first).astype(jnp.float32)
    freq = ROPE_BASE ** (-(jnp.arange(HEAD_DIM // 2, dtype=jnp.float32) * 2.0 / HEAD_DIM))
    angle = place[:, None] * freq[None, :]
    cosine = jnp.concatenate([jnp.cos(angle), jnp.cos(angle)], axis=-1)
    sine = jnp.concatenate([jnp.sin(angle), jnp.sin(angle)], axis=-1)
    return (cosine, sine)

def rotate_half(values_in):
    middle = values_in.shape[-1] // 2
    return jnp.concatenate([-values_in[..., middle:], values_in[..., :middle]], axis=-1)

def rotary_apply(values_in, cosine, sine):
    return values_in * cosine[:, None, :] + rotate_half(values_in) * sine[:, None, :]

def attend(block_in):
    queries, keys_in, values_in, docs = block_in
    scores = low_back(jnp.einsum('qhd,khd->hqk', queries, keys_in, precision=lax.Precision.HIGHEST)) * HEAD_DIM ** (-0.5)
    index = jnp.arange(TOK_DEV, dtype=jnp.int32)
    allowed = (docs[:, None] == docs[None, :]) & (index[None, :] <= index[:, None])
    scores = jnp.where(allowed[None], scores, NEG)
    probs = low(jax.nn.softmax(scores, axis=-1))
    return jnp.einsum('hqk,khd->qhd', probs, values_in, precision=lax.Precision.HIGHEST)

def reference(layer_input, doc_ids, expert_ids, route_weights, attn_gain, qkv_weight, qkv_bias, out_weight, mlp_gain, expert_gate_up, expert_down, shared_gate_up, shared_down, shared_gate, cotangent):
    cosine, sine = rope_tables(doc_ids)
    choose = (expert_ids[:, :, None] == jnp.arange(E, dtype=jnp.int32)[None, None, :]).astype(jnp.float32)
    route = lax.optimization_barrier(jnp.sum(route_weights.astype(jnp.float32)[:, :, None] * choose, axis=1))
    docs_blocked = doc_ids.reshape(N_DP, TOK_DEV)

    def forward(inputs, gain_one, weight_qkv, bias_qkv, weight_out, gain_two, expert_mixw, expert_downw, shared_mixw, shared_downw, shared_gatew):
        normed_one = low(rms_norm(inputs, gain_one))
        projected = low_back(matmul(normed_one, weight_qkv) + bias_qkv.reshape(-1))
        projected = projected.reshape(TOKENS, HEADS, 3, HEAD_DIM)
        queries = low(low_back(rotary_apply(projected[:, :, 0], cosine, sine)))
        keys_all = low(low_back(rotary_apply(projected[:, :, 1], cosine, sine)))
        values_all = low(low_back(projected[:, :, 2]))
        blocked = (queries.reshape(N_DP, TOK_DEV, HEADS, HEAD_DIM), keys_all.reshape(N_DP, TOK_DEV, HEADS, HEAD_DIM), values_all.reshape(N_DP, TOK_DEV, HEADS, HEAD_DIM), docs_blocked)
        attended = lax.map(jax.checkpoint(attend), blocked)
        attended = low(low_back(attended.reshape(TOKENS, HEADS * HEAD_DIM)))
        residual = inputs + low_back(matmul(attended, weight_out))
        normed_two = low(rms_norm(residual, gain_two))
        mixture = jnp.zeros((TOKENS, D), dtype=jnp.float32)
        for expert in range(E):
            mixed = low_back(jnp.einsum('td,dcf->tcf', normed_two, expert_mixw[expert], precision=lax.Precision.HIGHEST))
            active = low(jax.nn.silu(mixed[:, 0]) * mixed[:, 1])
            mixture = mixture + route[:, expert:expert + 1] * low_back(matmul(active, expert_downw[expert]))
        shared_mixed = low_back(jnp.einsum('td,dcf->tcf', normed_two, shared_mixw, precision=lax.Precision.HIGHEST))
        shared_active = low(jax.nn.silu(shared_mixed[:, 0]) * shared_mixed[:, 1])
        shared_out = low_back(matmul(shared_active, shared_downw))
        gate_open = jax.nn.sigmoid(matmul(normed_two, shared_gatew))
        return residual + mixture + gate_open[:, None] * shared_out
    primals = tuple((operand.astype(jnp.float32) for operand in (layer_input, attn_gain, qkv_weight, qkv_bias, out_weight, mlp_gain, expert_gate_up, expert_down, shared_gate_up, shared_down, shared_gate)))
    output, pullback = jax.vjp(forward, *primals)
    grads = pullback(cotangent.astype(jnp.float32))
    return (output.astype(jnp.bfloat16), grads[0].astype(jnp.bfloat16), grads[1], grads[2], grads[3], grads[4], grads[5], grads[6], grads[7], grads[8], grads[9], grads[10])
```

```python
import functools

import jax
import jax.numpy as jnp
from jax import lax
from jax.experimental import pallas as pl
from jax.experimental.pallas import tpu as pltpu
from jax.sharding import PartitionSpec as P

EPS = 1e-06
ROPE_BASE = 1000000.0
NEG = -1e30
F32 = jnp.float32
BF16 = jnp.bfloat16
VMEM_LIMIT = 60 * 1024 * 1024


def nt(left, right):
    return lax.dot_general(left, right, (((1,), (1,)), ((), ())), preferred_element_type=F32)


def tn(left, right):
    return lax.dot_general(left, right, (((0,), (0,)), ((), ())), preferred_element_type=F32)


def nn(left, right):
    return jnp.dot(left, right, preferred_element_type=F32)


def rms_norm(values_in, gain_vec):
    factor = lax.rsqrt(jnp.mean(values_in * values_in, axis=-1, keepdims=True) + EPS)
    return (values_in * factor * gain_vec, factor)


def norm_back(values_in, factor, gain_vec, upstream):
    scaled = gain_vec * upstream
    inner = jnp.mean(scaled * values_in, axis=-1, keepdims=True)
    return factor * scaled - values_in * factor**3 * inner


def rotate_half(values_in):
    middle = values_in.shape[-1] // 2
    return jnp.concatenate([-values_in[..., middle:], values_in[..., :middle]], axis=-1)


def rotary_apply(values_in, cosine, sine):
    return values_in * cosine[:, None, :] + rotate_half(values_in) * sine[:, None, :]


def rotary_back(upstream, cosine, sine):
    return upstream * cosine[:, None, :] - rotate_half(upstream * sine[:, None, :])


def hidden(w_one, w_two, tokens, branch, route_row):
    units = w_two.shape[0]
    mix = nt(w_one, tokens)
    gate, up = mix[:units], mix[units:]
    back = nt(w_two, branch)
    sigma = 1.0 / (1.0 + jnp.exp(-gate))
    silu = gate * sigma
    act = silu * up
    scaled = back * route_row
    gate_grad = scaled * up * sigma * (1.0 + gate * (1.0 - sigma))
    mix_grad = jnp.concatenate([gate_grad.astype(BF16), (scaled * silu).astype(BF16)], axis=0)
    return act, back, (act * route_row).astype(BF16), mix_grad


def open_row(gate_rows, tokens):
    return 1.0 / (1.0 + jnp.exp(-nt(gate_rows, tokens)[:1]))


def own_kernel(experts, tok_ref, cot_ref, route_ref, gate_ref, w1e_ref, w1s_ref, w2e_ref, w2s_ref,
               out_ref, dx_ref, logit_ref, open_ref):
    step = pl.program_id(0)
    units, width = w2e_ref.shape[-2:]

    @pl.when(step == 0)
    def _():
        out_ref[...] = jnp.zeros_like(out_ref)
        dx_ref[...] = jnp.zeros_like(dx_ref)
        logit_ref[...] = jnp.zeros_like(logit_ref)
        open_ref[...] = open_row(gate_ref[...], tok_ref[...])

    def tile(w_one, w_two, route_row, shared):
        act, back, weighted, mix_grad = hidden(w_one, w_two, tok_ref[...], cot_ref[...], route_row)
        if shared:
            logit_ref[...] += jnp.sum(act * back, axis=0, keepdims=True)
        out_ref[...] += tn(weighted, w_two)
        dx_ref[...] += tn(mix_grad, w_one)

    @pl.when(step < experts)
    def _():
        tile(w1e_ref[...].reshape(2 * units, width), w2e_ref[0], route_ref[0], False)

    @pl.when(step >= experts)
    def _():
        tile(w1s_ref[...].reshape(2 * units, width), w2s_ref[0], open_ref[...], True)

    @pl.when(step == pl.num_programs(0) - 1)
    def _():
        opened = open_ref[...]
        logit = opened * (1.0 - opened) * logit_ref[...]
        logit_ref[...] = logit
        column = jnp.broadcast_to(logit, (8, logit.shape[1])).T[:, :1]
        dx_ref[...] += column * gate_ref[:1].astype(F32)


def own_mlp(tokens, cotangent, route, gate_rows, w1e, w1s, w2e, w2s):
    count, width = tokens.shape
    experts, units = w2e.shape[:2]
    shared = w2s.shape[0]
    last = experts - 1
    whole = lambda *shape: pl.BlockSpec(shape, lambda i: (0,) * len(shape))
    expert = lambda i: jnp.minimum(i, last)
    common = lambda i: jnp.maximum(i - experts, 0)
    return pl.pallas_call(
        functools.partial(own_kernel, experts),
        grid=(experts + shared,),
        in_specs=[
            whole(count, width),
            whole(count, width),
            pl.BlockSpec((1, 1, count), lambda i: (expert(i), 0, 0)),
            whole(*gate_rows.shape),
            pl.BlockSpec((1, 2, units, width), lambda i: (expert(i), 0, 0, 0)),
            pl.BlockSpec((2, 1, units, width), lambda i: (0, common(i), 0, 0)),
            pl.BlockSpec((1, units, width), lambda i: (expert(i), 0, 0)),
            pl.BlockSpec((1, units, width), lambda i: (common(i), 0, 0)),
        ],
        out_specs=[whole(count, width), whole(count, width), whole(1, count)],
        out_shape=[
            jax.ShapeDtypeStruct((count, width), F32),
            jax.ShapeDtypeStruct((count, width), F32),
            jax.ShapeDtypeStruct((1, count), F32),
        ],
        scratch_shapes=[pltpu.VMEM((1, count), F32)],
        compiler_params=pltpu.CompilerParams(
            dimension_semantics=("arbitrary",), vmem_limit_bytes=VMEM_LIMIT
        ),
        cost_estimate=pl.CostEstimate(
            flops=2 * 6 * count * width * units * (experts + shared),
            bytes_accessed=6 * width * units * (experts + shared),
            transcendentals=count * units * (experts + shared),
        ),
        name="own_mlp",
    )(tokens, cotangent, route[:, None, :], gate_rows, w1e, w1s, w2e, w2s)


def grads_kernel(experts_here, where_ref, tok_ref, cot_ref, route_ref, gate_ref, w1e_ref, w1s_ref, w2e_ref,
                 w2s_ref, one_mine_ref, one_peer_ref, two_mine_ref, two_peer_ref):
    step = pl.program_id(0)
    units, width = w2e_ref.shape[-2:]
    blocks, _, count = route_ref.shape
    part = one_mine_ref.shape[-1]
    core = where_ref[0]
    first = pl.multiple_of(where_ref[1] * part, part)
    other = pl.multiple_of(where_ref[2] * part, part)

    for ref in (one_mine_ref, one_peer_ref, two_mine_ref, two_peer_ref):
        ref[...] = jnp.zeros_like(ref)

    def tile(w_one, w_two, row_of):
        def block(number, carry):
            rows = pl.ds(pl.multiple_of(number * count, count), count)
            tokens, branch = tok_ref[rows, :], cot_ref[rows, :]
            _, _, weighted, mix_grad = hidden(w_one, w_two, tokens, branch, row_of(number, tokens))
            for start, one_ref, two_ref in ((first, one_mine_ref, two_mine_ref), (other, one_peer_ref, two_peer_ref)):
                cols = pl.ds(start, part)
                one_ref[...] += nn(mix_grad, tok_ref[rows, cols]).reshape(one_ref.shape)
                two_ref[...] += nn(weighted, cot_ref[rows, cols]).reshape(two_ref.shape)
            return carry

        lax.fori_loop(0, blocks, block, 0)

    @pl.when(step < experts_here)
    def _():
        expert = core * experts_here + step
        tile(w1e_ref[...].reshape(2 * units, width), w2e_ref[0], lambda n, _: route_ref[n, pl.ds(expert, 1), :])

    @pl.when(step >= experts_here)
    def _():
        tile(w1s_ref[...].reshape(2 * units, width), w2s_ref[0], lambda _, tokens: open_row(gate_ref[...], tokens))


def all_grads(where, tokens, cotangent, route, gate_rows, w1e, w1s, w2e, w2s, part):
    total, width = tokens.shape
    experts, units = w2e.shape[:2]
    shared = w2s.shape[0]
    here, here_shared = experts // 2, shared // 2
    expert = lambda i, at: at[0] * here + jnp.minimum(i, here - 1)
    common = lambda i, at: at[0] * here_shared + jnp.maximum(i - here, 0)
    whole = lambda *shape: pl.BlockSpec(shape, lambda i, at: (0,) * len(shape), pipeline_mode=pl.Buffered(1))
    tiles = here + here_shared
    one = jax.ShapeDtypeStruct((tiles, 2, units, part), F32)
    two = jax.ShapeDtypeStruct((tiles, units, part), F32)
    one_spec = pl.BlockSpec((1, 2, units, part), lambda i, at: (i, 0, 0, 0))
    two_spec = pl.BlockSpec((1, units, part), lambda i, at: (i, 0, 0))
    return pl.pallas_call(
        functools.partial(grads_kernel, here),
        grid_spec=pltpu.PrefetchScalarGridSpec(
            num_scalar_prefetch=1,
            grid=(tiles,),
            in_specs=[
                whole(total, width),
                whole(total, width),
                whole(*route.shape),
                whole(*gate_rows.shape),
                pl.BlockSpec((1, 2, units, width), lambda i, at: (expert(i, at), 0, 0, 0)),
                pl.BlockSpec((2, 1, units, width), lambda i, at: (0, common(i, at), 0, 0)),
                pl.BlockSpec((1, units, width), lambda i, at: (expert(i, at), 0, 0)),
                pl.BlockSpec((1, units, width), lambda i, at: (common(i, at), 0, 0)),
            ],
            out_specs=[one_spec, one_spec, two_spec, two_spec],
        ),
        out_shape=[one, one, two, two],
        compiler_params=pltpu.CompilerParams(
            dimension_semantics=("arbitrary",), vmem_limit_bytes=VMEM_LIMIT
        ),
        cost_estimate=pl.CostEstimate(
            flops=2 * 3 * total * (width + 2 * part) * units * tiles,
            bytes_accessed=6 * width * units * tiles + 4 * total * width,
            transcendentals=total * units * tiles,
        ),
        name="all_grads",
    )(where, tokens, cotangent, route, gate_rows, w1e, w1s, w2e, w2s)


def round_kernel(in_ref, out_ref):
    out_ref[...] = in_ref[0].astype(BF16)


def rounded(gathered):
    blocks, count, width = gathered.shape
    return pl.pallas_call(
        round_kernel,
        grid=(blocks,),
        in_specs=[pl.BlockSpec((1, count, width), lambda i: (i, 0, 0))],
        out_specs=pl.BlockSpec((count, width), lambda i: (i, 0)),
        out_shape=jax.ShapeDtypeStruct((blocks * count, width), BF16),
        compiler_params=pltpu.CompilerParams(
            dimension_semantics=("arbitrary",), vmem_limit_bytes=32 * 1024 * 1024
        ),
        name="rounded",
    )(gathered)


def split_kernel(in_ref, out_ref, route_ref):
    count = out_ref.shape[0]
    out_ref[...] = in_ref[0, :count].astype(BF16)
    route_ref[...] = in_ref[0, count:, :count][None]


def split_rounded(gathered, count):
    blocks, rows, width = gathered.shape
    extra = rows - count
    return pl.pallas_call(
        split_kernel,
        grid=(blocks,),
        in_specs=[pl.BlockSpec((1, rows, width), lambda i: (i, 0, 0))],
        out_specs=[
            pl.BlockSpec((count, width), lambda i: (i, 0)),
            pl.BlockSpec((1, extra, count), lambda i: (i, 0, 0)),
        ],
        out_shape=[
            jax.ShapeDtypeStruct((blocks * count, width), BF16),
            jax.ShapeDtypeStruct((blocks, extra, count), F32),
        ],
        compiler_params=pltpu.CompilerParams(
            dimension_semantics=("arbitrary",), vmem_limit_bytes=32 * 1024 * 1024
        ),
        name="split_rounded",
    )(gathered)


def shards(
    n_dp,
    n_tensor,
    layer_input,
    doc_ids,
    expert_ids,
    route_weights,
    attn_gain,
    qkv_weight,
    qkv_bias,
    out_weight,
    mlp_gain,
    expert_gate_up,
    expert_down,
    shared_gate_up,
    shared_down,
    shared_gate,
    cotangent,
):
    count, width = layer_input.shape
    heads_here = qkv_bias.shape[0]
    head_dim = qkv_bias.shape[1] // 3
    experts, units = expert_down.shape[:2]
    shared = shared_down.shape[0] // units
    part = width // n_dp
    scale = head_dim ** (-0.5)
    me = lax.axis_index("dp")
    core = me % 2
    swap = [(i, i ^ 1) for i in range(n_dp)]

    choose = expert_ids[:, :, None] == jnp.arange(experts, dtype=jnp.int32)[None, None, :]
    route = jnp.sum(route_weights[:, :, None] * choose.astype(F32), axis=1).T
    upstream = cotangent.astype(F32)
    cot_all = lax.all_gather(
        jnp.concatenate([upstream, jnp.pad(route, ((0, 0), (0, width - count)))], axis=0), "dp"
    )
    w1e = jnp.transpose(expert_gate_up, (0, 2, 3, 1))
    w1s = jnp.transpose(shared_gate_up, (1, 2, 0)).reshape(2, shared, units, width)
    w2s = shared_down.reshape(shared, units, width)
    gate_rows = jnp.broadcast_to(shared_gate[None, :], (16, width))

    inputs = layer_input.astype(F32)
    gain_one = attn_gain.astype(F32)
    gain_two = mlp_gain.astype(F32)
    normed_one, factor_one = rms_norm(inputs, gain_one)
    normed_one_low = normed_one.astype(BF16)
    projected = nn(normed_one_low, qkv_weight) + qkv_bias.reshape(-1).astype(F32)
    projected = projected.reshape(count, heads_here, 3, head_dim)
    index = jnp.arange(count, dtype=jnp.int32)
    place = (me * count + index - doc_ids).astype(F32)
    freq = ROPE_BASE ** (-(jnp.arange(head_dim // 2, dtype=F32) * 2.0 / head_dim))
    angle = place[:, None] * freq[None, :]
    cosine = jnp.concatenate([jnp.cos(angle), jnp.cos(angle)], axis=-1)
    sine = jnp.concatenate([jnp.sin(angle), jnp.sin(angle)], axis=-1)
    query_low = rotary_apply(projected[:, :, 0], cosine, sine).astype(BF16)
    key_low = rotary_apply(projected[:, :, 1], cosine, sine).astype(BF16)
    value_low = projected[:, :, 2].astype(BF16)
    allowed = (doc_ids[:, None] == doc_ids[None, :]) & (index[None, :] <= index[:, None])
    scores = jnp.einsum("qhd,khd->hqk", query_low, key_low, preferred_element_type=F32) * scale
    scores = jnp.where(allowed[None], scores, NEG)
    exponent = jnp.exp(scores - jnp.max(scores, axis=-1, keepdims=True))
    probs = exponent / jnp.sum(exponent, axis=-1, keepdims=True)
    probs_low = probs.astype(BF16)
    attended = jnp.einsum("hqk,khd->qhd", probs_low, value_low, preferred_element_type=F32)
    attended = attended.astype(BF16).reshape(count, heads_here * head_dim)
    residual = inputs + lax.psum(nn(attended, out_weight), "tensor")
    normed_two, factor_two = rms_norm(residual, gain_two)
    normed_two_low = normed_two.astype(BF16)

    tok_all = lax.all_gather(normed_two_low.astype(F32), "dp")
    mlp_part, normed_two_grad, logit_grad = own_mlp(
        normed_two_low, cotangent, route, gate_rows, w1e, w1s, expert_down, w2s
    )
    normed_two_total = lax.psum(normed_two_grad, "tensor")
    mlp_gain_part = jnp.sum(normed_two_grad * residual * factor_two, axis=0)
    shared_gate_part = jnp.sum(logit_grad[0][:, None] * normed_two_low.astype(F32), axis=0)

    cot_low, route_all = split_rounded(cot_all, count)
    where = jnp.stack([core, me, me ^ 1])
    one_mine, one_peer, two_mine, two_peer = all_grads(
        where, rounded(tok_all), cot_low, route_all, gate_rows, w1e, w1s, expert_down, w2s, part
    )
    one_peer = lax.ppermute(one_peer, "dp", swap)
    two_peer = lax.ppermute(two_peer, "dp", swap)

    def joined(mine, peer):
        return jnp.where(core == 0, jnp.concatenate([mine, peer]), jnp.concatenate([peer, mine]))

    half = experts // 2
    expert_gate_up_grad = jnp.transpose(joined(one_mine[:half], one_peer[:half]), (0, 3, 1, 2))
    expert_down_grad = joined(two_mine[:half], two_peer[:half])
    shared_gate_up_grad = jnp.transpose(joined(one_mine[half:], one_peer[half:]), (3, 1, 0, 2)).reshape(
        part, 2, shared * units
    )
    shared_down_grad = joined(two_mine[half:], two_peer[half:]).reshape(shared * units, part)

    residual_grad = upstream + norm_back(residual, factor_two, gain_two, normed_two_total)
    branch_grad = residual_grad.astype(BF16)
    out_weight_grad = tn(attended, branch_grad)
    out_weight_grad = lax.psum_scatter(out_weight_grad, "dp", scatter_dimension=1, tiled=True)
    attended_grad = nt(branch_grad, out_weight).astype(BF16).reshape(count, heads_here, head_dim)
    prob_grad = jnp.einsum("qhd,khd->hqk", attended_grad, value_low, preferred_element_type=F32)
    inner = jnp.sum(probs * prob_grad, axis=-1, keepdims=True)
    score_low = (probs * (prob_grad - inner) * scale).astype(BF16)
    query_grads = jnp.einsum("hqk,khd->qhd", score_low, key_low, preferred_element_type=F32)
    key_grad = jnp.einsum("hqk,qhd->khd", score_low, query_low, preferred_element_type=F32)
    value_grad = jnp.einsum("hqk,qhd->khd", probs_low, attended_grad, preferred_element_type=F32)
    query_round = lax.optimization_barrier(query_grads.astype(BF16)).astype(F32)
    key_round = lax.optimization_barrier(key_grad.astype(BF16)).astype(F32)
    projected_grad = jnp.stack(
        [rotary_back(query_round, cosine, sine), rotary_back(key_round, cosine, sine), value_grad], axis=2
    )
    projected_grad = projected_grad.astype(BF16).reshape(count, heads_here * 3 * head_dim)
    normed_one_grad = nt(projected_grad, qkv_weight)
    normed_one_total, mlp_sum = lax.psum((normed_one_grad, mlp_part), "tensor")
    qkv_weight_grad = lax.psum_scatter(tn(normed_one_low, projected_grad), "dp", scatter_dimension=0, tiled=True)

    layer_output = (residual + mlp_sum).astype(BF16)
    attn_gain_part = jnp.sum(normed_one_grad * inputs * factor_one, axis=0)
    bias_part = jnp.sum(projected_grad, axis=0, dtype=F32)
    place_of = lax.axis_index("tensor") == jnp.arange(n_tensor)
    small = jnp.concatenate(
        [attn_gain_part, mlp_gain_part, shared_gate_part, (place_of[:, None] * bias_part[None, :]).reshape(-1)]
    )
    small = lax.psum(small, ("dp", "tensor"))
    gains = lax.dynamic_slice(small[: 3 * width].reshape(3, width), (0, me * part), (3, part))
    bias = small[3 * width :].reshape(n_tensor, heads_here, 3 * head_dim)
    bias = lax.dynamic_index_in_dim(bias, lax.axis_index("tensor"), 0, keepdims=False)
    bias_cols = 3 * head_dim // n_dp
    qkv_bias_grad = lax.dynamic_slice(bias, (0, me * bias_cols), (heads_here, bias_cols))
    input_grad = (residual_grad + norm_back(inputs, factor_one, gain_one, normed_one_total)).astype(BF16)
    return (
        layer_output,
        input_grad,
        gains[0],
        qkv_weight_grad,
        qkv_bias_grad,
        out_weight_grad,
        gains[1],
        expert_gate_up_grad,
        expert_down_grad,
        shared_gate_up_grad,
        shared_down_grad,
        gains[2],
    )


def solution(mesh):
    placed = (
        P("dp", None),
        P("dp"),
        P("dp", None),
        P("dp", None),
        P(),
        P(None, "tensor"),
        P("tensor", None),
        P("tensor", None),
        P(),
        P(None, None, None, "tensor"),
        P(None, "tensor", None),
        P(None, None, "tensor"),
        P("tensor", None),
        P(),
        P("dp", None),
    )
    return jax.shard_map(
        functools.partial(shards, mesh.shape["dp"], mesh.shape["tensor"]),
        mesh=mesh,
        in_specs=placed,
        out_specs=(
            P("dp", None),
            P("dp", None),
            P("dp"),
            P("dp", "tensor"),
            P("tensor", "dp"),
            P("tensor", "dp"),
            P("dp"),
            P(None, "dp", None, "tensor"),
            P(None, "tensor", "dp"),
            P("dp", None, "tensor"),
            P("tensor", "dp"),
            P("dp"),
        ),
        check_vma=False,
    )
```

```python
import functools

import jax
import jax.numpy as jnp
from jax import lax
from jax.experimental import pallas as pl
from jax.experimental.pallas import tpu as pltpu
from jax.sharding import PartitionSpec as P

EPS = 1e-06
ROPE_BASE = 1000000.0
NEG = -1e30
F32 = jnp.float32
BF16 = jnp.bfloat16
VMEM_LIMIT = 60 * 1024 * 1024
BLOCKS = 8
LIGHT = pl.CostEstimate(flops=1 << 20, bytes_accessed=1 << 16, transcendentals=0)


def nt(left, right):
    return lax.dot_general(left, right, (((1,), (1,)), ((), ())), preferred_element_type=F32)


def tn(left, right):
    return lax.dot_general(left, right, (((0,), (0,)), ((), ())), preferred_element_type=F32)


def nn(left, right):
    return jnp.dot(left, right, preferred_element_type=F32)


def norm_back(values_in, factor, gain_vec, upstream):
    scaled = gain_vec * upstream
    inner = jnp.mean(scaled * values_in, axis=-1, keepdims=True)
    return factor * scaled - values_in * factor**3 * inner


def turned(values, cosine, sine):
    return values * cosine + pltpu.roll(values, values.shape[1] // 2, 1) * sine


def turned_back(values, cosine, sine):
    return values * cosine - pltpu.roll(values, values.shape[1] // 2, 1) * sine


def head_probs(queries, keys, row_ref, col_ref):
    count = queries.shape[0]
    scores = nt(queries, keys) * queries.shape[1] ** (-0.5)
    rows = lax.broadcasted_iota(jnp.int32, (count, count), 0)
    cols = lax.broadcasted_iota(jnp.int32, (count, count), 1)
    scores = jnp.where((col_ref[...] == row_ref[...]) & (cols <= rows), scores, NEG)
    exponent = jnp.exp(scores - jnp.max(scores, axis=-1, keepdims=True))
    return exponent / jnp.sum(exponent, axis=-1, keepdims=True)


def split_columns(whole_ref, split_ref):
    part = whole_ref.shape[1] // BLOCKS
    for k in range(BLOCKS):
        split_ref[k % 2, :, k // 2 * part : (k // 2 + 1) * part] = whole_ref[:, k * part : (k + 1) * part]


def attn_kernel(x_ref, gain_ref, weight_ref, bias_ref, cos_ref, sin_ref, row_ref, col_ref, out_weight_ref,
                part_ref, split_ref, qkv_ref, attended_ref, normed_ref):
    head = pl.program_id(0)
    dim = cos_ref.shape[1]

    @pl.when(head == 0)
    def _():
        values = x_ref[...].astype(F32)
        factor = lax.rsqrt(jnp.mean(values * values, axis=-1, keepdims=True) + EPS)
        normed_ref[...] = (values * factor * gain_ref[...]).astype(BF16)
        split_columns(normed_ref, split_ref)

    projected = nn(normed_ref[...], weight_ref[...]) + bias_ref[0]
    queries = turned(projected[:, :dim], cos_ref[...], sin_ref[...]).astype(BF16)
    keys = turned(projected[:, dim : 2 * dim], cos_ref[...], sin_ref[...]).astype(BF16)
    values = projected[:, 2 * dim :].astype(BF16)
    qkv_ref[:, :dim] = queries
    qkv_ref[:, dim : 2 * dim] = keys
    qkv_ref[:, 2 * dim :] = values
    probs = head_probs(queries, keys, row_ref, col_ref)
    cols = pl.ds(pl.multiple_of(head * dim, dim), dim)
    attended_ref[:, cols] = nn(probs.astype(BF16), values).astype(BF16)

    @pl.when(head == pl.num_programs(0) - 1)
    def _():
        part_ref[...] = nn(attended_ref[...], out_weight_ref[...])


def whole(*shape):
    return pl.BlockSpec(shape, lambda *at: (0,) * len(shape))


def attention(x, gain, weight, bias, cosine, sine, row, col, out_weight):
    count, width = x.shape
    heads, _, cols = bias.shape
    return pl.pallas_call(
        attn_kernel,
        grid=(heads,),
        in_specs=[
            whole(count, width),
            whole(1, width),
            pl.BlockSpec((width, cols), lambda h: (0, h)),
            pl.BlockSpec((1, 1, cols), lambda h: (h, 0, 0)),
            whole(*cosine.shape),
            whole(*sine.shape),
            whole(1, count),
            whole(count, 1),
            whole(*out_weight.shape),
        ],
        out_specs=[
            whole(count, width),
            whole(2, count, width // 2),
            pl.BlockSpec((count, cols), lambda h: (0, h)),
            whole(count, out_weight.shape[0]),
        ],
        out_shape=[
            jax.ShapeDtypeStruct((count, width), F32),
            jax.ShapeDtypeStruct((2, count, width // 2), BF16),
            jax.ShapeDtypeStruct((count, heads * cols), BF16),
            jax.ShapeDtypeStruct((count, out_weight.shape[0]), BF16),
        ],
        scratch_shapes=[pltpu.VMEM((count, width), BF16)],
        compiler_params=pltpu.CompilerParams(
            dimension_semantics=("arbitrary",), vmem_limit_bytes=32 * 1024 * 1024
        ),
        cost_estimate=LIGHT,
        name="attention",
    )(x, gain, weight, bias, cosine, sine, row, col, out_weight)


def norm_kernel(x_ref, sum_ref, gain_ref, residual_ref, low_ref, wide_ref):
    residual = x_ref[...].astype(F32) + sum_ref[...]
    factor = lax.rsqrt(jnp.mean(residual * residual, axis=-1, keepdims=True) + EPS)
    low = (residual * factor * gain_ref[...]).astype(BF16)
    residual_ref[...] = residual
    low_ref[...] = low
    wide_ref[...] = low.astype(F32)


def second_norm(x, attn_sum, gain):
    count, width = x.shape
    rows = count // 4
    spec = pl.BlockSpec((rows, width), lambda i: (i, 0))
    return pl.pallas_call(
        norm_kernel,
        grid=(4,),
        in_specs=[spec, spec, whole(1, width)],
        out_specs=[spec, spec, spec],
        out_shape=[
            jax.ShapeDtypeStruct((count, width), F32),
            jax.ShapeDtypeStruct((count, width), BF16),
            jax.ShapeDtypeStruct((count, width), F32),
        ],
        compiler_params=pltpu.CompilerParams(
            dimension_semantics=("arbitrary",), vmem_limit_bytes=32 * 1024 * 1024
        ),
        name="second_norm",
    )(x, attn_sum, gain)


def back_kernel(total_ref, residual_ref, cot_ref, gain_ref, out_weight_ref, qkv_ref, weight_ref, cos_ref, sin_ref,
                row_ref, col_ref, normed_grad_ref, residual_grad_ref, split_ref, projected_grad_ref, bias_ref,
                mlp_gain_ref, branch_ref, attended_grad_ref):
    head = pl.program_id(0)
    dim = cos_ref.shape[1]

    @pl.when(head == 0)
    def _():
        total, residual = total_ref[...], residual_ref[...]
        factor = lax.rsqrt(jnp.mean(residual * residual, axis=-1, keepdims=True) + EPS)
        scaled = gain_ref[...] * total
        inner = jnp.mean(scaled * residual, axis=-1, keepdims=True)
        residual_grad = cot_ref[...].astype(F32) + (factor * scaled - residual * factor**3 * inner)
        residual_grad_ref[...] = residual_grad
        branch_ref[...] = residual_grad.astype(BF16)
        split_columns(branch_ref, split_ref)
        mlp_gain_ref[...] = jnp.sum(total * residual * factor, axis=0, keepdims=True)
        attended_grad = nt(branch_ref[...], out_weight_ref[...]).astype(BF16)
        for k in range(attended_grad_ref.shape[0]):
            attended_grad_ref[k] = attended_grad[:, k * dim : (k + 1) * dim]

    queries, keys, values = qkv_ref[:, :dim], qkv_ref[:, dim : 2 * dim], qkv_ref[:, 2 * dim :]
    attended_grad = attended_grad_ref[head]
    probs = head_probs(queries, keys, row_ref, col_ref)
    prob_grad = nt(attended_grad, values)
    inner = jnp.sum(probs * prob_grad, axis=-1, keepdims=True)
    score = (probs * (prob_grad - inner) * dim ** (-0.5)).astype(BF16)
    query_grad = nn(score, keys).astype(BF16).astype(F32)
    key_grad = tn(score, queries).astype(BF16).astype(F32)
    value_grad = tn(probs.astype(BF16), attended_grad)
    grad = jnp.concatenate(
        [
            turned_back(query_grad, cos_ref[...], sin_ref[...]).astype(BF16),
            turned_back(key_grad, cos_ref[...], sin_ref[...]).astype(BF16),
            value_grad.astype(BF16),
        ],
        axis=1,
    )
    projected_grad_ref[...] = grad
    bias_ref[...] = jnp.sum(grad.astype(F32), axis=0, keepdims=True)
    product = nt(grad, weight_ref[...])

    @pl.when(head == 0)
    def _():
        normed_grad_ref[...] = product

    @pl.when(head > 0)
    def _():
        normed_grad_ref[...] += product


def attention_back(total, residual, cotangent, gain, out_weight, qkv, weight, cosine, sine, row, col):
    count, width = total.shape
    dim = cosine.shape[1]
    cols = 3 * dim
    heads = qkv.shape[1] // cols
    return pl.pallas_call(
        back_kernel,
        grid=(heads,),
        in_specs=[
            whole(count, width),
            whole(count, width),
            whole(count, width),
            whole(1, width),
            whole(*out_weight.shape),
            pl.BlockSpec((count, cols), lambda h: (0, h)),
            pl.BlockSpec((width, cols), lambda h: (0, h)),
            whole(*cosine.shape),
            whole(*sine.shape),
            whole(1, count),
            whole(count, 1),
        ],
        out_specs=[
            whole(count, width),
            whole(count, width),
            whole(2, count, width // 2),
            pl.BlockSpec((count, cols), lambda h: (0, h)),
            pl.BlockSpec((1, cols), lambda h: (0, h)),
            whole(1, width),
        ],
        out_shape=[
            jax.ShapeDtypeStruct((count, width), F32),
            jax.ShapeDtypeStruct((count, width), F32),
            jax.ShapeDtypeStruct((2, count, width // 2), BF16),
            jax.ShapeDtypeStruct((count, heads * cols), BF16),
            jax.ShapeDtypeStruct((1, heads * cols), F32),
            jax.ShapeDtypeStruct((1, width), F32),
        ],
        scratch_shapes=[pltpu.VMEM((count, width), BF16), pltpu.VMEM((heads, count, dim), BF16)],
        compiler_params=pltpu.CompilerParams(
            dimension_semantics=("arbitrary",), vmem_limit_bytes=48 * 1024 * 1024
        ),
        cost_estimate=LIGHT,
        name="attention_back",
    )(total, residual, cotangent, gain, out_weight, qkv, weight, cosine, sine, row, col)


def hidden(w_one, w_two, tokens, branch, route_row):
    units = w_two.shape[0]
    mix = nt(w_one, tokens)
    gate, up = mix[:units], mix[units:]
    back = nt(w_two, branch)
    sigma = lax.logistic(gate)
    silu = gate * sigma
    act = silu * up
    scaled = back * route_row
    gate_grad = scaled * up * (sigma + silu * (1.0 - sigma))
    mix_grad = jnp.concatenate([gate_grad.astype(BF16), (scaled * silu).astype(BF16)], axis=0)
    return act, back, (act * route_row).astype(BF16), mix_grad


def open_row(gate_rows, tokens):
    return lax.logistic(nt(gate_rows, tokens)[:1])


def own_kernel(experts, tok_ref, cot_ref, route_ref, gate_ref, w1_ref, w2_ref, out_ref, dx_ref, logit_ref, open_ref):
    step = pl.program_id(0)
    group, units, width = w2_ref.shape
    shared = step * group >= experts

    @pl.when(step == 0)
    def _():
        out_ref[...] = jnp.zeros_like(out_ref)
        dx_ref[...] = jnp.zeros_like(dx_ref)
        logit_ref[...] = jnp.zeros_like(logit_ref)
        open_ref[...] = open_row(gate_ref[...], tok_ref[...])

    weighted, mix_grads = [], []
    for k in range(group):
        act, back, scaled, mix_grad = hidden(
            w1_ref[k].reshape(2 * units, width),
            w2_ref[k],
            tok_ref[...],
            cot_ref[...],
            jnp.where(shared, open_ref[...], route_ref[k]),
        )
        weighted.append(scaled)
        mix_grads.append(mix_grad)
        logit_ref[...] += jnp.where(shared, jnp.sum(act * back, axis=0, keepdims=True), 0.0)
    out_ref[...] += tn(jnp.concatenate(weighted), w2_ref[...].reshape(group * units, width))
    dx_ref[...] += tn(jnp.concatenate(mix_grads), w1_ref[...].reshape(group * 2 * units, width))

    @pl.when(step == pl.num_programs(0) - 1)
    def _():
        opened = open_ref[...]
        logit = opened * (1.0 - opened) * logit_ref[...]
        logit_ref[...] = logit
        column = jnp.broadcast_to(logit, (8, logit.shape[1])).T[:, :1]
        dx_ref[...] += column * gate_ref[:1].astype(F32)


def own_mlp(tokens, cotangent, route, gate_rows, w1, w2):
    count, width = tokens.shape
    tiles, units = w2.shape[:2]
    experts = route.shape[0]
    group = 2
    return pl.pallas_call(
        functools.partial(own_kernel, experts),
        grid=(tiles // group,),
        in_specs=[
            whole(count, width),
            whole(count, width),
            pl.BlockSpec((group, 1, count), lambda i: (jnp.minimum(i, experts // group - 1), 0, 0)),
            whole(*gate_rows.shape),
            pl.BlockSpec((group, 2, units, width), lambda i: (i, 0, 0, 0)),
            pl.BlockSpec((group, units, width), lambda i: (i, 0, 0)),
        ],
        out_specs=[whole(count, width), whole(count, width), whole(1, count)],
        out_shape=[
            jax.ShapeDtypeStruct((count, width), F32),
            jax.ShapeDtypeStruct((count, width), F32),
            jax.ShapeDtypeStruct((1, count), F32),
        ],
        scratch_shapes=[pltpu.VMEM((1, count), F32)],
        compiler_params=pltpu.CompilerParams(
            dimension_semantics=("arbitrary",), vmem_limit_bytes=VMEM_LIMIT
        ),
        cost_estimate=LIGHT,
        name="own_mlp",
    )(tokens, cotangent, route[:, None, :], gate_rows, w1, w2)


def chip_kernel(pieces, here, at_ref, *refs):
    token_refs, refs = refs[: 2 * pieces], refs[2 * pieces :]
    cot_ref, route_ref, gate_ref, w1_ref, w2_ref = refs[:5]
    mix_grad_ref, weighted_ref, part_ref, tok_ref, open_ref = refs[-5:]
    step = pl.program_id(0)
    units, width = w2_ref.shape[-2:]
    cores, experts, count = route_ref.shape
    core = at_ref[0]

    @pl.when(step == 0)
    def _():
        for owner in range(2):
            base = count * (core if owner == 0 else 1 - core)
            for k, ref in enumerate(token_refs[owner * pieces : (owner + 1) * pieces]):
                rows = ref.shape[0]
                tok_ref[pl.ds(pl.multiple_of(base + k * rows, rows), rows), :] = ref[...].astype(BF16)
        part = part_ref.shape[1]
        part_ref[...] = tok_ref[:, pl.ds(pl.multiple_of(at_ref[1] * part, part), part)]
        open_ref[...] = open_row(gate_ref[...], tok_ref[...])

    expert = jnp.minimum(core * here + step, experts - 1)
    route_row = jnp.concatenate([route_ref[k, pl.ds(expert, 1), :] for k in range(cores)], axis=1)
    _, _, weighted, mix_grad = hidden(
        w1_ref[...].reshape(2 * units, width),
        w2_ref[0],
        tok_ref[...],
        cot_ref[...],
        jnp.where(step >= here, open_ref[...], route_row),
    )
    mix_grad_ref[0] = mix_grad
    weighted_ref[0] = weighted


def chip_hidden(at, mine, peer, cotangent, route, gate_rows, w1, w2, kept, part):
    total, width = cotangent.shape
    tiles, units = w2.shape[:2]
    experts, count = route.shape[1:]
    here, shared = experts // 2, (tiles - experts) // 2
    rows = 2 * count
    own = lambda i, at: jnp.where(i < here, at[0] * here + i, experts + at[0] * shared + i - here)
    pieces = len(mine)
    fixed = lambda *shape: pl.BlockSpec(shape, lambda i, at: (0,) * len(shape))
    shapes = [
        jax.ShapeDtypeStruct((here + shared, 2 * units, total), BF16),
        jax.ShapeDtypeStruct((here + shared, units, total), BF16),
        jax.ShapeDtypeStruct((total, 2 * part), BF16),
    ]
    inputs = [*mine, *peer, cotangent, route, gate_rows, w1, w2]
    return pl.pallas_call(
        functools.partial(chip_kernel, pieces, here),
        grid_spec=pltpu.PrefetchScalarGridSpec(
            num_scalar_prefetch=1,
            grid=(here + shared,),
            in_specs=[
                *[fixed(*v.shape) for v in (*mine, *peer)],
                pl.BlockSpec((rows, width), lambda i, at: (at[2], 0)),
                pl.BlockSpec((2, experts, count), lambda i, at: (at[2], 0, 0)),
                fixed(*gate_rows.shape),
                pl.BlockSpec((1, 2, units, width), lambda i, at: (own(i, at), 0, 0, 0)),
                pl.BlockSpec((1, units, width), lambda i, at: (own(i, at), 0, 0)),
                *[pl.BlockSpec(memory_space=pl.ANY) for _ in kept],
            ],
            out_specs=[
                pl.BlockSpec((1, 2 * units, rows), lambda i, at: (i, 0, at[2])),
                pl.BlockSpec((1, units, rows), lambda i, at: (i, 0, at[2])),
                pl.BlockSpec((rows, 2 * part), lambda i, at: (at[2], 0)),
            ],
            scratch_shapes=[pltpu.VMEM((rows, width), BF16), pltpu.VMEM((1, rows), F32)],
        ),
        out_shape=shapes,
        input_output_aliases={1 + len(inputs) + k: k for k in range(len(kept))},
        compiler_params=pltpu.CompilerParams(
            dimension_semantics=("arbitrary",), vmem_limit_bytes=VMEM_LIMIT
        ),
        cost_estimate=LIGHT,
        name="chip_hidden",
    )(at, *inputs, *kept)


def weights_kernel(at_ref, mix_grad_ref, weighted_ref, tok_ref, cot_ref, one_mine_ref, one_peer_ref, two_mine_ref,
                   two_peer_ref):
    part = one_mine_ref.shape[-1]
    core = at_ref[0]
    one = nn(mix_grad_ref[0], tok_ref[...])
    two = nn(weighted_ref[0], cot_ref[...])
    for value, mine_ref, peer_ref in ((one, one_mine_ref, one_peer_ref), (two, two_mine_ref, two_peer_ref)):
        low, high = value[:, :part], value[:, part:]
        mine_ref[...] = jnp.where(core == 0, low, high).reshape(mine_ref.shape)
        peer_ref[...] = jnp.where(core == 0, high, low).reshape(peer_ref.shape)


def weight_grads(at, mix_grads, weighted, tokens, cotangent):
    tiles, units, total = weighted.shape
    part = tokens.shape[1] // 2
    one = jax.ShapeDtypeStruct((tiles, 2, units, part), F32)
    two = jax.ShapeDtypeStruct((tiles, units, part), F32)
    one_spec = pl.BlockSpec((1, 2, units, part), lambda i, at: (i, 0, 0, 0))
    two_spec = pl.BlockSpec((1, units, part), lambda i, at: (i, 0, 0))
    return pl.pallas_call(
        weights_kernel,
        grid_spec=pltpu.PrefetchScalarGridSpec(
            num_scalar_prefetch=1,
            grid=(tiles,),
            in_specs=[
                pl.BlockSpec((1, 2 * units, total), lambda i, at: (i, 0, 0)),
                pl.BlockSpec((1, units, total), lambda i, at: (i, 0, 0)),
                pl.BlockSpec((total, 2 * part), lambda i, at: (0, 0)),
                pl.BlockSpec((total, 2 * part), lambda i, at: (0, at[1])),
            ],
            out_specs=[one_spec, one_spec, two_spec, two_spec],
        ),
        out_shape=[one, one, two, two],
        compiler_params=pltpu.CompilerParams(
            dimension_semantics=("arbitrary",), vmem_limit_bytes=VMEM_LIMIT
        ),
        cost_estimate=LIGHT,
        name="weight_grads",
    )(at, mix_grads, weighted, tokens, cotangent)


def split_kernel(in_ref, out_ref, route_ref):
    count = out_ref.shape[0]
    out_ref[...] = in_ref[0, :count].astype(BF16)
    route_ref[...] = in_ref[0, count:, :count][None]


def split_rounded(gathered, count):
    blocks, rows, width = gathered.shape
    extra = rows - count
    return pl.pallas_call(
        split_kernel,
        grid=(blocks,),
        in_specs=[pl.BlockSpec((1, rows, width), lambda i: (i, 0, 0))],
        out_specs=[
            pl.BlockSpec((count, width), lambda i: (i, 0)),
            pl.BlockSpec((1, extra, count), lambda i: (i, 0, 0)),
        ],
        out_shape=[
            jax.ShapeDtypeStruct((blocks * count, width), BF16),
            jax.ShapeDtypeStruct((blocks, extra, count), F32),
        ],
        compiler_params=pltpu.CompilerParams(
            dimension_semantics=("arbitrary",), vmem_limit_bytes=32 * 1024 * 1024
        ),
        name="split_rounded",
    )(gathered)


def flip(value, bit):
    return lax.ppermute(value, "dp", [(i, i ^ bit) for i in range(8)])


def after(source, count):
    message = lax.ppermute(source[:8, :128], "dp", [(i, i ^ 1) for i in range(count)])
    return jnp.isnan(message[0, 0]).astype(jnp.int32)


def take(value, number, axis):
    return lax.dynamic_index_in_dim(value, number, axis, keepdims=False)


def scatter_first(held, me):
    along_x, along_y = (me // 2) % 2, me // 4
    half = held.shape[-1] // 256 * 128
    a, b = held[..., :half], held[..., half:]
    return (take(a, along_x, 1), take(a, 1 - along_x, 1), take(b, along_y, 0), take(b, 1 - along_y, 0))


def scatter_second(a, b, me):
    along_x, along_y = (me // 2) % 2, me // 4
    a = take(a, along_y, 0) + flip(take(a, 1 - along_y, 0), 4)
    b = take(b, along_x, 0) + flip(take(b, 1 - along_x, 0), 2)
    return jnp.concatenate([a, b], axis=-1)


def shards(
    n_dp,
    n_tensor,
    layer_input,
    doc_ids,
    expert_ids,
    route_weights,
    attn_gain,
    qkv_weight,
    qkv_bias,
    out_weight,
    mlp_gain,
    expert_gate_up,
    expert_down,
    shared_gate_up,
    shared_down,
    shared_gate,
    cotangent,
):
    count, width = layer_input.shape
    heads_here = qkv_bias.shape[0]
    head_dim = qkv_bias.shape[1] // 3
    experts, units = expert_down.shape[:2]
    shared = shared_down.shape[0] // units
    part = width // n_dp
    me = lax.axis_index("dp")
    core, chip = me % 2, me // 2
    tied = lax.optimization_barrier

    choose = expert_ids[:, :, None] == jnp.arange(experts, dtype=jnp.int32)[None, None, :]
    route = jnp.sum(route_weights[:, :, None] * choose.astype(F32), axis=1).T
    cot_all = lax.all_gather(
        jnp.concatenate([cotangent.astype(F32), jnp.pad(route, ((0, 0), (0, width - count)))], axis=0), "dp"
    )
    gate_rows = jnp.broadcast_to(shared_gate[None, :], (16, width))
    index = jnp.arange(count, dtype=jnp.int32)
    place = (me * count + index - doc_ids).astype(F32)
    freq = ROPE_BASE ** (-(jnp.arange(head_dim // 2, dtype=F32) * 2.0 / head_dim))
    angle = place[:, None] * freq[None, :]
    cosine = jnp.concatenate([jnp.cos(angle), jnp.cos(angle)], axis=-1)
    sine = jnp.concatenate([-jnp.sin(angle), jnp.sin(angle)], axis=-1)
    row, col = doc_ids[None, :], doc_ids[:, None]
    gain_one = attn_gain.astype(F32)[None, :]
    gain_two = mlp_gain.astype(F32)[None, :]
    attn_part, normed_one, qkv, attended = attention(
        layer_input, gain_one, qkv_weight, qkv_bias.astype(F32)[:, None, :], cosine, sine, row, col, out_weight
    )

    attn_part, shared_gate_up = tied((attn_part, shared_gate_up))
    attn_sum = lax.psum(attn_part, "tensor")
    w1 = jnp.concatenate(
        [
            jnp.transpose(expert_gate_up, (0, 2, 3, 1)),
            jnp.transpose(shared_gate_up.reshape(width, 2, shared, units), (2, 1, 3, 0)),
        ]
    )
    w2 = jnp.concatenate([expert_down, shared_down.reshape(shared, units, width)])
    cot_low, route_all = split_rounded(cot_all, count)
    attn_sum, w1, w2, cot_low, route_all = tied((attn_sum, w1, w2, cot_low, route_all))

    residual, tokens, tokens_wide = second_norm(layer_input, attn_sum, gain_two)
    if n_dp == 8:
        over_x, over_y = flip(tokens_wide, 2), flip(tokens_wide, 4)
        beside = flip(tokens_wide, 1)
    else:
        tok_all = lax.all_gather(tokens_wide, "dp")
    mlp_part, normed_two_part, logit_grad = own_mlp(tokens, cotangent, route, gate_rows, w1, w2)
    normed_two_part, mlp_part = tied((normed_two_part, mlp_part))
    normed_two_total = lax.psum(normed_two_part, "tensor")
    line = n_tensor == 4 and n_dp == 8
    if line:
        inwards = lax.ppermute(mlp_part, "tensor", [(0, 1), (3, 2)])

    kept = []
    pair = lambda other: jnp.stack([core, chip, other])
    hide = lambda other, mine, peer, kept: chip_hidden(
        pair(other), mine, peer, cot_low, route_all, gate_rows, w1, w2, kept, part
    )
    if n_dp == 8:
        over_x, over_y, other = tied((over_x, over_y, (chip ^ 1) + after(normed_two_part, n_dp)))
        low, high = flip(over_x[: count // 2], 4), flip(over_y[count // 2 :], 2)
        beside_x, beside_y = flip(over_x, 1), flip(over_y, 1)
        kept = hide(other, [over_x], [beside_x], kept)
        low, high, kept = tied((low, high, kept))
        beside_low, beside_high = flip(low, 1), flip(high, 1)
        kept = hide(chip ^ 2, [over_y], [beside_y], kept)
        kept = hide(chip ^ 3, [low, high], [beside_low, beside_high], kept)
        kept = hide(chip, [tokens_wide], [beside], kept)
    else:
        for k in range(n_dp // 2):
            kept = hide(k, [take(tok_all, 2 * k + core, 0)], [take(tok_all, 2 * k + 1 - core, 0)], kept)
    one_mine, one_peer, two_mine, two_peer = weight_grads(pair(chip), *kept, cot_low)
    if line:
        inwards, one_peer = tied((inwards, one_peer))
    one_mine, one_peer, two_mine, two_peer, normed_two_total = tied(
        (one_mine, one_peer, two_mine, two_peer, normed_two_total)
    )

    normed_one_part, residual_grad, branch_grad, projected_grad, bias_part, mlp_gain_part = attention_back(
        normed_two_total, residual, cotangent, gain_two, out_weight, qkv, qkv_weight, cosine, sine, row, col
    )
    normed_one_total = lax.psum_scatter(normed_one_part, "tensor", scatter_dimension=0, tiled=True)
    few = count // n_tensor
    inputs = layer_input.astype(F32)
    factor_one = lax.rsqrt(jnp.mean(inputs * inputs, axis=-1, keepdims=True) + EPS)
    mine = lambda v: lax.dynamic_slice_in_dim(v, lax.axis_index("tensor") * few, few, 0)
    input_grad = norm_back(mine(inputs), mine(factor_one), gain_one, normed_one_total)
    input_grad = lax.all_gather(input_grad, "tensor", axis=0, tiled=True)
    swap = [(i, i ^ 1) for i in range(n_dp)]
    one_peer, two_peer = lax.ppermute(one_peer, "dp", swap), lax.ppermute(two_peer, "dp", swap)
    attn_gain_part = jnp.sum(normed_one_part * inputs * factor_one, axis=0)
    shared_gate_part = jnp.sum(logit_grad[0][:, None] * tokens.astype(F32), axis=0)
    my_slot = lax.axis_index("tensor") == jnp.arange(n_tensor)
    small = jnp.concatenate(
        [
            attn_gain_part,
            mlp_gain_part[0] * my_slot[0],
            shared_gate_part,
            (my_slot[:, None] * bias_part).reshape(-1),
        ]
    )
    spot = lax.axis_index("tensor")
    if line:
        inwards, projected_grad = tied((inwards, projected_grad))
    if n_dp == 8:
        def products(c):
            return (
                tn(take(normed_one, c, 0), projected_grad).reshape(2, 2, part, -1),
                tn(take(branch_grad, c, 0), attended).reshape(2, 2, part, -1),
            )

        other = 1 - core + after(normed_one_part, n_dp)
        sent = products(other)
        arrived = [flip(v, 1) for v in sent]
        if line:
            mlp_part, sent = tied((mlp_part, sent))
            partial = mlp_part + inwards
            across = lax.ppermute(partial, "tensor", [(1, 2), (2, 1)])
            small, partial = tied((small, partial))
        else:
            small, sent = tied((small, sent))
        small = lax.psum(small, ("dp", "tensor"))
        small, arrived = tied((small, arrived))
        held = products(1 - other)
        firsts = [scatter_first(h + v, me) for h, v in zip(held, arrived, strict=True)]
        moved = [(flip(a_other, 2), flip(b_other, 4)) for _, a_other, _, b_other in firsts]
        if line:
            across, moved = tied((across, moved))
            partial = partial + across
            outwards = lax.ppermute(partial, "tensor", [(1, 0), (2, 3)])
        steps = [(a + a_in, b + b_in) for (a, _, b, _), (a_in, b_in) in zip(firsts, moved, strict=True)]
        qkv_weight_grad, out_weight_grad = [scatter_second(a, b, me) for a, b in steps]
        out_weight_grad = out_weight_grad.T
        input_grad, qkv_weight_grad = tied((input_grad, qkv_weight_grad))
        if line:
            outwards, qkv_weight_grad = tied((outwards, qkv_weight_grad))
    else:
        small = lax.psum(small, ("dp", "tensor"))
        joint = lambda v: v.reshape(2, count, BLOCKS // 2, -1).transpose(1, 2, 0, 3).reshape(count, width)
        out_weight_grad = lax.psum_scatter(tn(attended, joint(branch_grad)), "dp", scatter_dimension=1, tiled=True)
        qkv_weight_grad = lax.psum_scatter(
            tn(joint(normed_one), projected_grad), "dp", scatter_dimension=0, tiled=True
        )

    gains = lax.dynamic_slice(small[: 3 * width].reshape(3, width), (0, me * part), (3, part))
    bias = take(small[3 * width :].reshape(n_tensor, heads_here, 3 * head_dim), lax.axis_index("tensor"), 0)
    bias_cols = 3 * head_dim // n_dp
    qkv_bias_grad = lax.dynamic_slice(bias, (0, me * bias_cols), (heads_here, bias_cols))
    input_grad = (residual_grad + input_grad).astype(BF16)

    if line:
        mlp_sum = jnp.where((spot == 1) | (spot == 2), partial, outwards)
    else:
        mlp_sum = lax.psum(mlp_part, "tensor")
    layer_output = (residual + mlp_sum).astype(BF16)

    def joined(mine, peer):
        return jnp.where(core == 0, jnp.concatenate([mine, peer]), jnp.concatenate([peer, mine]))

    half = experts // 2
    expert_gate_up_grad = jnp.transpose(joined(one_mine[:half], one_peer[:half]), (0, 3, 1, 2))
    expert_down_grad = joined(two_mine[:half], two_peer[:half])
    shared_gate_up_grad = jnp.transpose(joined(one_mine[half:], one_peer[half:]), (3, 1, 0, 2)).reshape(
        part, 2, shared * units
    )
    shared_down_grad = joined(two_mine[half:], two_peer[half:]).reshape(shared * units, part)
    return (
        layer_output,
        input_grad,
        gains[0],
        qkv_weight_grad,
        qkv_bias_grad,
        out_weight_grad,
        gains[1],
        expert_gate_up_grad,
        expert_down_grad,
        shared_gate_up_grad,
        shared_down_grad,
        gains[2],
    )


def solution(mesh):
    placed = (
        P("dp", None),
        P("dp"),
        P("dp", None),
        P("dp", None),
        P(),
        P(None, "tensor"),
        P("tensor", None),
        P("tensor", None),
        P(),
        P(None, None, None, "tensor"),
        P(None, "tensor", None),
        P(None, None, "tensor"),
        P("tensor", None),
        P(),
        P("dp", None),
    )
    return jax.shard_map(
        functools.partial(shards, mesh.shape["dp"], mesh.shape["tensor"]),
        mesh=mesh,
        in_specs=placed,
        out_specs=(
            P("dp", None),
            P("dp", None),
            P("dp"),
            P("dp", "tensor"),
            P("tensor", "dp"),
            P("tensor", "dp"),
            P("dp"),
            P(None, "dp", None, "tensor"),
            P(None, "tensor", "dp"),
            P("dp", None, "tensor"),
            P("tensor", "dp"),
            P("dp"),
        ),
        check_vma=False,
    )
```

```python
import functools

import jax
import jax.numpy as jnp
from jax import lax
from jax.experimental import pallas as pl
from jax.experimental.pallas import tpu as pltpu
from jax.sharding import PartitionSpec as P

EPS = 1e-06
ROPE_BASE = 1000000.0
NEG = -1e30
F32 = jnp.float32
BF16 = jnp.bfloat16
VMEM_LIMIT = 60 * 1024 * 1024
BLOCKS = 8
LIGHT = pl.CostEstimate(flops=1 << 20, bytes_accessed=1 << 16, transcendentals=0)


def nt(left, right):
    return lax.dot_general(left, right, (((1,), (1,)), ((), ())), preferred_element_type=F32)


def tn(left, right):
    return lax.dot_general(left, right, (((0,), (0,)), ((), ())), preferred_element_type=F32)


def nn(left, right):
    return jnp.dot(left, right, preferred_element_type=F32)


def norm_back(values_in, factor, gain_vec, upstream):
    scaled = gain_vec * upstream
    inner = jnp.mean(scaled * values_in, axis=-1, keepdims=True)
    return factor * scaled - values_in * factor**3 * inner


def turned(values, cosine, sine):
    return values * cosine + pltpu.roll(values, values.shape[1] // 2, 1) * sine


def turned_back(values, cosine, sine):
    return values * cosine - pltpu.roll(values, values.shape[1] // 2, 1) * sine


def head_probs(queries, keys, row_ref, col_ref):
    count = queries.shape[0]
    scores = nt(queries, keys) * queries.shape[1] ** (-0.5)
    rows = lax.broadcasted_iota(jnp.int32, (count, count), 0)
    cols = lax.broadcasted_iota(jnp.int32, (count, count), 1)
    scores = jnp.where((col_ref[...] == row_ref[...]) & (cols <= rows), scores, NEG)
    exponent = jnp.exp(scores - jnp.max(scores, axis=-1, keepdims=True))
    return exponent / jnp.sum(exponent, axis=-1, keepdims=True)


def split_columns(whole_ref, split_ref):
    part = whole_ref.shape[1] // BLOCKS
    for k in range(BLOCKS):
        split_ref[k % 2, :, k // 2 * part : (k // 2 + 1) * part] = whole_ref[:, k * part : (k + 1) * part]


def attn_kernel(x_ref, gain_ref, weight_ref, bias_ref, cos_ref, sin_ref, row_ref, col_ref, out_weight_ref,
                part_ref, split_ref, qkv_ref, attended_ref, normed_ref):
    head = pl.program_id(0)
    dim = cos_ref.shape[1]

    @pl.when(head == 0)
    def _():
        values = x_ref[...].astype(F32)
        factor = lax.rsqrt(jnp.mean(values * values, axis=-1, keepdims=True) + EPS)
        normed_ref[...] = (values * factor * gain_ref[...]).astype(BF16)
        split_columns(normed_ref, split_ref)

    projected = nn(normed_ref[...], weight_ref[...]) + bias_ref[0]
    queries = turned(projected[:, :dim], cos_ref[...], sin_ref[...]).astype(BF16)
    keys = turned(projected[:, dim : 2 * dim], cos_ref[...], sin_ref[...]).astype(BF16)
    values = projected[:, 2 * dim :].astype(BF16)
    qkv_ref[:, :dim] = queries
    qkv_ref[:, dim : 2 * dim] = keys
    qkv_ref[:, 2 * dim :] = values
    probs = head_probs(queries, keys, row_ref, col_ref)
    cols = pl.ds(pl.multiple_of(head * dim, dim), dim)
    attended_ref[:, cols] = nn(probs.astype(BF16), values).astype(BF16)

    @pl.when(head == pl.num_programs(0) - 1)
    def _():
        part_ref[...] = nn(attended_ref[...], out_weight_ref[...])


def whole(*shape):
    return pl.BlockSpec(shape, lambda *at: (0,) * len(shape))


def attention(x, gain, weight, bias, cosine, sine, row, col, out_weight):
    count, width = x.shape
    heads, _, cols = bias.shape
    return pl.pallas_call(
        attn_kernel,
        grid=(heads,),
        in_specs=[
            whole(count, width),
            whole(1, width),
            pl.BlockSpec((width, cols), lambda h: (0, h)),
            pl.BlockSpec((1, 1, cols), lambda h: (h, 0, 0)),
            whole(*cosine.shape),
            whole(*sine.shape),
            whole(1, count),
            whole(count, 1),
            whole(*out_weight.shape),
        ],
        out_specs=[
            whole(count, width),
            whole(2, count, width // 2),
            pl.BlockSpec((count, cols), lambda h: (0, h)),
            whole(count, out_weight.shape[0]),
        ],
        out_shape=[
            jax.ShapeDtypeStruct((count, width), F32),
            jax.ShapeDtypeStruct((2, count, width // 2), BF16),
            jax.ShapeDtypeStruct((count, heads * cols), BF16),
            jax.ShapeDtypeStruct((count, out_weight.shape[0]), BF16),
        ],
        scratch_shapes=[pltpu.VMEM((count, width), BF16)],
        compiler_params=pltpu.CompilerParams(
            dimension_semantics=("arbitrary",), vmem_limit_bytes=32 * 1024 * 1024
        ),
        cost_estimate=LIGHT,
        name="attention",
    )(x, gain, weight, bias, cosine, sine, row, col, out_weight)


def norm_kernel(x_ref, sum_ref, gain_ref, residual_ref, low_ref, wide_ref):
    residual = x_ref[...].astype(F32) + sum_ref[...]
    factor = lax.rsqrt(jnp.mean(residual * residual, axis=-1, keepdims=True) + EPS)
    low = (residual * factor * gain_ref[...]).astype(BF16)
    residual_ref[...] = residual
    low_ref[...] = low
    wide_ref[...] = low.astype(F32)


def second_norm(x, attn_sum, gain):
    count, width = x.shape
    rows = count // 4
    spec = pl.BlockSpec((rows, width), lambda i: (i, 0))
    return pl.pallas_call(
        norm_kernel,
        grid=(4,),
        in_specs=[spec, spec, whole(1, width)],
        out_specs=[spec, spec, spec],
        out_shape=[
            jax.ShapeDtypeStruct((count, width), F32),
            jax.ShapeDtypeStruct((count, width), BF16),
            jax.ShapeDtypeStruct((count, width), F32),
        ],
        compiler_params=pltpu.CompilerParams(
            dimension_semantics=("arbitrary",), vmem_limit_bytes=32 * 1024 * 1024
        ),
        name="second_norm",
    )(x, attn_sum, gain)


def back_kernel(inner_ref, held_top_ref, got_top_ref, held_low_ref, got_low_ref, residual_ref, cot_ref, gain_ref, out_weight_ref, qkv_ref, weight_ref, cos_ref, sin_ref,
                row_ref, col_ref, normed_grad_ref, residual_grad_ref, split_ref, projected_grad_ref, bias_ref,
                mlp_gain_ref, branch_ref, attended_grad_ref):
    head = pl.program_id(0)
    dim = cos_ref.shape[1]

    @pl.when(head == 0)
    def _():
        total = jnp.where(
            inner_ref[0] == 1,
            jnp.concatenate([held_top_ref[...], held_low_ref[...]]),
            jnp.concatenate([got_top_ref[...], got_low_ref[...]]),
        )
        residual = residual_ref[...]
        factor = lax.rsqrt(jnp.mean(residual * residual, axis=-1, keepdims=True) + EPS)
        scaled = gain_ref[...] * total
        inner = jnp.mean(scaled * residual, axis=-1, keepdims=True)
        residual_grad = cot_ref[...].astype(F32) + (factor * scaled - residual * factor**3 * inner)
        residual_grad_ref[...] = residual_grad
        branch_ref[...] = residual_grad.astype(BF16)
        split_columns(branch_ref, split_ref)
        mlp_gain_ref[...] = jnp.sum(total * residual * factor, axis=0, keepdims=True)
        attended_grad = nt(branch_ref[...], out_weight_ref[...]).astype(BF16)
        for k in range(attended_grad_ref.shape[0]):
            attended_grad_ref[k] = attended_grad[:, k * dim : (k + 1) * dim]

    queries, keys, values = qkv_ref[:, :dim], qkv_ref[:, dim : 2 * dim], qkv_ref[:, 2 * dim :]
    attended_grad = attended_grad_ref[head]
    probs = head_probs(queries, keys, row_ref, col_ref)
    prob_grad = nt(attended_grad, values)
    inner = jnp.sum(probs * prob_grad, axis=-1, keepdims=True)
    score = (probs * (prob_grad - inner) * dim ** (-0.5)).astype(BF16)
    query_grad = nn(score, keys).astype(BF16).astype(F32)
    key_grad = tn(score, queries).astype(BF16).astype(F32)
    value_grad = tn(probs.astype(BF16), attended_grad)
    grad = jnp.concatenate(
        [
            turned_back(query_grad, cos_ref[...], sin_ref[...]).astype(BF16),
            turned_back(key_grad, cos_ref[...], sin_ref[...]).astype(BF16),
            value_grad.astype(BF16),
        ],
        axis=1,
    )
    projected_grad_ref[...] = grad
    bias_ref[...] = jnp.sum(grad.astype(F32), axis=0, keepdims=True)
    product = nt(grad, weight_ref[...])

    @pl.when(head == 0)
    def _():
        normed_grad_ref[...] = product

    @pl.when(head > 0)
    def _():
        normed_grad_ref[...] += product


def attention_back(inner, totals, residual, cotangent, gain, out_weight, qkv, weight, cosine, sine, row, col):
    count, width = residual.shape
    dim = cosine.shape[1]
    cols = 3 * dim
    heads = qkv.shape[1] // cols
    return pl.pallas_call(
        back_kernel,
        grid=(heads,),
        in_specs=[
            pl.BlockSpec(memory_space=pltpu.SMEM),
            *[whole(count // 2, width)] * 4,
            whole(count, width),
            whole(count, width),
            whole(1, width),
            whole(*out_weight.shape),
            pl.BlockSpec((count, cols), lambda h: (0, h)),
            pl.BlockSpec((width, cols), lambda h: (0, h)),
            whole(*cosine.shape),
            whole(*sine.shape),
            whole(1, count),
            whole(count, 1),
        ],
        out_specs=[
            whole(count, width),
            whole(count, width),
            whole(2, count, width // 2),
            pl.BlockSpec((count, cols), lambda h: (0, h)),
            pl.BlockSpec((1, cols), lambda h: (0, h)),
            whole(1, width),
        ],
        out_shape=[
            jax.ShapeDtypeStruct((count, width), F32),
            jax.ShapeDtypeStruct((count, width), F32),
            jax.ShapeDtypeStruct((2, count, width // 2), BF16),
            jax.ShapeDtypeStruct((count, heads * cols), BF16),
            jax.ShapeDtypeStruct((1, heads * cols), F32),
            jax.ShapeDtypeStruct((1, width), F32),
        ],
        scratch_shapes=[pltpu.VMEM((count, width), BF16), pltpu.VMEM((heads, count, dim), BF16)],
        compiler_params=pltpu.CompilerParams(
            dimension_semantics=("arbitrary",), vmem_limit_bytes=48 * 1024 * 1024
        ),
        cost_estimate=LIGHT,
        name="attention_back",
    )(inner, *totals, residual, cotangent, gain, out_weight, qkv, weight, cosine, sine, row, col)


def hidden(w_one, w_two, tokens, branch, route_row):
    units = w_two.shape[0]
    mix = nt(w_one, tokens)
    gate, up = mix[:units], mix[units:]
    back = nt(w_two, branch)
    sigma = lax.logistic(gate)
    silu = gate * sigma
    act = silu * up
    scaled = back * route_row
    gate_grad = scaled * up * (sigma + silu * (1.0 - sigma))
    mix_grad = jnp.concatenate([gate_grad.astype(BF16), (scaled * silu).astype(BF16)], axis=0)
    return act, back, (act * route_row).astype(BF16), mix_grad


def open_row(gate_rows, tokens):
    return lax.logistic(nt(gate_rows, tokens)[:1])


def own_kernel(experts, tok_ref, cot_ref, route_ref, gate_ref, w1_ref, w2_ref, out_top_ref, out_low_ref, dx_top_ref,
               dx_low_ref, logit_ref, open_ref):
    step = pl.program_id(0)
    group, units, width = w2_ref.shape
    shared = step * group >= experts

    @pl.when(step == 0)
    def _():
        for ref in (out_top_ref, out_low_ref, dx_top_ref, dx_low_ref):
            ref[...] = jnp.zeros_like(ref)
        logit_ref[...] = jnp.zeros_like(logit_ref)
        open_ref[...] = open_row(gate_ref[...], tok_ref[...])

    weighted, mix_grads = [], []
    for k in range(group):
        act, back, scaled, mix_grad = hidden(
            w1_ref[k].reshape(2 * units, width),
            w2_ref[k],
            tok_ref[...],
            cot_ref[...],
            jnp.where(shared, open_ref[...], route_ref[k]),
        )
        weighted.append(scaled)
        mix_grads.append(mix_grad)
        logit_ref[...] += jnp.where(shared, jnp.sum(act * back, axis=0, keepdims=True), 0.0)
    rows = out_top_ref.shape[0]
    out = tn(jnp.concatenate(weighted), w2_ref[...].reshape(group * units, width))
    out_top_ref[...] += out[:rows]
    out_low_ref[...] += out[rows:]
    dx = tn(jnp.concatenate(mix_grads), w1_ref[...].reshape(group * 2 * units, width))
    dx_top_ref[...] += dx[:rows]
    dx_low_ref[...] += dx[rows:]

    @pl.when(step == pl.num_programs(0) - 1)
    def _():
        opened = open_ref[...]
        logit = opened * (1.0 - opened) * logit_ref[...]
        logit_ref[...] = logit
        column = jnp.broadcast_to(logit, (8, logit.shape[1])).T[:, :1]
        dx_top_ref[...] += column[:rows] * gate_ref[:1].astype(F32)
        dx_low_ref[...] += column[rows:] * gate_ref[:1].astype(F32)


def own_mlp(tokens, cotangent, route, gate_rows, w1, w2):
    count, width = tokens.shape
    tiles, units = w2.shape[:2]
    experts = route.shape[0]
    group = 2
    return pl.pallas_call(
        functools.partial(own_kernel, experts),
        grid=(tiles // group,),
        in_specs=[
            whole(count, width),
            whole(count, width),
            pl.BlockSpec((group, 1, count), lambda i: (jnp.minimum(i, experts // group - 1), 0, 0)),
            whole(*gate_rows.shape),
            pl.BlockSpec((group, 2, units, width), lambda i: (i, 0, 0, 0)),
            pl.BlockSpec((group, units, width), lambda i: (i, 0, 0)),
        ],
        out_specs=[*[whole(count // 2, width)] * 4, whole(1, count)],
        out_shape=[
            *[jax.ShapeDtypeStruct((count // 2, width), F32)] * 4,
            jax.ShapeDtypeStruct((1, count), F32),
        ],
        scratch_shapes=[pltpu.VMEM((1, count), F32)],
        compiler_params=pltpu.CompilerParams(
            dimension_semantics=("arbitrary",), vmem_limit_bytes=VMEM_LIMIT
        ),
        cost_estimate=LIGHT,
        name="own_mlp",
    )(tokens, cotangent, route[:, None, :], gate_rows, w1, w2)


def chip_kernel(pieces, here, at_ref, *refs):
    token_refs, refs = refs[: sum(pieces)], refs[sum(pieces) :]
    cot_ref, route_ref, gate_ref, w1_ref, w2_ref = refs[:5]
    mix_grad_ref, weighted_ref, part_ref, tok_ref, open_ref = refs[-5:]
    step, which = pl.program_id(0), pl.program_id(1)
    units, width = w2_ref.shape[-2:]
    cores, experts, count = route_ref.shape
    core = at_ref[0]

    for chip in range(len(pieces) // 2):
        @pl.when((step == 0) & (which == chip))
        def _():
            for owner in range(2):
                base = count * (core if owner == 0 else 1 - core)
                first = sum(pieces[: 2 * chip + owner])
                for k, ref in enumerate(token_refs[first : first + pieces[2 * chip + owner]]):
                    rows = ref.shape[0]
                    tok_ref[chip, pl.ds(pl.multiple_of(base + k * rows, rows), rows), :] = ref[...].astype(BF16)
            open_ref[chip] = open_row(gate_ref[...], tok_ref[chip])

    part = part_ref.shape[1]
    part_ref[...] = tok_ref[which, :, pl.ds(pl.multiple_of(at_ref[1] * part, part), part)]
    expert = jnp.minimum(core * here + step, experts - 1)
    route_row = jnp.concatenate([route_ref[k, pl.ds(expert, 1), :] for k in range(cores)], axis=1)
    _, _, weighted, mix_grad = hidden(
        w1_ref[...].reshape(2 * units, width),
        w2_ref[0],
        tok_ref[which],
        cot_ref[...],
        jnp.where(step >= here, open_ref[which], route_row),
    )
    mix_grad_ref[0] = mix_grad
    weighted_ref[0] = weighted


def chip_hidden(at, tokens, cotangent, route, gate_rows, w1, w2, kept, part):
    total, width = cotangent.shape
    tiles, units = w2.shape[:2]
    experts, count = route.shape[1:]
    here, shared = experts // 2, (tiles - experts) // 2
    rows = 2 * count
    own = lambda i, at: jnp.where(i < here, at[0] * here + i, experts + at[0] * shared + i - here)
    chips = len(tokens) // 2
    pieces = tuple(len(t) for t in tokens)
    tokens = [v for t in tokens for v in t]
    fixed = lambda *shape: pl.BlockSpec(shape, lambda i, j, at: (0,) * len(shape), pipeline_mode=pl.Buffered(1))
    shapes = [
        jax.ShapeDtypeStruct((here + shared, 2 * units, total), BF16),
        jax.ShapeDtypeStruct((here + shared, units, total), BF16),
        jax.ShapeDtypeStruct((total, 2 * part), BF16),
    ]
    inputs = [*tokens, cotangent, route, gate_rows, w1, w2]
    return pl.pallas_call(
        functools.partial(chip_kernel, pieces, here),
        grid_spec=pltpu.PrefetchScalarGridSpec(
            num_scalar_prefetch=1,
            grid=(here + shared, chips),
            in_specs=[
                *[fixed(*v.shape) for v in tokens],
                pl.BlockSpec((rows, width), lambda i, j, at: (at[2 + j], 0)),
                pl.BlockSpec((2, experts, count), lambda i, j, at: (at[2 + j], 0, 0)),
                fixed(*gate_rows.shape),
                pl.BlockSpec((1, 2, units, width), lambda i, j, at: (own(i, at), 0, 0, 0)),
                pl.BlockSpec((1, units, width), lambda i, j, at: (own(i, at), 0, 0)),
                *[pl.BlockSpec(memory_space=pl.ANY) for _ in kept],
            ],
            out_specs=[
                pl.BlockSpec((1, 2 * units, rows), lambda i, j, at: (i, 0, at[2 + j])),
                pl.BlockSpec((1, units, rows), lambda i, j, at: (i, 0, at[2 + j])),
                pl.BlockSpec((rows, 2 * part), lambda i, j, at: (at[2 + j], 0)),
            ],
            scratch_shapes=[pltpu.VMEM((chips, rows, width), BF16), pltpu.VMEM((chips, 1, rows), F32)],
        ),
        out_shape=shapes,
        input_output_aliases={1 + len(inputs) + k: k for k in range(len(kept))},
        compiler_params=pltpu.CompilerParams(
            dimension_semantics=("arbitrary", "arbitrary"), vmem_limit_bytes=VMEM_LIMIT
        ),
        cost_estimate=LIGHT,
        name="chip_hidden",
    )(at, *inputs, *kept)


def weights_kernel(at_ref, mix_grad_ref, weighted_ref, tok_ref, cot_ref, one_mine_ref, one_peer_ref, two_mine_ref,
                   two_peer_ref):
    part = one_mine_ref.shape[-1]
    core = at_ref[0]
    one = nn(mix_grad_ref[0], tok_ref[...])
    two = nn(weighted_ref[0], cot_ref[...])
    for value, mine_ref, peer_ref in ((one, one_mine_ref, one_peer_ref), (two, two_mine_ref, two_peer_ref)):
        low, high = value[:, :part], value[:, part:]
        mine_ref[...] = jnp.where(core == 0, low, high).reshape(mine_ref.shape)
        peer_ref[...] = jnp.where(core == 0, high, low).reshape(peer_ref.shape)


def weight_grads(at, mix_grads, weighted, tokens, cotangent):
    tiles, units, total = weighted.shape
    part = tokens.shape[1] // 2
    one = jax.ShapeDtypeStruct((tiles, 2, units, part), F32)
    two = jax.ShapeDtypeStruct((tiles, units, part), F32)
    one_spec = pl.BlockSpec((1, 2, units, part), lambda i, at: (i, 0, 0, 0))
    two_spec = pl.BlockSpec((1, units, part), lambda i, at: (i, 0, 0))
    return pl.pallas_call(
        weights_kernel,
        grid_spec=pltpu.PrefetchScalarGridSpec(
            num_scalar_prefetch=1,
            grid=(tiles,),
            in_specs=[
                pl.BlockSpec((1, 2 * units, total), lambda i, at: (i, 0, 0)),
                pl.BlockSpec((1, units, total), lambda i, at: (i, 0, 0)),
                pl.BlockSpec((total, 2 * part), lambda i, at: (0, 0)),
                pl.BlockSpec((total, 2 * part), lambda i, at: (0, at[1])),
            ],
            out_specs=[one_spec, one_spec, two_spec, two_spec],
        ),
        out_shape=[one, one, two, two],
        compiler_params=pltpu.CompilerParams(
            dimension_semantics=("arbitrary",), vmem_limit_bytes=VMEM_LIMIT
        ),
        cost_estimate=LIGHT,
        name="weight_grads",
    )(at, mix_grads, weighted, tokens, cotangent)


def split_kernel(in_ref, out_ref, route_ref):
    count = out_ref.shape[0]
    out_ref[...] = in_ref[0, :count].astype(BF16)
    route_ref[...] = in_ref[0, count:, :count][None]


def split_rounded(gathered, count):
    blocks, rows, width = gathered.shape
    extra = rows - count
    return pl.pallas_call(
        split_kernel,
        grid=(blocks,),
        in_specs=[pl.BlockSpec((1, rows, width), lambda i: (i, 0, 0))],
        out_specs=[
            pl.BlockSpec((count, width), lambda i: (i, 0)),
            pl.BlockSpec((1, extra, count), lambda i: (i, 0, 0)),
        ],
        out_shape=[
            jax.ShapeDtypeStruct((blocks * count, width), BF16),
            jax.ShapeDtypeStruct((blocks, extra, count), F32),
        ],
        compiler_params=pltpu.CompilerParams(
            dimension_semantics=("arbitrary",), vmem_limit_bytes=32 * 1024 * 1024
        ),
        name="split_rounded",
    )(gathered)


def flip(value, bit):
    return lax.ppermute(value, "dp", [(i, i ^ bit) for i in range(8)])


def butterfly(value):
    value = value + flip(value, 1)
    for bit in (1, 2):
        value = value + lax.ppermute(value, "tensor", [(i, i ^ bit) for i in range(4)])
    for bit in (2, 4):
        value = value + flip(value, bit)
    return value


def take(value, number, axis):
    return lax.dynamic_index_in_dim(value, number, axis, keepdims=False)


def scatter_first(held, me):
    along_x, along_y = (me // 2) % 2, me // 4
    half = held.shape[-1] // 256 * 128
    a, b = held[..., :half], held[..., half:]
    return (take(a, along_x, 1), take(a, 1 - along_x, 1), take(b, along_y, 0), take(b, 1 - along_y, 0))


def scatter_second(a, b, me):
    along_x, along_y = (me // 2) % 2, me // 4
    a = take(a, along_y, 0) + flip(take(a, 1 - along_y, 0), 4)
    b = take(b, along_x, 0) + flip(take(b, 1 - along_x, 0), 2)
    return jnp.concatenate([a, b], axis=-1)


def shards(
    n_dp,
    n_tensor,
    layer_input,
    doc_ids,
    expert_ids,
    route_weights,
    attn_gain,
    qkv_weight,
    qkv_bias,
    out_weight,
    mlp_gain,
    expert_gate_up,
    expert_down,
    shared_gate_up,
    shared_down,
    shared_gate,
    cotangent,
):
    count, width = layer_input.shape
    heads_here = qkv_bias.shape[0]
    head_dim = qkv_bias.shape[1] // 3
    experts, units = expert_down.shape[:2]
    shared = shared_down.shape[0] // units
    part = width // n_dp
    me = lax.axis_index("dp")
    core, chip = me % 2, me // 2
    tied = lax.optimization_barrier

    choose = expert_ids[:, :, None] == jnp.arange(experts, dtype=jnp.int32)[None, None, :]
    route = jnp.sum(route_weights[:, :, None] * choose.astype(F32), axis=1).T
    cot_all = lax.all_gather(
        jnp.concatenate([cotangent.astype(F32), jnp.pad(route, ((0, 0), (0, width - count)))], axis=0), "dp"
    )
    gate_rows = jnp.broadcast_to(shared_gate[None, :], (16, width))
    index = jnp.arange(count, dtype=jnp.int32)
    place = (me * count + index - doc_ids).astype(F32)
    freq = ROPE_BASE ** (-(jnp.arange(head_dim // 2, dtype=F32) * 2.0 / head_dim))
    angle = place[:, None] * freq[None, :]
    cosine = jnp.concatenate([jnp.cos(angle), jnp.cos(angle)], axis=-1)
    sine = jnp.concatenate([-jnp.sin(angle), jnp.sin(angle)], axis=-1)
    row, col = doc_ids[None, :], doc_ids[:, None]
    gain_one = attn_gain.astype(F32)[None, :]
    gain_two = mlp_gain.astype(F32)[None, :]
    attn_part, normed_one, qkv, attended = attention(
        layer_input, gain_one, qkv_weight, qkv_bias.astype(F32)[:, None, :], cosine, sine, row, col, out_weight
    )

    attn_part, shared_gate_up = tied((attn_part, shared_gate_up))
    attn_sum = lax.psum(attn_part, "tensor")
    w1 = jnp.concatenate(
        [
            jnp.transpose(expert_gate_up, (0, 2, 3, 1)),
            jnp.transpose(shared_gate_up.reshape(width, 2, shared, units), (2, 1, 3, 0)),
        ]
    )
    w2 = jnp.concatenate([expert_down, shared_down.reshape(shared, units, width)])
    cot_low, route_all = split_rounded(cot_all, count)
    attn_sum, w1, w2, cot_low, route_all = tied((attn_sum, w1, w2, cot_low, route_all))

    residual, tokens, tokens_wide = second_norm(layer_input, attn_sum, gain_two)
    if n_dp == 8:
        over_x, over_y = flip(tokens_wide, 2), flip(tokens_wide, 4)
        beside = flip(tokens_wide, 1)
    else:
        tok_all = lax.all_gather(tokens_wide, "dp")
    mlp_top, mlp_low, grad_top, grad_low, logit_grad = own_mlp(tokens, cotangent, route, gate_rows, w1, w2)
    line = n_tensor == 4 and n_dp == 8
    spot = lax.axis_index("tensor")
    hide = lambda chips, tokens, kept: chip_hidden(
        jnp.stack([core, chip, *chips]), tokens, cot_low, route_all, gate_rows, w1, w2, kept, part
    )
    if line:
        is_inner = (spot == 1) | (spot == 2)
        inwards = lambda v: lax.ppermute(v, "tensor", [(0, 1), (3, 2)])
        across = lambda v: lax.ppermute(v, "tensor", [(1, 2), (2, 1)])
        outwards = lambda v: lax.ppermute(v, "tensor", [(1, 0), (2, 3)])
        ready = jnp.isnan(logit_grad[0, 0]).astype(jnp.int32)
        over_x, over_y, ready = tied((over_x, over_y, ready))
        low, high = flip(over_x[: count // 2], 4), flip(over_y[count // 2 :], 2)
        beside_x, beside_y = flip(over_x, 1), flip(over_y, 1)
        got = inwards(grad_top)
        kept = hide([chip + ready], [[tokens_wide], [beside]], [])
        got, beside_x, beside_y, grad_low, kept = tied((got, beside_x, beside_y, grad_low, kept))
        grad_top = grad_top + got
        got, got_low = across(grad_top), inwards(grad_low)
        kept = hide([chip ^ 1], [[over_x], [beside_x]], kept)
        got, got_low, low, high, mlp_top, kept = tied((got, got_low, low, high, mlp_top, kept))
        grad_top, grad_low = grad_top + got, grad_low + got_low
        end_top, got_low, got = outwards(grad_top), across(grad_low), inwards(mlp_top)
        beside_low, beside_high = flip(low, 1), flip(high, 1)
        kept = hide([chip ^ 2], [[over_y], [beside_y]], kept)
        end_top, got_low, got, mlp_low, beside_low, beside_high, kept = tied(
            (end_top, got_low, got, mlp_low, beside_low, beside_high, kept)
        )
        grad_low, mlp_top = grad_low + got_low, mlp_top + got
        end_low, got, got_low = outwards(grad_low), across(mlp_top), inwards(mlp_low)
        kept = hide([chip ^ 3], [[low, high], [beside_low, beside_high]], kept)
        end_low, got, got_low, kept = tied((end_low, got, got_low, kept))
        totals = [grad_top, end_top, grad_low, end_low]
    else:
        is_inner = spot >= 0
        kept = []
        for k in range(n_dp // 2):
            kept = hide([k], [[take(tok_all, 2 * k + core, 0)], [take(tok_all, 2 * k + 1 - core, 0)]], kept)
        totals = [lax.psum(v, "tensor") for v in (grad_top, grad_low)]
        totals = [totals[0], totals[0], totals[1], totals[1]]

    normed_one_part, residual_grad, branch_grad, projected_grad, bias_part, mlp_gain_part = attention_back(
        is_inner.astype(jnp.int32)[None], totals, residual, cotangent, gain_two, out_weight, qkv, qkv_weight,
        cosine, sine, row, col,
    )
    normed_one_total = lax.psum_scatter(normed_one_part, "tensor", scatter_dimension=0, tiled=True)
    few = count // n_tensor
    inputs = layer_input.astype(F32)
    factor_one = lax.rsqrt(jnp.mean(inputs * inputs, axis=-1, keepdims=True) + EPS)
    attn_gain_part = jnp.sum(normed_one_part * inputs * factor_one, axis=0)
    shared_gate_part = jnp.sum(logit_grad[0][:, None] * tokens.astype(F32), axis=0)
    my_slot = spot == jnp.arange(n_tensor)
    small = jnp.concatenate(
        [
            attn_gain_part,
            mlp_gain_part[0] * my_slot[0],
            shared_gate_part,
            (my_slot[:, None] * bias_part).reshape(-1),
        ]
    )
    swap = lambda v: lax.ppermute(v, "dp", [(i, i ^ 1) for i in range(n_dp)])
    own_rows = lambda v: lax.dynamic_slice_in_dim(v, spot * few, few, 0)

    if line:
        def products(c):
            return (
                tn(take(normed_one, c, 0), projected_grad).reshape(2, 2, part, -1),
                tn(take(branch_grad, c, 0), attended).reshape(2, 2, part, -1),
            )

        arrived = [flip(v, 1) for v in products(1 - core)]
        small = butterfly(small.reshape(-1, 128)).reshape(-1)
        small, arrived = tied((small, arrived))
        got, got_low, residual_grad = tied((got, got_low, residual_grad))
        mlp_top, mlp_low = mlp_top + got, mlp_low + got_low
        end_top, got_low = outwards(mlp_top), across(mlp_low)
        held = products(core)
        firsts = [scatter_first(h + v, me) for h, v in zip(held, arrived, strict=True)]
        firsts, kept = tied((firsts, kept))
        moved = [(flip(a_other, 2), flip(b_other, 4)) for _, a_other, _, b_other in firsts]
        one_mine, one_peer, two_mine, two_peer = weight_grads(jnp.stack([core, chip]), *kept, cot_low)
        one_mine, one_peer, normed_one_total = tied((one_mine, one_peer, normed_one_total))
        one_peer, two_peer = swap(one_peer), swap(two_peer)
        input_grad = norm_back(own_rows(inputs), own_rows(factor_one), gain_one, normed_one_total)
        input_grad, moved, end_top, got_low = tied((input_grad, moved, end_top, got_low))
        input_grad = lax.all_gather(input_grad, "tensor", axis=0, tiled=True)
        mlp_low = mlp_low + got_low
        end_low = outwards(mlp_low)
        steps = [(a + a_in, b + b_in) for (a, _, b, _), (a_in, b_in) in zip(firsts, moved, strict=True)]
        qkv_weight_grad, out_weight_grad = [scatter_second(a, b, me) for a, b in steps]
        out_weight_grad = out_weight_grad.T
        mlp_sum = jnp.where(
            is_inner, jnp.concatenate([mlp_top, mlp_low]), jnp.concatenate([end_top, end_low])
        )
    else:
        small = lax.psum(small, ("dp", "tensor"))
        one_mine, one_peer, two_mine, two_peer = weight_grads(jnp.stack([core, chip]), *kept, cot_low)
        one_peer, two_peer = swap(one_peer), swap(two_peer)
        input_grad = norm_back(own_rows(inputs), own_rows(factor_one), gain_one, normed_one_total)
        input_grad = lax.all_gather(input_grad, "tensor", axis=0, tiled=True)
        joint = lambda v: v.reshape(2, count, BLOCKS // 2, -1).transpose(1, 2, 0, 3).reshape(count, width)
        out_weight_grad = lax.psum_scatter(tn(attended, joint(branch_grad)), "dp", scatter_dimension=1, tiled=True)
        qkv_weight_grad = lax.psum_scatter(
            tn(joint(normed_one), projected_grad), "dp", scatter_dimension=0, tiled=True
        )
        mlp_sum = lax.psum(jnp.concatenate([mlp_top, mlp_low]), "tensor")

    gains = lax.dynamic_slice(small[: 3 * width].reshape(3, width), (0, me * part), (3, part))
    bias = take(small[3 * width :].reshape(n_tensor, heads_here, 3 * head_dim), spot, 0)
    bias_cols = 3 * head_dim // n_dp
    qkv_bias_grad = lax.dynamic_slice(bias, (0, me * bias_cols), (heads_here, bias_cols))
    input_grad = (residual_grad + input_grad).astype(BF16)
    layer_output = (residual + mlp_sum).astype(BF16)

    def joined(mine, peer):
        return jnp.where(core == 0, jnp.concatenate([mine, peer]), jnp.concatenate([peer, mine]))

    half = experts // 2
    expert_gate_up_grad = jnp.transpose(joined(one_mine[:half], one_peer[:half]), (0, 3, 1, 2))
    expert_down_grad = joined(two_mine[:half], two_peer[:half])
    shared_gate_up_grad = jnp.transpose(joined(one_mine[half:], one_peer[half:]), (3, 1, 0, 2)).reshape(
        part, 2, shared * units
    )
    shared_down_grad = joined(two_mine[half:], two_peer[half:]).reshape(shared * units, part)
    return (
        layer_output,
        input_grad,
        gains[0],
        qkv_weight_grad,
        qkv_bias_grad,
        out_weight_grad,
        gains[1],
        expert_gate_up_grad,
        expert_down_grad,
        shared_gate_up_grad,
        shared_down_grad,
        gains[2],
    )


def solution(mesh):
    placed = (
        P("dp", None),
        P("dp"),
        P("dp", None),
        P("dp", None),
        P(),
        P(None, "tensor"),
        P("tensor", None),
        P("tensor", None),
        P(),
        P(None, None, None, "tensor"),
        P(None, "tensor", None),
        P(None, None, "tensor"),
        P("tensor", None),
        P(),
        P("dp", None),
    )
    return jax.shard_map(
        functools.partial(shards, mesh.shape["dp"], mesh.shape["tensor"]),
        mesh=mesh,
        in_specs=placed,
        out_specs=(
            P("dp", None),
            P("dp", None),
            P("dp"),
            P("dp", "tensor"),
            P("tensor", "dp"),
            P("tensor", "dp"),
            P("dp"),
            P(None, "dp", None, "tensor"),
            P(None, "tensor", "dp"),
            P("dp", None, "tensor"),
            P("tensor", "dp"),
            P("dp"),
        ),
        check_vma=False,
    )
```

```python
import functools

import jax
import jax.numpy as jnp
from jax import lax
from jax.experimental import pallas as pl
from jax.experimental.pallas import tpu as pltpu
from jax.sharding import PartitionSpec as P

EPS = 1e-06
ROPE_BASE = 1000000.0
NEG = -1e30
F32 = jnp.float32
BF16 = jnp.bfloat16
VMEM_LIMIT = 60 * 1024 * 1024
BLOCKS = 8
LIGHT = pl.CostEstimate(flops=1 << 20, bytes_accessed=1 << 16, transcendentals=0)


def nt(left, right):
    return lax.dot_general(left, right, (((1,), (1,)), ((), ())), preferred_element_type=F32)


def tn(left, right):
    return lax.dot_general(left, right, (((0,), (0,)), ((), ())), preferred_element_type=F32)


def nn(left, right):
    return jnp.dot(left, right, preferred_element_type=F32)


def norm_back(values_in, factor, gain_vec, upstream):
    scaled = gain_vec * upstream
    inner = jnp.mean(scaled * values_in, axis=-1, keepdims=True)
    return factor * scaled - values_in * factor**3 * inner


def turned(values, cosine, sine):
    return values * cosine + pltpu.roll(values, values.shape[1] // 2, 1) * sine


def turned_back(values, cosine, sine):
    return values * cosine - pltpu.roll(values, values.shape[1] // 2, 1) * sine


def head_probs(queries, keys, row_ref, col_ref):
    count = queries.shape[0]
    scores = nt(queries, keys) * queries.shape[1] ** (-0.5)
    rows = lax.broadcasted_iota(jnp.int32, (count, count), 0)
    cols = lax.broadcasted_iota(jnp.int32, (count, count), 1)
    scores = jnp.where((col_ref[...] == row_ref[...]) & (cols <= rows), scores, NEG)
    exponent = jnp.exp(scores - jnp.max(scores, axis=-1, keepdims=True))
    return exponent / jnp.sum(exponent, axis=-1, keepdims=True)


def split_columns(whole_ref, split_ref):
    part = whole_ref.shape[1] // BLOCKS
    for k in range(BLOCKS):
        split_ref[k % 2, :, k // 2 * part : (k // 2 + 1) * part] = whole_ref[:, k * part : (k + 1) * part]


def attn_kernel(x_ref, gain_ref, weight_ref, bias_ref, cos_ref, sin_ref, row_ref, col_ref, out_weight_ref,
                part_ref, split_ref, qkv_ref, attended_ref, normed_ref):
    head = pl.program_id(0)
    dim = cos_ref.shape[1]

    @pl.when(head == 0)
    def _():
        values = x_ref[...].astype(F32)
        factor = lax.rsqrt(jnp.mean(values * values, axis=-1, keepdims=True) + EPS)
        normed_ref[...] = (values * factor * gain_ref[...]).astype(BF16)
        split_columns(normed_ref, split_ref)

    projected = nn(normed_ref[...], weight_ref[...]) + bias_ref[0]
    queries = turned(projected[:, :dim], cos_ref[...], sin_ref[...]).astype(BF16)
    keys = turned(projected[:, dim : 2 * dim], cos_ref[...], sin_ref[...]).astype(BF16)
    values = projected[:, 2 * dim :].astype(BF16)
    qkv_ref[:, :dim] = queries
    qkv_ref[:, dim : 2 * dim] = keys
    qkv_ref[:, 2 * dim :] = values
    probs = head_probs(queries, keys, row_ref, col_ref)
    cols = pl.ds(pl.multiple_of(head * dim, dim), dim)
    attended_ref[:, cols] = nn(probs.astype(BF16), values).astype(BF16)

    @pl.when(head == pl.num_programs(0) - 1)
    def _():
        part_ref[...] = nn(attended_ref[...], out_weight_ref[...])


def whole(*shape):
    return pl.BlockSpec(shape, lambda *at: (0,) * len(shape))


def attention(x, gain, weight, bias, cosine, sine, row, col, out_weight):
    count, width = x.shape
    heads, _, cols = bias.shape
    return pl.pallas_call(
        attn_kernel,
        grid=(heads,),
        in_specs=[
            whole(count, width),
            whole(1, width),
            pl.BlockSpec((width, cols), lambda h: (0, h)),
            pl.BlockSpec((1, 1, cols), lambda h: (h, 0, 0)),
            whole(*cosine.shape),
            whole(*sine.shape),
            whole(1, count),
            whole(count, 1),
            whole(*out_weight.shape),
        ],
        out_specs=[
            whole(count, width),
            whole(2, count, width // 2),
            pl.BlockSpec((count, cols), lambda h: (0, h)),
            whole(count, out_weight.shape[0]),
        ],
        out_shape=[
            jax.ShapeDtypeStruct((count, width), F32),
            jax.ShapeDtypeStruct((2, count, width // 2), BF16),
            jax.ShapeDtypeStruct((count, heads * cols), BF16),
            jax.ShapeDtypeStruct((count, out_weight.shape[0]), BF16),
        ],
        scratch_shapes=[pltpu.VMEM((count, width), BF16)],
        compiler_params=pltpu.CompilerParams(
            dimension_semantics=("arbitrary",), vmem_limit_bytes=32 * 1024 * 1024
        ),
        cost_estimate=LIGHT,
        name="attention",
    )(x, gain, weight, bias, cosine, sine, row, col, out_weight)


def norm_kernel(x_ref, sum_ref, gain_ref, residual_ref, low_ref, wide_ref):
    residual = x_ref[...].astype(F32) + sum_ref[...]
    factor = lax.rsqrt(jnp.mean(residual * residual, axis=-1, keepdims=True) + EPS)
    low = (residual * factor * gain_ref[...]).astype(BF16)
    residual_ref[...] = residual
    low_ref[...] = low
    wide_ref[...] = low.astype(F32)


def second_norm(x, attn_sum, gain):
    count, width = x.shape
    rows = count // 4
    spec = pl.BlockSpec((rows, width), lambda i: (i, 0))
    return pl.pallas_call(
        norm_kernel,
        grid=(4,),
        in_specs=[spec, spec, whole(1, width)],
        out_specs=[spec, spec, spec],
        out_shape=[
            jax.ShapeDtypeStruct((count, width), F32),
            jax.ShapeDtypeStruct((count, width), BF16),
            jax.ShapeDtypeStruct((count, width), F32),
        ],
        compiler_params=pltpu.CompilerParams(
            dimension_semantics=("arbitrary",), vmem_limit_bytes=32 * 1024 * 1024
        ),
        name="second_norm",
    )(x, attn_sum, gain)


def back_kernel(inner_ref, held_top_ref, got_top_ref, held_low_ref, got_low_ref, residual_ref, cot_ref, gain_ref, out_weight_ref, qkv_ref, weight_ref, cos_ref, sin_ref,
                row_ref, col_ref, x_ref, extra_ref, normed_grad_ref, residual_grad_ref, split_ref, projected_grad_ref, bias_ref,
                mlp_gain_ref, branch_ref, attended_grad_ref):
    head = pl.program_id(0)
    dim = cos_ref.shape[1]

    @pl.when(head == 0)
    def _():
        total = jnp.where(
            inner_ref[0] == 1,
            jnp.concatenate([held_top_ref[...], held_low_ref[...]]),
            jnp.concatenate([got_top_ref[...], got_low_ref[...]]),
        )
        residual = residual_ref[...]
        factor = lax.rsqrt(jnp.mean(residual * residual, axis=-1, keepdims=True) + EPS)
        scaled = gain_ref[...] * total
        inner = jnp.mean(scaled * residual, axis=-1, keepdims=True)
        residual_grad = cot_ref[...].astype(F32) + (factor * scaled - residual * factor**3 * inner)
        residual_grad_ref[...] = residual_grad
        branch_ref[...] = residual_grad.astype(BF16)
        split_columns(branch_ref, split_ref)
        mlp_gain_ref[...] = jnp.sum(total * residual * factor, axis=0, keepdims=True)
        attended_grad = nt(branch_ref[...], out_weight_ref[...]).astype(BF16)
        for k in range(attended_grad_ref.shape[0]):
            attended_grad_ref[k] = attended_grad[:, k * dim : (k + 1) * dim]

    queries, keys, values = qkv_ref[:, :dim], qkv_ref[:, dim : 2 * dim], qkv_ref[:, 2 * dim :]
    attended_grad = attended_grad_ref[head]
    probs = head_probs(queries, keys, row_ref, col_ref)
    prob_grad = nt(attended_grad, values)
    inner = jnp.sum(probs * prob_grad, axis=-1, keepdims=True)
    score = (probs * (prob_grad - inner) * dim ** (-0.5)).astype(BF16)
    query_grad = nn(score, keys).astype(BF16).astype(F32)
    key_grad = tn(score, queries).astype(BF16).astype(F32)
    value_grad = tn(probs.astype(BF16), attended_grad)
    grad = jnp.concatenate(
        [
            turned_back(query_grad, cos_ref[...], sin_ref[...]).astype(BF16),
            turned_back(key_grad, cos_ref[...], sin_ref[...]).astype(BF16),
            value_grad.astype(BF16),
        ],
        axis=1,
    )
    projected_grad_ref[...] = grad
    bias_ref[...] = jnp.sum(grad.astype(F32), axis=0, keepdims=True)
    product = nt(grad, weight_ref[...])
    groups, few = normed_grad_ref.shape[0], normed_grad_ref.shape[1] - 8

    @pl.when(head == 0)
    def _():
        for k in range(groups):
            normed_grad_ref[k, :few] = product[k * few : (k + 1) * few]

    @pl.when(head > 0)
    def _():
        for k in range(groups):
            normed_grad_ref[k, :few] += product[k * few : (k + 1) * few]

    @pl.when(head == pl.num_programs(0) - 1)
    def _():
        total = jnp.zeros((1, x_ref.shape[1]), F32)
        for k in range(groups):
            x = x_ref[k * few : (k + 1) * few].astype(F32)
            factor = lax.rsqrt(jnp.mean(x * x, axis=-1, keepdims=True) + EPS)
            total += jnp.sum(normed_grad_ref[k, :few] * x * factor, axis=0, keepdims=True)
        rows = lax.broadcasted_iota(jnp.int32, (8, x_ref.shape[1]), 0)
        small = jnp.where(rows == 0, total, jnp.where(rows == 1, extra_ref[...], 0.0))
        for k in range(groups):
            normed_grad_ref[k, few:] = small


def attention_back(inner, totals, residual, cotangent, gain, out_weight, qkv, weight, cosine, sine, row, col, x, extra,
                   groups):
    count, width = residual.shape
    dim = cosine.shape[1]
    cols = 3 * dim
    heads = qkv.shape[1] // cols
    return pl.pallas_call(
        back_kernel,
        grid=(heads,),
        in_specs=[
            pl.BlockSpec(memory_space=pltpu.SMEM),
            *[whole(count // 2, width)] * 4,
            whole(count, width),
            whole(count, width),
            whole(1, width),
            whole(*out_weight.shape),
            pl.BlockSpec((count, cols), lambda h: (0, h)),
            pl.BlockSpec((width, cols), lambda h: (0, h)),
            whole(*cosine.shape),
            whole(*sine.shape),
            whole(1, count),
            whole(count, 1),
            whole(count, width),
            whole(1, width),
        ],
        out_specs=[
            whole(groups, count // groups + 8, width),
            whole(count, width),
            whole(2, count, width // 2),
            pl.BlockSpec((count, cols), lambda h: (0, h)),
            pl.BlockSpec((1, cols), lambda h: (0, h)),
            whole(1, width),
        ],
        out_shape=[
            jax.ShapeDtypeStruct((groups, count // groups + 8, width), F32),
            jax.ShapeDtypeStruct((count, width), F32),
            jax.ShapeDtypeStruct((2, count, width // 2), BF16),
            jax.ShapeDtypeStruct((count, heads * cols), BF16),
            jax.ShapeDtypeStruct((1, heads * cols), F32),
            jax.ShapeDtypeStruct((1, width), F32),
        ],
        scratch_shapes=[pltpu.VMEM((count, width), BF16), pltpu.VMEM((heads, count, dim), BF16)],
        compiler_params=pltpu.CompilerParams(
            dimension_semantics=("arbitrary",), vmem_limit_bytes=48 * 1024 * 1024
        ),
        cost_estimate=LIGHT,
        name="attention_back",
    )(inner, *totals, residual, cotangent, gain, out_weight, qkv, weight, cosine, sine, row, col, x, extra)


def hidden(w_one, w_two, tokens, branch, route_row):
    units = w_two.shape[0]
    mix = nt(w_one, tokens)
    gate, up = mix[:units], mix[units:]
    back = nt(w_two, branch)
    sigma = lax.logistic(gate)
    silu = gate * sigma
    act = silu * up
    scaled = back * route_row
    gate_grad = scaled * up * (sigma + silu * (1.0 - sigma))
    mix_grad = jnp.concatenate([gate_grad.astype(BF16), (scaled * silu).astype(BF16)], axis=0)
    return act, back, (act * route_row).astype(BF16), mix_grad


def open_row(gate_rows, tokens):
    return lax.logistic(nt(gate_rows, tokens)[:1])


def own_kernel(experts, tok_ref, cot_ref, route_ref, gate_ref, w1_ref, w2_ref, out_top_ref, out_low_ref, dx_top_ref,
               dx_low_ref, logit_ref, open_ref):
    step = pl.program_id(0)
    group, units, width = w2_ref.shape
    shared = step * group >= experts

    @pl.when(step == 0)
    def _():
        for ref in (out_top_ref, out_low_ref, dx_top_ref, dx_low_ref):
            ref[...] = jnp.zeros_like(ref)
        logit_ref[...] = jnp.zeros_like(logit_ref)
        open_ref[...] = open_row(gate_ref[...], tok_ref[...])

    weighted, mix_grads = [], []
    for k in range(group):
        act, back, scaled, mix_grad = hidden(
            w1_ref[k].reshape(2 * units, width),
            w2_ref[k],
            tok_ref[...],
            cot_ref[...],
            jnp.where(shared, open_ref[...], route_ref[k]),
        )
        weighted.append(scaled)
        mix_grads.append(mix_grad)
        logit_ref[...] += jnp.where(shared, jnp.sum(act * back, axis=0, keepdims=True), 0.0)
    rows = out_top_ref.shape[0]
    out = tn(jnp.concatenate(weighted), w2_ref[...].reshape(group * units, width))
    out_top_ref[...] += out[:rows]
    out_low_ref[...] += out[rows:]
    dx = tn(jnp.concatenate(mix_grads), w1_ref[...].reshape(group * 2 * units, width))
    dx_top_ref[...] += dx[:rows]
    dx_low_ref[...] += dx[rows:]

    @pl.when(step == pl.num_programs(0) - 1)
    def _():
        opened = open_ref[...]
        logit = opened * (1.0 - opened) * logit_ref[...]
        logit_ref[...] = logit
        column = jnp.broadcast_to(logit, (8, logit.shape[1])).T[:, :1]
        dx_top_ref[...] += column[:rows] * gate_ref[:1].astype(F32)
        dx_low_ref[...] += column[rows:] * gate_ref[:1].astype(F32)


def own_mlp(tokens, cotangent, route, gate_rows, w1, w2):
    count, width = tokens.shape
    tiles, units = w2.shape[:2]
    experts = route.shape[0]
    group = 2
    return pl.pallas_call(
        functools.partial(own_kernel, experts),
        grid=(tiles // group,),
        in_specs=[
            whole(count, width),
            whole(count, width),
            pl.BlockSpec((group, 1, count), lambda i: (jnp.minimum(i, experts // group - 1), 0, 0)),
            whole(*gate_rows.shape),
            pl.BlockSpec((group, 2, units, width), lambda i: (i, 0, 0, 0)),
            pl.BlockSpec((group, units, width), lambda i: (i, 0, 0)),
        ],
        out_specs=[*[whole(count // 2, width)] * 4, whole(1, count)],
        out_shape=[
            *[jax.ShapeDtypeStruct((count // 2, width), F32)] * 4,
            jax.ShapeDtypeStruct((1, count), F32),
        ],
        scratch_shapes=[pltpu.VMEM((1, count), F32)],
        compiler_params=pltpu.CompilerParams(
            dimension_semantics=("arbitrary",), vmem_limit_bytes=VMEM_LIMIT
        ),
        cost_estimate=LIGHT,
        name="own_mlp",
    )(tokens, cotangent, route[:, None, :], gate_rows, w1, w2)


def chip_kernel(here, at_ref, even_ref, odd_ref, cot_ref, route_ref, gate_ref, w1_ref, w2_ref, *refs):
    mix_grad_ref, weighted_ref, part_ref, tok_ref, open_ref = refs[-5:]
    step = pl.program_id(0)
    units, width = w2_ref.shape[-2:]
    cores, experts, count = route_ref.shape
    core = at_ref[0]

    @pl.when(step == 0)
    def _():
        for start, ref in ((at_ref[3], even_ref), (at_ref[4], odd_ref)):
            tok_ref[pl.ds(pl.multiple_of(start, count), count), :] = ref[...].reshape(count, width).astype(BF16)
        part = part_ref.shape[1]
        part_ref[...] = tok_ref[:, pl.ds(pl.multiple_of(at_ref[1] * part, part), part)]
        open_ref[...] = open_row(gate_ref[...], tok_ref[...])

    expert = jnp.minimum(core * here + step, experts - 1)
    route_row = jnp.concatenate([route_ref[k, pl.ds(expert, 1), :] for k in range(cores)], axis=1)
    _, _, weighted, mix_grad = hidden(
        w1_ref[...].reshape(2 * units, width),
        w2_ref[0],
        tok_ref[...],
        cot_ref[...],
        jnp.where(step >= here, open_ref[...], route_row),
    )
    mix_grad_ref[0] = mix_grad
    weighted_ref[0] = weighted


def chip_hidden(at, tokens, cotangent, route, gate_rows, w1, w2, kept, part):
    total, width = cotangent.shape
    tiles, units = w2.shape[:2]
    experts, count = route.shape[1:]
    here, shared = experts // 2, (tiles - experts) // 2
    rows = 2 * count
    own = lambda i, at: jnp.where(i < here, at[0] * here + i, experts + at[0] * shared + i - here)
    fixed = lambda *shape: pl.BlockSpec(shape, lambda i, at: (0,) * len(shape))
    if len(tokens) == 2:
        sources = [fixed(count, width), fixed(count, width)]
    else:
        tokens = [tokens[0], tokens[0]]
        sources = [
            pl.BlockSpec((1, count, width), lambda i, at: (2 * at[2], 0, 0)),
            pl.BlockSpec((1, count, width), lambda i, at: (2 * at[2] + 1, 0, 0)),
        ]
    shapes = [
        jax.ShapeDtypeStruct((here + shared, 2 * units, total), BF16),
        jax.ShapeDtypeStruct((here + shared, units, total), BF16),
        jax.ShapeDtypeStruct((total, 2 * part), BF16),
    ]
    inputs = [*tokens, cotangent, route, gate_rows, w1, w2]
    return pl.pallas_call(
        functools.partial(chip_kernel, here),
        grid_spec=pltpu.PrefetchScalarGridSpec(
            num_scalar_prefetch=1,
            grid=(here + shared,),
            in_specs=[
                *sources,
                pl.BlockSpec((rows, width), lambda i, at: (at[2], 0)),
                pl.BlockSpec((2, experts, count), lambda i, at: (at[2], 0, 0)),
                fixed(*gate_rows.shape),
                pl.BlockSpec((1, 2, units, width), lambda i, at: (own(i, at), 0, 0, 0)),
                pl.BlockSpec((1, units, width), lambda i, at: (own(i, at), 0, 0)),
                *[pl.BlockSpec(memory_space=pl.ANY) for _ in kept],
            ],
            out_specs=[
                pl.BlockSpec((1, 2 * units, rows), lambda i, at: (i, 0, at[2])),
                pl.BlockSpec((1, units, rows), lambda i, at: (i, 0, at[2])),
                pl.BlockSpec((rows, 2 * part), lambda i, at: (at[2], 0)),
            ],
            scratch_shapes=[pltpu.VMEM((rows, width), BF16), pltpu.VMEM((1, rows), F32)],
        ),
        out_shape=shapes,
        input_output_aliases={1 + len(inputs) + k: k for k in range(len(kept))},
        compiler_params=pltpu.CompilerParams(
            dimension_semantics=("arbitrary",), vmem_limit_bytes=VMEM_LIMIT
        ),
        cost_estimate=LIGHT,
        name="chip_hidden",
    )(at, *inputs, *kept)


def both_products(normed_ref, projected_ref, branch_ref, attended_ref):
    return jnp.concatenate(
        [tn(normed_ref[0], projected_ref[...]), tn(branch_ref[0], attended_ref[...])], axis=1
    )


def sent_kernel(at_ref, normed_ref, projected_ref, branch_ref, attended_ref, out_ref):
    out_ref[0] = both_products(normed_ref, projected_ref, branch_ref, attended_ref)


def held_kernel(at_ref, normed_ref, projected_ref, branch_ref, attended_ref, arrived_ref, *out_refs):
    block = pl.program_id(0)
    along_y, along_x = block // 2, lax.rem(block, 2)
    value = both_products(normed_ref, projected_ref, branch_ref, attended_ref) + arrived_ref[0]
    half = value.shape[1] // 2
    x_keep_ref, x_send_ref, y_keep_ref, y_send_ref = out_refs
    for same, index, columns, keep_ref, send_ref in (
        (along_x == at_ref[1], along_y, value[:, :half], x_keep_ref, x_send_ref),
        (along_y == at_ref[2], along_x, value[:, half:], y_keep_ref, y_send_ref),
    ):
        @pl.when(same)
        def _():
            keep_ref[index] = columns

        @pl.when(jnp.logical_not(same))
        def _():
            send_ref[index] = columns


def token_products(at, normed, projected, branch, attended, arrived):
    _, count, half = normed.shape
    blocks = BLOCKS // 2
    part = half // blocks
    cols = projected.shape[1] + attended.shape[1]
    side = pl.BlockSpec((1, count, part), lambda i, at: (at[0], 0, i))
    fixed = lambda *shape: pl.BlockSpec(shape, lambda i, at: (0,) * len(shape))
    block = pl.BlockSpec((1, part, cols), lambda i, at: (i, 0, 0))
    inputs = [normed, projected, branch, attended]
    in_specs = [side, fixed(*projected.shape), side, fixed(*attended.shape)]
    if arrived is None:
        kernel, out_specs = sent_kernel, block
        out_shape = jax.ShapeDtypeStruct((blocks, part, cols), F32)
    else:
        kernel, out_specs = held_kernel, [fixed(2, part, cols // 2)] * 4
        out_shape = [jax.ShapeDtypeStruct((2, part, cols // 2), F32)] * 4
        inputs, in_specs = [*inputs, arrived], [*in_specs, block]
    return pl.pallas_call(
        kernel,
        grid_spec=pltpu.PrefetchScalarGridSpec(
            num_scalar_prefetch=1, grid=(blocks,), in_specs=in_specs, out_specs=out_specs
        ),
        out_shape=out_shape,
        compiler_params=pltpu.CompilerParams(
            dimension_semantics=("arbitrary",), vmem_limit_bytes=VMEM_LIMIT
        ),
        cost_estimate=LIGHT,
        name="token_products",
    )(at, *inputs)


def turn_kernel(at_ref, x_keep_ref, x_got_ref, y_keep_ref, y_got_ref, x_own_ref, x_send_ref, y_own_ref, y_send_ref):
    for mine, keep_ref, got_ref, own_ref, send_ref in (
        (at_ref[2], x_keep_ref, x_got_ref, x_own_ref, x_send_ref),
        (at_ref[1], y_keep_ref, y_got_ref, y_own_ref, y_send_ref),
    ):
        own_ref[...] = keep_ref[mine] + got_ref[mine]
        send_ref[...] = keep_ref[1 - mine] + got_ref[1 - mine]


def turned_blocks(at, x_keep, x_got, y_keep, y_got):
    _, part, cols = x_keep.shape
    rows = part // 4
    spec = pl.BlockSpec((2, rows, cols), lambda i, at: (0, i, 0))
    out = pl.BlockSpec((rows, cols), lambda i, at: (i, 0))
    return pl.pallas_call(
        turn_kernel,
        grid_spec=pltpu.PrefetchScalarGridSpec(
            num_scalar_prefetch=1, grid=(4,), in_specs=[spec] * 4, out_specs=[out] * 4
        ),
        out_shape=[jax.ShapeDtypeStruct((part, cols), F32)] * 4,
        compiler_params=pltpu.CompilerParams(
            dimension_semantics=("arbitrary",), vmem_limit_bytes=32 * 1024 * 1024
        ),
        cost_estimate=LIGHT,
        name="turned_blocks",
    )(at, x_keep, x_got, y_keep, y_got)


def weights_kernel(at_ref, mix_grad_ref, weighted_ref, tok_ref, cot_ref, one_mine_ref, one_peer_ref, two_mine_ref,
                   two_peer_ref):
    part = one_mine_ref.shape[-1]
    core = at_ref[0]
    one = nn(mix_grad_ref[0], tok_ref[...])
    two = nn(weighted_ref[0], cot_ref[...])
    for value, mine_ref, peer_ref in ((one, one_mine_ref, one_peer_ref), (two, two_mine_ref, two_peer_ref)):
        low, high = value[:, :part], value[:, part:]
        mine_ref[...] = jnp.where(core == 0, low, high).reshape(mine_ref.shape)
        peer_ref[...] = jnp.where(core == 0, high, low).reshape(peer_ref.shape)


def weight_grads(at, mix_grads, weighted, tokens, cotangent):
    tiles, units, total = weighted.shape
    part = tokens.shape[1] // 2
    one = jax.ShapeDtypeStruct((tiles, 2, units, part), F32)
    two = jax.ShapeDtypeStruct((tiles, units, part), F32)
    one_spec = pl.BlockSpec((1, 2, units, part), lambda i, at: (i, 0, 0, 0))
    two_spec = pl.BlockSpec((1, units, part), lambda i, at: (i, 0, 0))
    return pl.pallas_call(
        weights_kernel,
        grid_spec=pltpu.PrefetchScalarGridSpec(
            num_scalar_prefetch=1,
            grid=(tiles,),
            in_specs=[
                pl.BlockSpec((1, 2 * units, total), lambda i, at: (i, 0, 0)),
                pl.BlockSpec((1, units, total), lambda i, at: (i, 0, 0)),
                pl.BlockSpec((total, 2 * part), lambda i, at: (0, 0)),
                pl.BlockSpec((total, 2 * part), lambda i, at: (0, at[1])),
            ],
            out_specs=[one_spec, one_spec, two_spec, two_spec],
        ),
        out_shape=[one, one, two, two],
        compiler_params=pltpu.CompilerParams(
            dimension_semantics=("arbitrary",), vmem_limit_bytes=VMEM_LIMIT
        ),
        cost_estimate=LIGHT,
        name="weight_grads",
    )(at, mix_grads, weighted, tokens, cotangent)


def split_kernel(in_ref, out_ref, route_ref):
    count = out_ref.shape[0]
    out_ref[...] = in_ref[0, :count].astype(BF16)
    route_ref[...] = in_ref[0, count:, :count][None]


def split_rounded(gathered, count):
    blocks, rows, width = gathered.shape
    extra = rows - count
    return pl.pallas_call(
        split_kernel,
        grid=(blocks,),
        in_specs=[pl.BlockSpec((1, rows, width), lambda i: (i, 0, 0))],
        out_specs=[
            pl.BlockSpec((count, width), lambda i: (i, 0)),
            pl.BlockSpec((1, extra, count), lambda i: (i, 0, 0)),
        ],
        out_shape=[
            jax.ShapeDtypeStruct((blocks * count, width), BF16),
            jax.ShapeDtypeStruct((blocks, extra, count), F32),
        ],
        compiler_params=pltpu.CompilerParams(
            dimension_semantics=("arbitrary",), vmem_limit_bytes=32 * 1024 * 1024
        ),
        name="split_rounded",
    )(gathered)


def flip(value, bit):
    return lax.ppermute(value, "dp", [(i, i ^ bit) for i in range(8)])


def take(value, number, axis):
    return lax.dynamic_index_in_dim(value, number, axis, keepdims=False)


def shards(
    n_dp,
    n_tensor,
    layer_input,
    doc_ids,
    expert_ids,
    route_weights,
    attn_gain,
    qkv_weight,
    qkv_bias,
    out_weight,
    mlp_gain,
    expert_gate_up,
    expert_down,
    shared_gate_up,
    shared_down,
    shared_gate,
    cotangent,
):
    count, width = layer_input.shape
    heads_here = qkv_bias.shape[0]
    head_dim = qkv_bias.shape[1] // 3
    experts, units = expert_down.shape[:2]
    shared = shared_down.shape[0] // units
    part = width // n_dp
    me = lax.axis_index("dp")
    core, chip = me % 2, me // 2
    tied = lax.optimization_barrier

    choose = expert_ids[:, :, None] == jnp.arange(experts, dtype=jnp.int32)[None, None, :]
    route = jnp.sum(route_weights[:, :, None] * choose.astype(F32), axis=1).T
    cot_all = lax.all_gather(
        jnp.concatenate([cotangent.astype(F32), jnp.pad(route, ((0, 0), (0, width - count)))], axis=0), "dp"
    )
    gate_rows = jnp.broadcast_to(shared_gate[None, :], (16, width))
    index = jnp.arange(count, dtype=jnp.int32)
    place = (me * count + index - doc_ids).astype(F32)
    freq = ROPE_BASE ** (-(jnp.arange(head_dim // 2, dtype=F32) * 2.0 / head_dim))
    angle = place[:, None] * freq[None, :]
    cosine = jnp.concatenate([jnp.cos(angle), jnp.cos(angle)], axis=-1)
    sine = jnp.concatenate([-jnp.sin(angle), jnp.sin(angle)], axis=-1)
    row, col = doc_ids[None, :], doc_ids[:, None]
    gain_one = attn_gain.astype(F32)[None, :]
    gain_two = mlp_gain.astype(F32)[None, :]
    attn_part, normed_one, qkv, attended = attention(
        layer_input, gain_one, qkv_weight, qkv_bias.astype(F32)[:, None, :], cosine, sine, row, col, out_weight
    )

    attn_part, shared_gate_up = tied((attn_part, shared_gate_up))
    attn_sum = lax.psum(attn_part, "tensor")
    w1 = jnp.concatenate(
        [
            jnp.transpose(expert_gate_up, (0, 2, 3, 1)),
            jnp.transpose(shared_gate_up.reshape(width, 2, shared, units), (2, 1, 3, 0)),
        ]
    )
    w2 = jnp.concatenate([expert_down, shared_down.reshape(shared, units, width)])
    cot_low, route_all = split_rounded(cot_all, count)
    attn_sum, w1, w2, cot_low, route_all = tied((attn_sum, w1, w2, cot_low, route_all))

    residual, tokens, tokens_wide = second_norm(layer_input, attn_sum, gain_two)
    swap = lambda v: lax.ppermute(v, "dp", [(i, i ^ 1) for i in range(n_dp)])
    beside = swap(tokens_wide)
    tok_all = lax.all_gather(tokens_wide, "dp")
    mlp_top, mlp_low, grad_top, grad_low, logit_grad = own_mlp(tokens, cotangent, route, gate_rows, w1, w2)
    line = n_tensor == 4 and n_dp == 8
    spot = lax.axis_index("tensor")
    hide = lambda other, starts, tokens, kept: chip_hidden(
        jnp.stack([core, chip, other, *starts]), tokens, cot_low, route_all, gate_rows, w1, w2, kept, part
    )
    in_order = (jnp.int32(0), jnp.int32(count))
    beside_starts = (core * count, (1 - core) * count)
    shared_gate_part = jnp.sum(logit_grad[0][:, None] * tokens.astype(F32), axis=0, keepdims=True)
    if line:
        is_inner = (spot == 1) | (spot == 2)
        inwards = lambda v: lax.ppermute(v, "tensor", [(0, 1), (3, 2)])
        across = lambda v: lax.ppermute(v, "tensor", [(1, 2), (2, 1)])
        outwards = lambda v: lax.ppermute(v, "tensor", [(1, 0), (2, 3)])
        ready = jnp.isnan(logit_grad[0, 0]).astype(jnp.int32)
        got = inwards(grad_top)
        kept = hide(chip + ready, beside_starts, [tokens_wide, beside], [])
        got, grad_low, kept = tied((got, grad_low, kept))
        grad_top = grad_top + got
        got, got_low = across(grad_top), inwards(grad_low)
        got, got_low, mlp_top, tok_all, shared_gate_part, kept = tied(
            (got, got_low, mlp_top, tok_all, shared_gate_part, kept)
        )
        grad_top, grad_low = grad_top + got, grad_low + got_low
        end_top, got_low, got = outwards(grad_top), across(grad_low), inwards(mlp_top)
        kept = hide(chip ^ 1, in_order, [tok_all], kept)
        end_top, got_low, got, mlp_low, kept = tied((end_top, got_low, got, mlp_low, kept))
        grad_low, mlp_top = grad_low + got_low, mlp_top + got
        end_low, got, got_low = outwards(grad_low), across(mlp_top), inwards(mlp_low)
        kept = hide(chip ^ 2, in_order, [tok_all], kept)
        end_low, got, got_low, kept = tied((end_low, got, got_low, kept))
        totals = [grad_top, end_top, grad_low, end_low]
    else:
        is_inner = spot >= 0
        kept = []
        for k in range(n_dp // 2):
            kept = hide(jnp.int32(k), in_order, [tok_all], kept)
        totals = [lax.psum(v, "tensor") for v in (grad_top, grad_low)]
        totals = [totals[0], totals[0], totals[1], totals[1]]

    normed_one_part, residual_grad, branch_grad, projected_grad, bias_part, mlp_gain_part = attention_back(
        is_inner.astype(jnp.int32)[None], totals, residual, cotangent, gain_two, out_weight, qkv, qkv_weight,
        cosine, sine, row, col, layer_input, shared_gate_part, n_tensor,
    )
    few = count // n_tensor
    summed = lax.psum_scatter(normed_one_part.reshape(-1, width), "tensor", scatter_dimension=0, tiled=True)
    own_rows = lambda v: lax.dynamic_slice_in_dim(v, spot * few, few, 0)

    def finish(summed):
        inputs = own_rows(layer_input).astype(F32)
        factor = lax.rsqrt(jnp.mean(inputs * inputs, axis=-1, keepdims=True) + EPS)
        bias_row = jnp.pad(bias_part, ((0, 0), (0, width - bias_part.shape[1])))
        small = jnp.concatenate([summed[few : few + 2], mlp_gain_part, bias_row])
        return norm_back(inputs, factor, gain_one, summed[:few]), jnp.pad(small, ((0, 4), (0, 0)))

    if line:
        got, got_low, mlp_top, mlp_low, projected_grad = tied((got, got_low, mlp_top, mlp_low, projected_grad))
        mlp_top, mlp_low = mlp_top + got, mlp_low + got_low
        end_top, got_low = outwards(mlp_top), across(mlp_low)
        mlp_low, projected_grad = tied((mlp_low, projected_grad))
        at = jnp.stack([core, chip % 2, chip // 2])
        other_at = jnp.stack([1 - core, chip % 2, chip // 2])
        arrived = swap(token_products(other_at, normed_one, projected_grad, branch_grad, attended, None))
        x_keep, x_send, y_keep, y_send = token_products(
            at, normed_one, projected_grad, branch_grad, attended, arrived
        )
        x_send, y_send, kept, got_low = tied((x_send, y_send, kept, got_low))
        mlp_low = mlp_low + got_low
        end_low = outwards(mlp_low)
        x_got, y_got = flip(x_send, 2), flip(y_send, 4)
        kept = hide(chip ^ 3, in_order, [tok_all], kept)
        one_mine, one_peer, two_mine, two_peer = weight_grads(jnp.stack([core, chip]), *kept, cot_low)
        one_mine, one_peer, summed = tied((one_mine, one_peer, summed))
        one_peer, two_peer = swap(one_peer), swap(two_peer)
        input_grad, small = finish(summed)
        input_grad, x_got, y_got, end_top, end_low = tied((input_grad, x_got, y_got, end_top, end_low))
        input_grad = lax.all_gather(input_grad, "tensor", axis=0, tiled=True)
        x_own, x_send, y_own, y_send = turned_blocks(at, x_keep, x_got, y_keep, y_got)
        x_got, y_got = flip(x_send, 4), flip(y_send, 2)
        small, x_own = tied((small, x_own))
        for bit in (1, 2, 4):
            small = small + flip(small, bit)
        both = jnp.concatenate([x_own + x_got, y_own + y_got], axis=1)
        cut = projected_grad.shape[1]
        qkv_weight_grad, out_weight_grad = both[:, :cut], both[:, cut:].T
        mlp_sum = jnp.where(
            is_inner, jnp.concatenate([mlp_top, mlp_low]), jnp.concatenate([end_top, end_low])
        )
    else:
        one_mine, one_peer, two_mine, two_peer = weight_grads(jnp.stack([core, chip]), *kept, cot_low)
        one_peer, two_peer = swap(one_peer), swap(two_peer)
        input_grad, small = finish(summed)
        input_grad = lax.all_gather(input_grad, "tensor", axis=0, tiled=True)
        small = lax.psum(small, "dp")
        joint = lambda v: v.reshape(2, count, BLOCKS // 2, -1).transpose(1, 2, 0, 3).reshape(count, width)
        out_weight_grad = lax.psum_scatter(tn(attended, joint(branch_grad)), "dp", scatter_dimension=1, tiled=True)
        qkv_weight_grad = lax.psum_scatter(
            tn(joint(normed_one), projected_grad), "dp", scatter_dimension=0, tiled=True
        )
        mlp_sum = lax.psum(jnp.concatenate([mlp_top, mlp_low]), "tensor")

    attn_gain_grad, shared_gate_grad, mlp_gain_grad = lax.dynamic_slice(small, (0, me * part), (3, part))
    bias_cols = 3 * head_dim // n_dp
    bias = small[3, : heads_here * 3 * head_dim].reshape(heads_here, 3 * head_dim)
    qkv_bias_grad = lax.dynamic_slice(bias, (0, me * bias_cols), (heads_here, bias_cols))
    input_grad = (residual_grad + input_grad).astype(BF16)
    layer_output = (residual + mlp_sum).astype(BF16)

    def joined(mine, peer):
        return jnp.where(core == 0, jnp.concatenate([mine, peer]), jnp.concatenate([peer, mine]))

    half = experts // 2
    expert_gate_up_grad = jnp.transpose(joined(one_mine[:half], one_peer[:half]), (0, 3, 1, 2))
    expert_down_grad = joined(two_mine[:half], two_peer[:half])
    shared_gate_up_grad = jnp.transpose(joined(one_mine[half:], one_peer[half:]), (3, 1, 0, 2)).reshape(
        part, 2, shared * units
    )
    shared_down_grad = joined(two_mine[half:], two_peer[half:]).reshape(shared * units, part)
    return (
        layer_output,
        input_grad,
        attn_gain_grad,
        qkv_weight_grad,
        qkv_bias_grad,
        out_weight_grad,
        mlp_gain_grad,
        expert_gate_up_grad,
        expert_down_grad,
        shared_gate_up_grad,
        shared_down_grad,
        shared_gate_grad,
    )


def solution(mesh):
    placed = (
        P("dp", None),
        P("dp"),
        P("dp", None),
        P("dp", None),
        P(),
        P(None, "tensor"),
        P("tensor", None),
        P("tensor", None),
        P(),
        P(None, None, None, "tensor"),
        P(None, "tensor", None),
        P(None, None, "tensor"),
        P("tensor", None),
        P(),
        P("dp", None),
    )
    return jax.shard_map(
        functools.partial(shards, mesh.shape["dp"], mesh.shape["tensor"]),
        mesh=mesh,
        in_specs=placed,
        out_specs=(
            P("dp", None),
            P("dp", None),
            P("dp"),
            P("dp", "tensor"),
            P("tensor", "dp"),
            P("tensor", "dp"),
            P("dp"),
            P(None, "dp", None, "tensor"),
            P(None, "tensor", "dp"),
            P("dp", None, "tensor"),
            P("tensor", "dp"),
            P("dp"),
        ),
        check_vma=False,
    )
```

```python
import functools

import jax
import jax.numpy as jnp
from jax import lax
from jax.experimental import pallas as pl
from jax.experimental.pallas import tpu as pltpu
from jax.sharding import PartitionSpec as P

EPS = 1e-06
ROPE_BASE = 1000000.0
NEG = -1e30
F32 = jnp.float32
BF16 = jnp.bfloat16
VMEM_LIMIT = 60 * 1024 * 1024
BLOCKS = 8
LIGHT = pl.CostEstimate(flops=1 << 20, bytes_accessed=1 << 16, transcendentals=0)


def nt(left, right):
    return lax.dot_general(left, right, (((1,), (1,)), ((), ())), preferred_element_type=F32)


def tn(left, right):
    return lax.dot_general(left, right, (((0,), (0,)), ((), ())), preferred_element_type=F32)


def nn(left, right):
    return jnp.dot(left, right, preferred_element_type=F32)


def norm_back(values_in, factor, gain_vec, upstream):
    scaled = gain_vec * upstream
    inner = jnp.mean(scaled * values_in, axis=-1, keepdims=True)
    return factor * scaled - values_in * factor**3 * inner


def turned(values, cosine, sine):
    return values * cosine + pltpu.roll(values, values.shape[1] // 2, 1) * sine


def turned_back(values, cosine, sine):
    return values * cosine - pltpu.roll(values, values.shape[1] // 2, 1) * sine


def head_probs(queries, keys, row_ref, col_ref):
    count = queries.shape[0]
    scores = nt(queries, keys) * queries.shape[1] ** (-0.5)
    rows = lax.broadcasted_iota(jnp.int32, (count, count), 0)
    cols = lax.broadcasted_iota(jnp.int32, (count, count), 1)
    scores = jnp.where((col_ref[...] == row_ref[...]) & (cols <= rows), scores, NEG)
    exponent = jnp.exp(scores - jnp.max(scores, axis=-1, keepdims=True))
    return exponent / jnp.sum(exponent, axis=-1, keepdims=True)


def split_columns(whole_ref, split_ref):
    part = whole_ref.shape[1] // BLOCKS
    for k in range(BLOCKS):
        split_ref[k % 2, :, k // 2 * part : (k // 2 + 1) * part] = whole_ref[:, k * part : (k + 1) * part]


def attn_kernel(x_ref, gain_ref, weight_ref, bias_ref, cos_ref, sin_ref, row_ref, col_ref, out_weight_ref,
                part_ref, split_ref, qkv_ref, attended_ref, normed_ref):
    head = pl.program_id(0)
    dim = cos_ref.shape[1]

    @pl.when(head == 0)
    def _():
        values = x_ref[...].astype(F32)
        factor = lax.rsqrt(jnp.mean(values * values, axis=-1, keepdims=True) + EPS)
        normed_ref[...] = (values * factor * gain_ref[...]).astype(BF16)
        split_columns(normed_ref, split_ref)

    projected = nn(normed_ref[...], weight_ref[...]) + bias_ref[0]
    queries = turned(projected[:, :dim], cos_ref[...], sin_ref[...]).astype(BF16)
    keys = turned(projected[:, dim : 2 * dim], cos_ref[...], sin_ref[...]).astype(BF16)
    values = projected[:, 2 * dim :].astype(BF16)
    qkv_ref[:, :dim] = queries
    qkv_ref[:, dim : 2 * dim] = keys
    qkv_ref[:, 2 * dim :] = values
    probs = head_probs(queries, keys, row_ref, col_ref)
    cols = pl.ds(pl.multiple_of(head * dim, dim), dim)
    attended_ref[:, cols] = nn(probs.astype(BF16), values).astype(BF16)

    @pl.when(head == pl.num_programs(0) - 1)
    def _():
        part_ref[...] = nn(attended_ref[...], out_weight_ref[...])


def whole(*shape):
    return pl.BlockSpec(shape, lambda *at: (0,) * len(shape))


def attention(x, gain, weight, bias, cosine, sine, row, col, out_weight):
    count, width = x.shape
    heads, _, cols = bias.shape
    return pl.pallas_call(
        attn_kernel,
        grid=(heads,),
        in_specs=[
            whole(count, width),
            whole(1, width),
            pl.BlockSpec((width, cols), lambda h: (0, h)),
            pl.BlockSpec((1, 1, cols), lambda h: (h, 0, 0)),
            whole(*cosine.shape),
            whole(*sine.shape),
            whole(1, count),
            whole(count, 1),
            whole(*out_weight.shape),
        ],
        out_specs=[
            whole(count, width),
            whole(2, count, width // 2),
            pl.BlockSpec((count, cols), lambda h: (0, h)),
            whole(count, out_weight.shape[0]),
        ],
        out_shape=[
            jax.ShapeDtypeStruct((count, width), F32),
            jax.ShapeDtypeStruct((2, count, width // 2), BF16),
            jax.ShapeDtypeStruct((count, heads * cols), BF16),
            jax.ShapeDtypeStruct((count, out_weight.shape[0]), BF16),
        ],
        scratch_shapes=[pltpu.VMEM((count, width), BF16)],
        compiler_params=pltpu.CompilerParams(
            dimension_semantics=("arbitrary",), vmem_limit_bytes=32 * 1024 * 1024
        ),
        cost_estimate=LIGHT,
        name="attention",
    )(x, gain, weight, bias, cosine, sine, row, col, out_weight)


def norm_kernel(x_ref, sum_ref, gain_ref, residual_ref, low_ref, wide_ref):
    residual = x_ref[...].astype(F32) + sum_ref[...]
    factor = lax.rsqrt(jnp.mean(residual * residual, axis=-1, keepdims=True) + EPS)
    low = (residual * factor * gain_ref[...]).astype(BF16)
    residual_ref[...] = residual
    low_ref[...] = low
    wide_ref[...] = low.astype(F32)


def second_norm(x, attn_sum, gain):
    count, width = x.shape
    rows = count // 4
    spec = pl.BlockSpec((rows, width), lambda i: (i, 0))
    return pl.pallas_call(
        norm_kernel,
        grid=(4,),
        in_specs=[spec, spec, whole(1, width)],
        out_specs=[spec, spec, spec],
        out_shape=[
            jax.ShapeDtypeStruct((count, width), F32),
            jax.ShapeDtypeStruct((count, width), BF16),
            jax.ShapeDtypeStruct((count, width), F32),
        ],
        compiler_params=pltpu.CompilerParams(
            dimension_semantics=("arbitrary",), vmem_limit_bytes=32 * 1024 * 1024
        ),
        name="second_norm",
    )(x, attn_sum, gain)


def back_kernel(inner_ref, held_top_ref, got_top_ref, held_low_ref, got_low_ref, residual_ref, cot_ref, gain_ref, out_weight_ref, qkv_ref, weight_ref, cos_ref, sin_ref,
                row_ref, col_ref, x_ref, extra_ref, normed_grad_ref, residual_grad_ref, split_ref, projected_grad_ref, bias_ref,
                mlp_gain_ref, branch_ref, attended_grad_ref):
    head = pl.program_id(0)
    dim = cos_ref.shape[1]

    @pl.when(head == 0)
    def _():
        total = jnp.where(
            inner_ref[0] == 1,
            jnp.concatenate([held_top_ref[...], held_low_ref[...]]),
            jnp.concatenate([got_top_ref[...], got_low_ref[...]]),
        )
        residual = residual_ref[...]
        factor = lax.rsqrt(jnp.mean(residual * residual, axis=-1, keepdims=True) + EPS)
        scaled = gain_ref[...] * total
        inner = jnp.mean(scaled * residual, axis=-1, keepdims=True)
        residual_grad = cot_ref[...].astype(F32) + (factor * scaled - residual * factor**3 * inner)
        residual_grad_ref[...] = residual_grad
        branch_ref[...] = residual_grad.astype(BF16)
        split_columns(branch_ref, split_ref)
        mlp_gain_ref[...] = jnp.sum(total * residual * factor, axis=0, keepdims=True)
        attended_grad = nt(branch_ref[...], out_weight_ref[...]).astype(BF16)
        for k in range(attended_grad_ref.shape[0]):
            attended_grad_ref[k] = attended_grad[:, k * dim : (k + 1) * dim]

    queries, keys, values = qkv_ref[:, :dim], qkv_ref[:, dim : 2 * dim], qkv_ref[:, 2 * dim :]
    attended_grad = attended_grad_ref[head]
    probs = head_probs(queries, keys, row_ref, col_ref)
    prob_grad = nt(attended_grad, values)
    inner = jnp.sum(probs * prob_grad, axis=-1, keepdims=True)
    score = (probs * (prob_grad - inner) * dim ** (-0.5)).astype(BF16)
    query_grad = nn(score, keys).astype(BF16).astype(F32)
    key_grad = tn(score, queries).astype(BF16).astype(F32)
    value_grad = tn(probs.astype(BF16), attended_grad)
    grad = jnp.concatenate(
        [
            turned_back(query_grad, cos_ref[...], sin_ref[...]).astype(BF16),
            turned_back(key_grad, cos_ref[...], sin_ref[...]).astype(BF16),
            value_grad.astype(BF16),
        ],
        axis=1,
    )
    projected_grad_ref[...] = grad
    bias_ref[...] = jnp.sum(grad.astype(F32), axis=0, keepdims=True)
    product = nt(grad, weight_ref[...])
    groups, few = normed_grad_ref.shape[0], normed_grad_ref.shape[1] - 8

    @pl.when(head == 0)
    def _():
        for k in range(groups):
            normed_grad_ref[k, :few] = product[k * few : (k + 1) * few]

    @pl.when(head > 0)
    def _():
        for k in range(groups):
            normed_grad_ref[k, :few] += product[k * few : (k + 1) * few]

    @pl.when(head == pl.num_programs(0) - 1)
    def _():
        total = jnp.zeros((1, x_ref.shape[1]), F32)
        for k in range(groups):
            x = x_ref[k * few : (k + 1) * few].astype(F32)
            factor = lax.rsqrt(jnp.mean(x * x, axis=-1, keepdims=True) + EPS)
            total += jnp.sum(normed_grad_ref[k, :few] * x * factor, axis=0, keepdims=True)
        rows = lax.broadcasted_iota(jnp.int32, (8, x_ref.shape[1]), 0)
        small = jnp.where(rows == 0, total, jnp.where(rows == 1, extra_ref[...], 0.0))
        for k in range(groups):
            normed_grad_ref[k, few:] = small


def attention_back(inner, totals, residual, cotangent, gain, out_weight, qkv, weight, cosine, sine, row, col, x, extra,
                   groups):
    count, width = residual.shape
    dim = cosine.shape[1]
    cols = 3 * dim
    heads = qkv.shape[1] // cols
    return pl.pallas_call(
        back_kernel,
        grid=(heads,),
        in_specs=[
            pl.BlockSpec(memory_space=pltpu.SMEM),
            *[whole(count // 2, width)] * 4,
            whole(count, width),
            whole(count, width),
            whole(1, width),
            whole(*out_weight.shape),
            pl.BlockSpec((count, cols), lambda h: (0, h)),
            pl.BlockSpec((width, cols), lambda h: (0, h)),
            whole(*cosine.shape),
            whole(*sine.shape),
            whole(1, count),
            whole(count, 1),
            whole(count, width),
            whole(1, width),
        ],
        out_specs=[
            whole(groups, count // groups + 8, width),
            whole(count, width),
            whole(2, count, width // 2),
            pl.BlockSpec((count, cols), lambda h: (0, h)),
            pl.BlockSpec((1, cols), lambda h: (0, h)),
            whole(1, width),
        ],
        out_shape=[
            jax.ShapeDtypeStruct((groups, count // groups + 8, width), F32),
            jax.ShapeDtypeStruct((count, width), F32),
            jax.ShapeDtypeStruct((2, count, width // 2), BF16),
            jax.ShapeDtypeStruct((count, heads * cols), BF16),
            jax.ShapeDtypeStruct((1, heads * cols), F32),
            jax.ShapeDtypeStruct((1, width), F32),
        ],
        scratch_shapes=[pltpu.VMEM((count, width), BF16), pltpu.VMEM((heads, count, dim), BF16)],
        compiler_params=pltpu.CompilerParams(
            dimension_semantics=("arbitrary",), vmem_limit_bytes=48 * 1024 * 1024
        ),
        cost_estimate=LIGHT,
        name="attention_back",
    )(inner, *totals, residual, cotangent, gain, out_weight, qkv, weight, cosine, sine, row, col, x, extra)


def hidden(w_one, w_two, tokens, branch, route_row):
    units = w_two.shape[0]
    mix = nt(w_one, tokens)
    gate, up = mix[:units], mix[units:]
    back = nt(w_two, branch)
    sigma = lax.logistic(gate)
    silu = gate * sigma
    act = silu * up
    scaled = back * route_row
    gate_grad = scaled * up * (sigma + silu * (1.0 - sigma))
    mix_grad = jnp.concatenate([gate_grad.astype(BF16), (scaled * silu).astype(BF16)], axis=0)
    return act, back, (act * route_row).astype(BF16), mix_grad


def open_row(gate_rows, tokens):
    return lax.logistic(nt(gate_rows, tokens)[:1])


def own_kernel(experts, tok_ref, cot_ref, route_ref, gate_ref, w1_ref, w2_ref, out_ref, dx_top_ref, dx_low_ref,
               logit_ref, open_ref):
    step = pl.program_id(0)
    group, units, width = w2_ref.shape
    shared = step * group >= experts

    @pl.when(step == 0)
    def _():
        for ref in (out_ref, dx_top_ref, dx_low_ref):
            ref[...] = jnp.zeros_like(ref)
        logit_ref[...] = jnp.zeros_like(logit_ref)
        open_ref[...] = open_row(gate_ref[...], tok_ref[...])

    weighted, mix_grads = [], []
    for k in range(group):
        act, back, scaled, mix_grad = hidden(
            w1_ref[k].reshape(2 * units, width),
            w2_ref[k],
            tok_ref[...],
            cot_ref[...],
            jnp.where(shared, open_ref[...], route_ref[k]),
        )
        weighted.append(scaled)
        mix_grads.append(mix_grad)
        logit_ref[...] += jnp.where(shared, jnp.sum(act * back, axis=0, keepdims=True), 0.0)
    rows = dx_top_ref.shape[0]
    out_ref[...] += tn(jnp.concatenate(weighted), w2_ref[...].reshape(group * units, width))
    dx = tn(jnp.concatenate(mix_grads), w1_ref[...].reshape(group * 2 * units, width))
    dx_top_ref[...] += dx[:rows]
    dx_low_ref[...] += dx[rows:]

    @pl.when(step == pl.num_programs(0) - 1)
    def _():
        opened = open_ref[...]
        logit = opened * (1.0 - opened) * logit_ref[...]
        logit_ref[...] = logit
        column = jnp.broadcast_to(logit, (8, logit.shape[1])).T[:, :1]
        dx_top_ref[...] += column[:rows] * gate_ref[:1].astype(F32)
        dx_low_ref[...] += column[rows:] * gate_ref[:1].astype(F32)


def own_mlp(tokens, cotangent, route, gate_rows, w1, w2):
    count, width = tokens.shape
    tiles, units = w2.shape[:2]
    experts = route.shape[0]
    group = 2
    return pl.pallas_call(
        functools.partial(own_kernel, experts),
        grid=(tiles // group,),
        in_specs=[
            whole(count, width),
            whole(count, width),
            pl.BlockSpec((group, 1, count), lambda i: (jnp.minimum(i, experts // group - 1), 0, 0)),
            whole(*gate_rows.shape),
            pl.BlockSpec((group, 2, units, width), lambda i: (i, 0, 0, 0)),
            pl.BlockSpec((group, units, width), lambda i: (i, 0, 0)),
        ],
        out_specs=[whole(count, width), *[whole(count // 2, width)] * 2, whole(1, count)],
        out_shape=[
            jax.ShapeDtypeStruct((count, width), F32),
            *[jax.ShapeDtypeStruct((count // 2, width), F32)] * 2,
            jax.ShapeDtypeStruct((1, count), F32),
        ],
        scratch_shapes=[pltpu.VMEM((1, count), F32)],
        compiler_params=pltpu.CompilerParams(
            dimension_semantics=("arbitrary",), vmem_limit_bytes=VMEM_LIMIT
        ),
        cost_estimate=LIGHT,
        name="own_mlp",
    )(tokens, cotangent, route[:, None, :], gate_rows, w1, w2)


def chip_kernel(here, at_ref, even_ref, odd_ref, cot_ref, route_ref, gate_ref, w1_ref, w2_ref, *refs):
    mix_grad_ref, weighted_ref, part_ref, tok_ref, open_ref = refs[-5:]
    step = pl.program_id(0)
    units, width = w2_ref.shape[-2:]
    cores, experts, count = route_ref.shape
    core = at_ref[0]

    @pl.when(step == 0)
    def _():
        for start, ref in ((at_ref[3], even_ref), (at_ref[4], odd_ref)):
            tok_ref[pl.ds(pl.multiple_of(start, count), count), :] = ref[...].reshape(count, width).astype(BF16)
        part = part_ref.shape[1]
        part_ref[...] = tok_ref[:, pl.ds(pl.multiple_of(at_ref[1] * part, part), part)]
        open_ref[...] = open_row(gate_ref[...], tok_ref[...])

    expert = jnp.minimum(core * here + step, experts - 1)
    route_row = jnp.concatenate([route_ref[k, pl.ds(expert, 1), :] for k in range(cores)], axis=1)
    _, _, weighted, mix_grad = hidden(
        w1_ref[...].reshape(2 * units, width),
        w2_ref[0],
        tok_ref[...],
        cot_ref[...],
        jnp.where(step >= here, open_ref[...], route_row),
    )
    mix_grad_ref[0] = mix_grad
    weighted_ref[0] = weighted


def chip_hidden(at, tokens, cotangent, route, gate_rows, w1, w2, kept, part):
    total, width = cotangent.shape
    tiles, units = w2.shape[:2]
    experts, count = route.shape[1:]
    here, shared = experts // 2, (tiles - experts) // 2
    rows = 2 * count
    own = lambda i, at: jnp.where(i < here, at[0] * here + i, experts + at[0] * shared + i - here)
    fixed = lambda *shape: pl.BlockSpec(shape, lambda i, at: (0,) * len(shape))
    if len(tokens) == 2:
        sources = [fixed(count, width), fixed(count, width)]
    else:
        tokens = [tokens[0], tokens[0]]
        sources = [
            pl.BlockSpec((1, count, width), lambda i, at: (2 * at[2], 0, 0)),
            pl.BlockSpec((1, count, width), lambda i, at: (2 * at[2] + 1, 0, 0)),
        ]
    shapes = [
        jax.ShapeDtypeStruct((here + shared, 2 * units, total), BF16),
        jax.ShapeDtypeStruct((here + shared, units, total), BF16),
        jax.ShapeDtypeStruct((total, 2 * part), BF16),
    ]
    inputs = [*tokens, cotangent, route, gate_rows, w1, w2]
    return pl.pallas_call(
        functools.partial(chip_kernel, here),
        grid_spec=pltpu.PrefetchScalarGridSpec(
            num_scalar_prefetch=1,
            grid=(here + shared,),
            in_specs=[
                *sources,
                pl.BlockSpec((rows, width), lambda i, at: (at[2], 0)),
                pl.BlockSpec((2, experts, count), lambda i, at: (at[2], 0, 0)),
                fixed(*gate_rows.shape),
                pl.BlockSpec((1, 2, units, width), lambda i, at: (own(i, at), 0, 0, 0)),
                pl.BlockSpec((1, units, width), lambda i, at: (own(i, at), 0, 0)),
                *[pl.BlockSpec(memory_space=pl.ANY) for _ in kept],
            ],
            out_specs=[
                pl.BlockSpec((1, 2 * units, rows), lambda i, at: (i, 0, at[2])),
                pl.BlockSpec((1, units, rows), lambda i, at: (i, 0, at[2])),
                pl.BlockSpec((rows, 2 * part), lambda i, at: (at[2], 0)),
            ],
            scratch_shapes=[pltpu.VMEM((rows, width), BF16), pltpu.VMEM((1, rows), F32)],
        ),
        out_shape=shapes,
        input_output_aliases={1 + len(inputs) + k: k for k in range(len(kept))},
        compiler_params=pltpu.CompilerParams(
            dimension_semantics=("arbitrary",), vmem_limit_bytes=VMEM_LIMIT
        ),
        cost_estimate=LIGHT,
        name="chip_hidden",
    )(at, *inputs, *kept)


def both_products(normed_ref, projected_ref, branch_ref, attended_ref):
    return jnp.concatenate(
        [tn(normed_ref[0], projected_ref[...]), tn(branch_ref[0], attended_ref[...])], axis=1
    )


def sent_kernel(at_ref, normed_ref, projected_ref, branch_ref, attended_ref, out_ref):
    out_ref[0] = both_products(normed_ref, projected_ref, branch_ref, attended_ref)


def held_kernel(at_ref, normed_ref, projected_ref, branch_ref, attended_ref, arrived_ref, *out_refs):
    block = pl.program_id(0)
    along_y, along_x = block // 2, lax.rem(block, 2)
    value = both_products(normed_ref, projected_ref, branch_ref, attended_ref) + arrived_ref[0]
    half = value.shape[1] // 2
    x_keep_ref, x_send_ref, y_keep_ref, y_send_ref = out_refs
    for same, index, columns, keep_ref, send_ref in (
        (along_x == at_ref[1], along_y, value[:, :half], x_keep_ref, x_send_ref),
        (along_y == at_ref[2], along_x, value[:, half:], y_keep_ref, y_send_ref),
    ):
        @pl.when(same)
        def _():
            keep_ref[index] = columns

        @pl.when(jnp.logical_not(same))
        def _():
            send_ref[index] = columns


def token_products(at, normed, projected, branch, attended, arrived):
    _, count, half = normed.shape
    blocks = BLOCKS // 2
    part = half // blocks
    cols = projected.shape[1] + attended.shape[1]
    side = pl.BlockSpec((1, count, part), lambda i, at: (at[0], 0, i))
    fixed = lambda *shape: pl.BlockSpec(shape, lambda i, at: (0,) * len(shape))
    block = pl.BlockSpec((1, part, cols), lambda i, at: (i, 0, 0))
    inputs = [normed, projected, branch, attended]
    in_specs = [side, fixed(*projected.shape), side, fixed(*attended.shape)]
    if arrived is None:
        kernel, out_specs = sent_kernel, block
        out_shape = jax.ShapeDtypeStruct((blocks, part, cols), F32)
    else:
        kernel, out_specs = held_kernel, [fixed(2, part, cols // 2)] * 4
        out_shape = [jax.ShapeDtypeStruct((2, part, cols // 2), F32)] * 4
        inputs, in_specs = [*inputs, arrived], [*in_specs, block]
    return pl.pallas_call(
        kernel,
        grid_spec=pltpu.PrefetchScalarGridSpec(
            num_scalar_prefetch=1, grid=(blocks,), in_specs=in_specs, out_specs=out_specs
        ),
        out_shape=out_shape,
        compiler_params=pltpu.CompilerParams(
            dimension_semantics=("arbitrary",), vmem_limit_bytes=VMEM_LIMIT
        ),
        cost_estimate=LIGHT,
        name="token_products",
    )(at, *inputs)


def turn_kernel(at_ref, x_keep_ref, x_got_ref, y_keep_ref, y_got_ref, x_own_ref, x_send_ref, y_own_ref, y_send_ref):
    for mine, keep_ref, got_ref, own_ref, send_ref in (
        (at_ref[2], x_keep_ref, x_got_ref, x_own_ref, x_send_ref),
        (at_ref[1], y_keep_ref, y_got_ref, y_own_ref, y_send_ref),
    ):
        own_ref[...] = keep_ref[mine] + got_ref[mine]
        send_ref[...] = keep_ref[1 - mine] + got_ref[1 - mine]


def turned_blocks(at, x_keep, x_got, y_keep, y_got):
    _, part, cols = x_keep.shape
    rows = part // 4
    spec = pl.BlockSpec((2, rows, cols), lambda i, at: (0, i, 0))
    out = pl.BlockSpec((rows, cols), lambda i, at: (i, 0))
    return pl.pallas_call(
        turn_kernel,
        grid_spec=pltpu.PrefetchScalarGridSpec(
            num_scalar_prefetch=1, grid=(4,), in_specs=[spec] * 4, out_specs=[out] * 4
        ),
        out_shape=[jax.ShapeDtypeStruct((part, cols), F32)] * 4,
        compiler_params=pltpu.CompilerParams(
            dimension_semantics=("arbitrary",), vmem_limit_bytes=32 * 1024 * 1024
        ),
        cost_estimate=LIGHT,
        name="turned_blocks",
    )(at, x_keep, x_got, y_keep, y_got)


def weights_kernel(here, at_ref, mix_grad_ref, weighted_ref, tok_ref, cot_ref, *refs):
    part = refs[0].shape[-1]
    expert_refs, shared_refs, peer_refs = refs[:2], refs[2:4], refs[4:]
    core, step = at_ref[0], pl.program_id(0)
    products = nn(mix_grad_ref[0], tok_ref[...]), nn(weighted_ref[0], cot_ref[...])
    for value, expert_ref, shared_ref, peer_ref in zip(products, expert_refs, shared_refs, peer_refs, strict=True):
        low, high = value[:, :part], value[:, part:]
        mine = jnp.where(core == 0, low, high)
        peer_ref[...] = jnp.where(core == 0, high, low).reshape(peer_ref.shape)

        @pl.when(step < here)
        def _():
            expert_ref[...] = mine.reshape(expert_ref.shape)

        @pl.when(step >= here)
        def _():
            shared_ref[...] = mine.reshape(shared_ref.shape)


def tile_specs(core_of, here, shared, units, part):
    expert = lambda i, at: core_of(at) * here + jnp.minimum(i, here - 1)
    common = lambda i, at: core_of(at) * shared + jnp.maximum(i - here, 0)
    return [
        pl.BlockSpec((1, 2, units, part), lambda i, at: (expert(i, at), 0, 0, 0)),
        pl.BlockSpec((1, units, part), lambda i, at: (expert(i, at), 0, 0)),
        pl.BlockSpec((1, 2, units, part), lambda i, at: (common(i, at), 0, 0, 0)),
        pl.BlockSpec((1, units, part), lambda i, at: (common(i, at), 0, 0)),
    ]


def weight_grads(at, mix_grads, weighted, tokens, cotangent, here):
    tiles, units, total = weighted.shape
    part = tokens.shape[1] // 2
    shared = tiles - here
    one = lambda count: jax.ShapeDtypeStruct((count, 2, units, part), F32)
    two = lambda count: jax.ShapeDtypeStruct((count, units, part), F32)
    return pl.pallas_call(
        functools.partial(weights_kernel, here),
        grid_spec=pltpu.PrefetchScalarGridSpec(
            num_scalar_prefetch=1,
            grid=(tiles,),
            in_specs=[
                pl.BlockSpec((1, 2 * units, total), lambda i, at: (i, 0, 0)),
                pl.BlockSpec((1, units, total), lambda i, at: (i, 0, 0)),
                pl.BlockSpec((total, 2 * part), lambda i, at: (0, 0)),
                pl.BlockSpec((total, 2 * part), lambda i, at: (0, at[3])),
            ],
            out_specs=[
                *tile_specs(lambda at: at[0], here, shared, units, part),
                pl.BlockSpec((1, 2, units, part), lambda i, at: (i, 0, 0, 0)),
                pl.BlockSpec((1, units, part), lambda i, at: (i, 0, 0)),
            ],
        ),
        out_shape=[one(2 * here), two(2 * here), one(2 * shared), two(2 * shared), one(tiles), two(tiles)],
        compiler_params=pltpu.CompilerParams(
            dimension_semantics=("arbitrary",), vmem_limit_bytes=VMEM_LIMIT
        ),
        cost_estimate=LIGHT,
        name="weight_grads",
    )(at, mix_grads, weighted, tokens, cotangent)


def place_kernel(here, at_ref, one_ref, two_ref, *refs):
    step = pl.program_id(0)
    expert_one_ref, expert_two_ref, shared_one_ref, shared_two_ref = refs[-4:]

    @pl.when(step < here)
    def _():
        expert_one_ref[...] = one_ref[...]
        expert_two_ref[...] = two_ref[...]

    @pl.when(step >= here)
    def _():
        shared_one_ref[...] = one_ref[...]
        shared_two_ref[...] = two_ref[...]


def place_peer(at, one, two, grads, here):
    tiles, units, part = two.shape
    return pl.pallas_call(
        functools.partial(place_kernel, here),
        grid_spec=pltpu.PrefetchScalarGridSpec(
            num_scalar_prefetch=1,
            grid=(tiles,),
            in_specs=[
                pl.BlockSpec((1, 2, units, part), lambda i, at: (i, 0, 0, 0)),
                pl.BlockSpec((1, units, part), lambda i, at: (i, 0, 0)),
                *[pl.BlockSpec(memory_space=pl.ANY)] * 4,
            ],
            out_specs=tile_specs(lambda at: 1 - at[0], here, tiles - here, units, part),
        ),
        out_shape=[jax.ShapeDtypeStruct(g.shape, g.dtype) for g in grads],
        input_output_aliases={3 + k: k for k in range(4)},
        compiler_params=pltpu.CompilerParams(
            dimension_semantics=("arbitrary",), vmem_limit_bytes=32 * 1024 * 1024
        ),
        cost_estimate=LIGHT,
        name="place_peer",
    )(at, one, two, *grads)


def split_kernel(in_ref, out_ref, route_ref):
    count = out_ref.shape[0]
    out_ref[...] = in_ref[0, :count].astype(BF16)
    route_ref[...] = in_ref[0, count:, :count][None]


def split_rounded(gathered, count):
    blocks, rows, width = gathered.shape
    extra = rows - count
    return pl.pallas_call(
        split_kernel,
        grid=(blocks,),
        in_specs=[pl.BlockSpec((1, rows, width), lambda i: (i, 0, 0))],
        out_specs=[
            pl.BlockSpec((count, width), lambda i: (i, 0)),
            pl.BlockSpec((1, extra, count), lambda i: (i, 0, 0)),
        ],
        out_shape=[
            jax.ShapeDtypeStruct((blocks * count, width), BF16),
            jax.ShapeDtypeStruct((blocks, extra, count), F32),
        ],
        compiler_params=pltpu.CompilerParams(
            dimension_semantics=("arbitrary",), vmem_limit_bytes=32 * 1024 * 1024
        ),
        name="split_rounded",
    )(gathered)


def flip(value, bit):
    return lax.ppermute(value, "dp", [(i, i ^ bit) for i in range(8)])


def take(value, number, axis):
    return lax.dynamic_index_in_dim(value, number, axis, keepdims=False)


def shards(
    n_dp,
    n_tensor,
    layer_input,
    doc_ids,
    expert_ids,
    route_weights,
    attn_gain,
    qkv_weight,
    qkv_bias,
    out_weight,
    mlp_gain,
    expert_gate_up,
    expert_down,
    shared_gate_up,
    shared_down,
    shared_gate,
    cotangent,
):
    count, width = layer_input.shape
    heads_here = qkv_bias.shape[0]
    head_dim = qkv_bias.shape[1] // 3
    experts, units = expert_down.shape[:2]
    shared = shared_down.shape[0] // units
    part = width // n_dp
    me = lax.axis_index("dp")
    core, chip = me % 2, me // 2
    tied = lax.optimization_barrier

    choose = expert_ids[:, :, None] == jnp.arange(experts, dtype=jnp.int32)[None, None, :]
    route = jnp.sum(route_weights[:, :, None] * choose.astype(F32), axis=1).T
    cot_all = lax.all_gather(
        jnp.concatenate([cotangent.astype(F32), jnp.pad(route, ((0, 0), (0, width - count)))], axis=0), "dp"
    )
    gate_rows = jnp.broadcast_to(shared_gate[None, :], (16, width))
    index = jnp.arange(count, dtype=jnp.int32)
    place = (me * count + index - doc_ids).astype(F32)
    freq = ROPE_BASE ** (-(jnp.arange(head_dim // 2, dtype=F32) * 2.0 / head_dim))
    angle = place[:, None] * freq[None, :]
    cosine = jnp.concatenate([jnp.cos(angle), jnp.cos(angle)], axis=-1)
    sine = jnp.concatenate([-jnp.sin(angle), jnp.sin(angle)], axis=-1)
    row, col = doc_ids[None, :], doc_ids[:, None]
    gain_one = attn_gain.astype(F32)[None, :]
    gain_two = mlp_gain.astype(F32)[None, :]
    attn_part, normed_one, qkv, attended = attention(
        layer_input, gain_one, qkv_weight, qkv_bias.astype(F32)[:, None, :], cosine, sine, row, col, out_weight
    )

    attn_part, shared_gate_up = tied((attn_part, shared_gate_up))
    attn_sum = lax.psum(attn_part, "tensor")
    w1 = jnp.concatenate(
        [
            jnp.transpose(expert_gate_up, (0, 2, 3, 1)),
            jnp.transpose(shared_gate_up.reshape(width, 2, shared, units), (2, 1, 3, 0)),
        ]
    )
    w2 = jnp.concatenate([expert_down, shared_down.reshape(shared, units, width)])
    cot_low, route_all = split_rounded(cot_all, count)
    attn_sum, w1, w2, cot_low, route_all = tied((attn_sum, w1, w2, cot_low, route_all))

    residual, tokens, tokens_wide = second_norm(layer_input, attn_sum, gain_two)
    swap = lambda v: lax.ppermute(v, "dp", [(i, i ^ 1) for i in range(n_dp)])
    beside = swap(tokens_wide)
    tok_all = lax.all_gather(tokens_wide, "dp")
    mlp_part, grad_top, grad_low, logit_grad = own_mlp(tokens, cotangent, route, gate_rows, w1, w2)
    mlp_sum = lax.psum_scatter(mlp_part, "tensor", scatter_dimension=0, tiled=True)
    line = n_tensor == 4 and n_dp == 8
    spot = lax.axis_index("tensor")
    hide = lambda other, starts, tokens, kept: chip_hidden(
        jnp.stack([core, chip, other, *starts]), tokens, cot_low, route_all, gate_rows, w1, w2, kept, part
    )
    in_order = (jnp.int32(0), jnp.int32(count))
    beside_starts = (core * count, (1 - core) * count)
    shared_gate_part = jnp.sum(logit_grad[0][:, None] * tokens.astype(F32), axis=0, keepdims=True)
    if line:
        is_inner = (spot == 1) | (spot == 2)
        inwards = lambda v: lax.ppermute(v, "tensor", [(0, 1), (3, 2)])
        across = lambda v: lax.ppermute(v, "tensor", [(1, 2), (2, 1)])
        outwards = lambda v: lax.ppermute(v, "tensor", [(1, 0), (2, 3)])
        ready = jnp.isnan(logit_grad[0, 0]).astype(jnp.int32)
        got = inwards(grad_top)
        kept = hide(chip + ready, beside_starts, [tokens_wide, beside], [])
        got, grad_low, kept = tied((got, grad_low, kept))
        grad_top = grad_top + got
        got, got_low = across(grad_top), inwards(grad_low)
        got, got_low, tok_all, shared_gate_part, kept = tied((got, got_low, tok_all, shared_gate_part, kept))
        grad_top, grad_low = grad_top + got, grad_low + got_low
        grad_top, mlp_sum = tied((grad_top, mlp_sum))
        mlp_sum = lax.all_gather(mlp_sum, "tensor", axis=0, tiled=True)
        end_top, got_low = outwards(grad_top), across(grad_low)
        kept = hide(chip ^ 1, in_order, [tok_all], kept)
        end_top, got_low, kept = tied((end_top, got_low, kept))
        grad_low = grad_low + got_low
        end_low = outwards(grad_low)
        kept = hide(chip ^ 2, in_order, [tok_all], kept)
        end_low, mlp_sum, kept = tied((end_low, mlp_sum, kept))
        totals = [grad_top, end_top, grad_low, end_low]
    else:
        is_inner = spot >= 0
        mlp_sum = lax.all_gather(mlp_sum, "tensor", axis=0, tiled=True)
        kept = []
        for k in range(n_dp // 2):
            kept = hide(jnp.int32(k), in_order, [tok_all], kept)
        totals = [lax.psum(v, "tensor") for v in (grad_top, grad_low)]
        totals = [totals[0], totals[0], totals[1], totals[1]]

    normed_one_part, residual_grad, branch_grad, projected_grad, bias_part, mlp_gain_part = attention_back(
        is_inner.astype(jnp.int32)[None], totals, residual, cotangent, gain_two, out_weight, qkv, qkv_weight,
        cosine, sine, row, col, layer_input, shared_gate_part, 1,
    )
    summed = lax.psum(normed_one_part.reshape(-1, width), "tensor")

    def finish(summed):
        inputs = layer_input.astype(F32)
        factor = lax.rsqrt(jnp.mean(inputs * inputs, axis=-1, keepdims=True) + EPS)
        bias_row = jnp.pad(bias_part, ((0, 0), (0, width - bias_part.shape[1])))
        small = jnp.concatenate([summed[count : count + 2], mlp_gain_part, bias_row])
        input_grad = (residual_grad + norm_back(inputs, factor, gain_one, summed[:count])).astype(BF16)
        return input_grad, jnp.pad(small, ((0, 4), (0, 0)))

    if line:
        at = jnp.stack([core, chip % 2, chip // 2, chip])
        other_at = jnp.stack([1 - core, chip % 2, chip // 2, chip])
        arrived = swap(token_products(other_at, normed_one, projected_grad, branch_grad, attended, None))
        x_keep, x_send, y_keep, y_send = token_products(
            at, normed_one, projected_grad, branch_grad, attended, arrived
        )
        x_send, y_send, kept = tied((x_send, y_send, kept))
        x_got, y_got = flip(x_send, 2), flip(y_send, 4)
        kept = hide(chip ^ 3, in_order, [tok_all], kept)
        *grads, one_peer, two_peer = weight_grads(at, *kept, cot_low, experts // 2)
        one_peer, x_got, y_got = tied((one_peer, x_got, y_got))
        x_own, x_send, y_own, y_send = turned_blocks(at, x_keep, x_got, y_keep, y_got)
        x_send, y_send, one_peer, two_peer, summed = tied((x_send, y_send, one_peer, two_peer, summed))
        x_got, y_got = flip(x_send, 4), flip(y_send, 2)
        one_peer, two_peer = swap(one_peer), swap(two_peer)
        summed, one_peer, two_peer = tied((summed, one_peer, two_peer))
        expert_one, expert_two, shared_one, shared_two = place_peer(at, one_peer, two_peer, grads, experts // 2)
        expert_one, summed = tied((expert_one, summed))
        input_grad, small = finish(summed)
        for bit in (1, 2, 4):
            small = small + flip(small, bit)
        x_got, y_got, input_grad, small, expert_one = tied((x_got, y_got, input_grad, small, expert_one))
        both = jnp.concatenate([x_own + x_got, y_own + y_got], axis=1)
        cut = projected_grad.shape[1]
        qkv_weight_grad, out_weight_grad = both[:, :cut], both[:, cut:].T
    else:
        at = jnp.stack([core, core, core, chip])
        *grads, one_peer, two_peer = weight_grads(at, *kept, cot_low, experts // 2)
        one_peer, two_peer = swap(one_peer), swap(two_peer)
        expert_one, expert_two, shared_one, shared_two = place_peer(at, one_peer, two_peer, grads, experts // 2)
        input_grad, small = finish(summed)
        small = lax.psum(small, "dp")
        joint = lambda v: v.reshape(2, count, BLOCKS // 2, -1).transpose(1, 2, 0, 3).reshape(count, width)
        out_weight_grad = lax.psum_scatter(tn(attended, joint(branch_grad)), "dp", scatter_dimension=1, tiled=True)
        qkv_weight_grad = lax.psum_scatter(
            tn(joint(normed_one), projected_grad), "dp", scatter_dimension=0, tiled=True
        )

    attn_gain_grad, shared_gate_grad, mlp_gain_grad = lax.dynamic_slice(small, (0, me * part), (3, part))
    bias_cols = 3 * head_dim // n_dp
    bias = small[3, : heads_here * 3 * head_dim].reshape(heads_here, 3 * head_dim)
    qkv_bias_grad = lax.dynamic_slice(bias, (0, me * bias_cols), (heads_here, bias_cols))
    layer_output = (residual + mlp_sum).astype(BF16)

    expert_gate_up_grad = jnp.transpose(expert_one, (0, 3, 1, 2))
    shared_gate_up_grad = jnp.transpose(shared_one, (3, 1, 0, 2)).reshape(part, 2, shared * units)
    shared_down_grad = shared_two.reshape(shared * units, part)
    return (
        layer_output,
        input_grad,
        attn_gain_grad,
        qkv_weight_grad,
        qkv_bias_grad,
        out_weight_grad,
        mlp_gain_grad,
        expert_gate_up_grad,
        expert_two,
        shared_gate_up_grad,
        shared_down_grad,
        shared_gate_grad,
    )


def solution(mesh):
    placed = (
        P("dp", None),
        P("dp"),
        P("dp", None),
        P("dp", None),
        P(),
        P(None, "tensor"),
        P("tensor", None),
        P("tensor", None),
        P(),
        P(None, None, None, "tensor"),
        P(None, "tensor", None),
        P(None, None, "tensor"),
        P("tensor", None),
        P(),
        P("dp", None),
    )
    return jax.shard_map(
        functools.partial(shards, mesh.shape["dp"], mesh.shape["tensor"]),
        mesh=mesh,
        in_specs=placed,
        out_specs=(
            P("dp", None),
            P("dp", None),
            P("dp"),
            P("dp", "tensor"),
            P("tensor", "dp"),
            P("tensor", "dp"),
            P("dp"),
            P(None, "dp", None, "tensor"),
            P(None, "tensor", "dp"),
            P("dp", None, "tensor"),
            P("tensor", "dp"),
            P("dp"),
        ),
        check_vma=False,
    )
```

```python
import functools

import jax
import jax.numpy as jnp
from jax import lax
from jax.experimental import pallas as pl
from jax.experimental.pallas import tpu as pltpu
from jax.sharding import PartitionSpec as P

EPS = 1e-06
ROPE_BASE = 1000000.0
NEG = -1e30
F32 = jnp.float32
BF16 = jnp.bfloat16
VMEM_LIMIT = 60 * 1024 * 1024
BLOCKS = 8
LIGHT = pl.CostEstimate(flops=1 << 20, bytes_accessed=1 << 16, transcendentals=0)


def nt(left, right):
    return lax.dot_general(left, right, (((1,), (1,)), ((), ())), preferred_element_type=F32)


def tn(left, right):
    return lax.dot_general(left, right, (((0,), (0,)), ((), ())), preferred_element_type=F32)


def nn(left, right):
    return jnp.dot(left, right, preferred_element_type=F32)


def norm_back(values_in, factor, gain_vec, upstream):
    scaled = gain_vec * upstream
    inner = jnp.mean(scaled * values_in, axis=-1, keepdims=True)
    return factor * scaled - values_in * factor**3 * inner


def turned(values, cosine, sine):
    return values * cosine + pltpu.roll(values, values.shape[1] // 2, 1) * sine


def turned_back(values, cosine, sine):
    return values * cosine - pltpu.roll(values, values.shape[1] // 2, 1) * sine


def head_probs(queries, keys, row_ref, col_ref):
    count = queries.shape[0]
    scores = nt(queries, keys) * queries.shape[1] ** (-0.5)
    rows = lax.broadcasted_iota(jnp.int32, (count, count), 0)
    cols = lax.broadcasted_iota(jnp.int32, (count, count), 1)
    scores = jnp.where((col_ref[...] == row_ref[...]) & (cols <= rows), scores, NEG)
    exponent = jnp.exp(scores - jnp.max(scores, axis=-1, keepdims=True))
    return exponent / jnp.sum(exponent, axis=-1, keepdims=True)


def split_columns(whole_ref, split_ref):
    part = whole_ref.shape[1] // BLOCKS
    for k in range(BLOCKS):
        split_ref[k % 2, :, k // 2 * part : (k // 2 + 1) * part] = whole_ref[:, k * part : (k + 1) * part]


def attn_kernel(x_ref, gain_ref, weight_ref, bias_ref, cos_ref, sin_ref, row_ref, col_ref, out_weight_ref,
                part_ref, split_ref, qkv_ref, attended_ref, normed_ref):
    head = pl.program_id(0)
    dim = cos_ref.shape[1]

    @pl.when(head == 0)
    def _():
        values = x_ref[...].astype(F32)
        factor = lax.rsqrt(jnp.mean(values * values, axis=-1, keepdims=True) + EPS)
        normed_ref[...] = (values * factor * gain_ref[...]).astype(BF16)
        split_columns(normed_ref, split_ref)

    projected = nn(normed_ref[...], weight_ref[...]) + bias_ref[0]
    queries = turned(projected[:, :dim], cos_ref[...], sin_ref[...]).astype(BF16)
    keys = turned(projected[:, dim : 2 * dim], cos_ref[...], sin_ref[...]).astype(BF16)
    values = projected[:, 2 * dim :].astype(BF16)
    qkv_ref[:, :dim] = queries
    qkv_ref[:, dim : 2 * dim] = keys
    qkv_ref[:, 2 * dim :] = values
    probs = head_probs(queries, keys, row_ref, col_ref)
    cols = pl.ds(pl.multiple_of(head * dim, dim), dim)
    attended_ref[:, cols] = nn(probs.astype(BF16), values).astype(BF16)

    @pl.when(head == pl.num_programs(0) - 1)
    def _():
        part_ref[...] = nn(attended_ref[...], out_weight_ref[...])


def whole(*shape):
    return pl.BlockSpec(shape, lambda *at: (0,) * len(shape))


def attention(x, gain, weight, bias, cosine, sine, row, col, out_weight):
    count, width = x.shape
    heads, _, cols = bias.shape
    return pl.pallas_call(
        attn_kernel,
        grid=(heads,),
        in_specs=[
            whole(count, width),
            whole(1, width),
            pl.BlockSpec((width, cols), lambda h: (0, h)),
            pl.BlockSpec((1, 1, cols), lambda h: (h, 0, 0)),
            whole(*cosine.shape),
            whole(*sine.shape),
            whole(1, count),
            whole(count, 1),
            whole(*out_weight.shape),
        ],
        out_specs=[
            whole(count, width),
            whole(2, count, width // 2),
            pl.BlockSpec((count, cols), lambda h: (0, h)),
            whole(count, out_weight.shape[0]),
        ],
        out_shape=[
            jax.ShapeDtypeStruct((count, width), F32),
            jax.ShapeDtypeStruct((2, count, width // 2), BF16),
            jax.ShapeDtypeStruct((count, heads * cols), BF16),
            jax.ShapeDtypeStruct((count, out_weight.shape[0]), BF16),
        ],
        scratch_shapes=[pltpu.VMEM((count, width), BF16)],
        compiler_params=pltpu.CompilerParams(
            dimension_semantics=("arbitrary",), vmem_limit_bytes=VMEM_LIMIT
        ),
        cost_estimate=LIGHT,
        name="attention",
    )(x, gain, weight, bias, cosine, sine, row, col, out_weight)


def norm_kernel(x_ref, sum_ref, gain_ref, residual_ref, low_ref, wide_ref):
    residual = x_ref[...].astype(F32) + sum_ref[...]
    factor = lax.rsqrt(jnp.mean(residual * residual, axis=-1, keepdims=True) + EPS)
    low = (residual * factor * gain_ref[...]).astype(BF16)
    residual_ref[...] = residual
    low_ref[...] = low
    wide_ref[...] = low.astype(F32)


def second_norm(x, attn_sum, gain):
    count, width = x.shape
    rows = count // 4
    spec = pl.BlockSpec((rows, width), lambda i: (i, 0))
    return pl.pallas_call(
        norm_kernel,
        grid=(4,),
        in_specs=[spec, spec, whole(1, width)],
        out_specs=[spec, spec, spec],
        out_shape=[
            jax.ShapeDtypeStruct((count, width), F32),
            jax.ShapeDtypeStruct((count, width), BF16),
            jax.ShapeDtypeStruct((count, width), F32),
        ],
        compiler_params=pltpu.CompilerParams(
            dimension_semantics=("arbitrary",), vmem_limit_bytes=VMEM_LIMIT
        ),
        name="second_norm",
    )(x, attn_sum, gain)


def back_kernel(total_ref, residual_ref, cot_ref, gain_ref, out_weight_ref, qkv_ref, weight_ref, cos_ref, sin_ref,
                row_ref, col_ref, x_ref, extra_ref, normed_grad_ref, residual_grad_ref, split_ref, projected_grad_ref, bias_ref,
                mlp_gain_ref, branch_ref, attended_grad_ref):
    head = pl.program_id(0)
    dim = cos_ref.shape[1]

    @pl.when(head == 0)
    def _():
        total = total_ref[...]
        residual = residual_ref[...]
        factor = lax.rsqrt(jnp.mean(residual * residual, axis=-1, keepdims=True) + EPS)
        scaled = gain_ref[...] * total
        inner = jnp.mean(scaled * residual, axis=-1, keepdims=True)
        residual_grad = cot_ref[...].astype(F32) + (factor * scaled - residual * factor**3 * inner)
        residual_grad_ref[...] = residual_grad
        branch_ref[...] = residual_grad.astype(BF16)
        split_columns(branch_ref, split_ref)
        mlp_gain_ref[...] = jnp.sum(total * residual * factor, axis=0, keepdims=True)
        attended_grad = nt(branch_ref[...], out_weight_ref[...]).astype(BF16)
        for k in range(attended_grad_ref.shape[0]):
            attended_grad_ref[k] = attended_grad[:, k * dim : (k + 1) * dim]

    queries, keys, values = qkv_ref[:, :dim], qkv_ref[:, dim : 2 * dim], qkv_ref[:, 2 * dim :]
    attended_grad = attended_grad_ref[head]
    probs = head_probs(queries, keys, row_ref, col_ref)
    prob_grad = nt(attended_grad, values)
    inner = jnp.sum(probs * prob_grad, axis=-1, keepdims=True)
    score = (probs * (prob_grad - inner) * dim ** (-0.5)).astype(BF16)
    query_grad = nn(score, keys).astype(BF16).astype(F32)
    key_grad = tn(score, queries).astype(BF16).astype(F32)
    value_grad = tn(probs.astype(BF16), attended_grad)
    grad = jnp.concatenate(
        [
            turned_back(query_grad, cos_ref[...], sin_ref[...]).astype(BF16),
            turned_back(key_grad, cos_ref[...], sin_ref[...]).astype(BF16),
            value_grad.astype(BF16),
        ],
        axis=1,
    )
    projected_grad_ref[...] = grad
    bias_ref[...] = jnp.sum(grad.astype(F32), axis=0, keepdims=True)
    product = nt(grad, weight_ref[...])
    groups, few = normed_grad_ref.shape[0], normed_grad_ref.shape[1] - 8

    @pl.when(head == 0)
    def _():
        for k in range(groups):
            normed_grad_ref[k, :few] = product[k * few : (k + 1) * few]

    @pl.when(head > 0)
    def _():
        for k in range(groups):
            normed_grad_ref[k, :few] += product[k * few : (k + 1) * few]

    @pl.when(head == pl.num_programs(0) - 1)
    def _():
        total = jnp.zeros((1, x_ref.shape[1]), F32)
        for k in range(groups):
            x = x_ref[k * few : (k + 1) * few].astype(F32)
            factor = lax.rsqrt(jnp.mean(x * x, axis=-1, keepdims=True) + EPS)
            total += jnp.sum(normed_grad_ref[k, :few] * x * factor, axis=0, keepdims=True)
        rows = lax.broadcasted_iota(jnp.int32, (8, x_ref.shape[1]), 0)
        small = jnp.where(rows == 0, total, jnp.where(rows == 1, extra_ref[...], 0.0))
        for k in range(groups):
            normed_grad_ref[k, few:] = small


def attention_back(total, residual, cotangent, gain, out_weight, qkv, weight, cosine, sine, row, col, x, extra,
                   groups):
    count, width = residual.shape
    dim = cosine.shape[1]
    cols = 3 * dim
    heads = qkv.shape[1] // cols
    return pl.pallas_call(
        back_kernel,
        grid=(heads,),
        in_specs=[
            whole(count, width),
            whole(count, width),
            whole(count, width),
            whole(1, width),
            whole(*out_weight.shape),
            pl.BlockSpec((count, cols), lambda h: (0, h)),
            pl.BlockSpec((width, cols), lambda h: (0, h)),
            whole(*cosine.shape),
            whole(*sine.shape),
            whole(1, count),
            whole(count, 1),
            whole(count, width),
            whole(1, width),
        ],
        out_specs=[
            whole(groups, count // groups + 8, width),
            whole(count, width),
            whole(2, count, width // 2),
            pl.BlockSpec((count, cols), lambda h: (0, h)),
            pl.BlockSpec((1, cols), lambda h: (0, h)),
            whole(1, width),
        ],
        out_shape=[
            jax.ShapeDtypeStruct((groups, count // groups + 8, width), F32),
            jax.ShapeDtypeStruct((count, width), F32),
            jax.ShapeDtypeStruct((2, count, width // 2), BF16),
            jax.ShapeDtypeStruct((count, heads * cols), BF16),
            jax.ShapeDtypeStruct((1, heads * cols), F32),
            jax.ShapeDtypeStruct((1, width), F32),
        ],
        scratch_shapes=[pltpu.VMEM((count, width), BF16), pltpu.VMEM((heads, count, dim), BF16)],
        compiler_params=pltpu.CompilerParams(
            dimension_semantics=("arbitrary",), vmem_limit_bytes=VMEM_LIMIT
        ),
        cost_estimate=LIGHT,
        name="attention_back",
    )(total, residual, cotangent, gain, out_weight, qkv, weight, cosine, sine, row, col, x, extra)


def hidden(w_one, w_two, tokens, branch, route_row):
    units = w_two.shape[0]
    mix = nt(w_one, tokens)
    gate, up = mix[:units], mix[units:]
    back = nt(w_two, branch)
    sigma = lax.logistic(gate)
    silu = gate * sigma
    act = silu * up
    scaled = back * route_row
    gate_grad = scaled * up * (sigma + silu * (1.0 - sigma))
    mix_grad = jnp.concatenate([gate_grad.astype(BF16), (scaled * silu).astype(BF16)], axis=0)
    return act, back, (act * route_row).astype(BF16), mix_grad


def open_row(gate_rows, tokens):
    return lax.logistic(nt(gate_rows, tokens)[:1])


def own_kernel(experts, tok_ref, cot_ref, route_ref, gate_ref, w1_ref, w2_ref, out_ref, dx_ref, logit_ref,
               open_ref):
    step = pl.program_id(0)
    group, units, width = w2_ref.shape
    shared = step * group >= experts

    @pl.when(step == 0)
    def _():
        for ref in (out_ref, dx_ref):
            ref[...] = jnp.zeros_like(ref)
        logit_ref[...] = jnp.zeros_like(logit_ref)
        open_ref[...] = open_row(gate_ref[...], tok_ref[...])

    weighted, mix_grads = [], []
    for k in range(group):
        act, back, scaled, mix_grad = hidden(
            w1_ref[k].reshape(2 * units, width),
            w2_ref[k],
            tok_ref[...],
            cot_ref[...],
            jnp.where(shared, open_ref[...], route_ref[k]),
        )
        weighted.append(scaled)
        mix_grads.append(mix_grad)
        logit_ref[...] += jnp.where(shared, jnp.sum(act * back, axis=0, keepdims=True), 0.0)
    out_ref[...] += tn(jnp.concatenate(weighted), w2_ref[...].reshape(group * units, width))
    dx_ref[...] += tn(jnp.concatenate(mix_grads), w1_ref[...].reshape(group * 2 * units, width))

    @pl.when(step == pl.num_programs(0) - 1)
    def _():
        opened = open_ref[...]
        logit = opened * (1.0 - opened) * logit_ref[...]
        logit_ref[...] = logit
        column = jnp.broadcast_to(logit, (8, logit.shape[1])).T[:, :1]
        dx_ref[...] += column * gate_ref[:1].astype(F32)


def own_mlp(tokens, cotangent, route, gate_rows, w1, w2):
    count, width = tokens.shape
    tiles, units = w2.shape[:2]
    experts = route.shape[0]
    group = 2
    return pl.pallas_call(
        functools.partial(own_kernel, experts),
        grid=(tiles // group,),
        in_specs=[
            whole(count, width),
            whole(count, width),
            pl.BlockSpec((group, 1, count), lambda i: (jnp.minimum(i, experts // group - 1), 0, 0)),
            whole(*gate_rows.shape),
            pl.BlockSpec((group, 2, units, width), lambda i: (i, 0, 0, 0)),
            pl.BlockSpec((group, units, width), lambda i: (i, 0, 0)),
        ],
        out_specs=[whole(count, width), whole(count, width), whole(1, count)],
        out_shape=[
            jax.ShapeDtypeStruct((count, width), F32),
            jax.ShapeDtypeStruct((count, width), F32),
            jax.ShapeDtypeStruct((1, count), F32),
        ],
        scratch_shapes=[pltpu.VMEM((1, count), F32)],
        compiler_params=pltpu.CompilerParams(
            dimension_semantics=("arbitrary",), vmem_limit_bytes=VMEM_LIMIT
        ),
        cost_estimate=LIGHT,
        name="own_mlp",
    )(tokens, cotangent, route[:, None, :], gate_rows, w1, w2)


def chip_kernel(here, at_ref, even_ref, odd_ref, cot_ref, route_ref, gate_ref, w1_ref, w2_ref, *refs):
    mix_grad_ref, weighted_ref, part_ref, tok_ref, open_ref = refs[-5:]
    step = pl.program_id(0)
    units, width = w2_ref.shape[-2:]
    cores, experts, count = route_ref.shape
    core = at_ref[0]

    @pl.when(step == 0)
    def _():
        for start, ref in ((at_ref[3], even_ref), (at_ref[4], odd_ref)):
            tok_ref[pl.ds(pl.multiple_of(start, count), count), :] = ref[...].reshape(count, width).astype(BF16)
        part = part_ref.shape[1]
        part_ref[...] = tok_ref[:, pl.ds(pl.multiple_of(at_ref[1] * part, part), part)]
        open_ref[...] = open_row(gate_ref[...], tok_ref[...])

    expert = jnp.minimum(core * here + step, experts - 1)
    route_row = jnp.concatenate([route_ref[k, pl.ds(expert, 1), :] for k in range(cores)], axis=1)
    _, _, weighted, mix_grad = hidden(
        w1_ref[...].reshape(2 * units, width),
        w2_ref[0],
        tok_ref[...],
        cot_ref[...],
        jnp.where(step >= here, open_ref[...], route_row),
    )
    mix_grad_ref[0] = mix_grad
    weighted_ref[0] = weighted


def chip_hidden(at, tokens, cotangent, route, gate_rows, w1, w2, kept, part):
    total, width = cotangent.shape
    tiles, units = w2.shape[:2]
    experts, count = route.shape[1:]
    here, shared = experts // 2, (tiles - experts) // 2
    rows = 2 * count
    own = lambda i, at: jnp.where(i < here, at[0] * here + i, experts + at[0] * shared + i - here)
    fixed = lambda *shape: pl.BlockSpec(shape, lambda i, at: (0,) * len(shape))
    if len(tokens) == 2:
        sources = [fixed(count, width), fixed(count, width)]
    else:
        tokens = [tokens[0], tokens[0]]
        sources = [
            pl.BlockSpec((1, count, width), lambda i, at: (2 * at[2], 0, 0)),
            pl.BlockSpec((1, count, width), lambda i, at: (2 * at[2] + 1, 0, 0)),
        ]
    shapes = [
        jax.ShapeDtypeStruct((here + shared, 2 * units, total), BF16),
        jax.ShapeDtypeStruct((here + shared, units, total), BF16),
        jax.ShapeDtypeStruct((total, 2 * part), BF16),
    ]
    inputs = [*tokens, cotangent, route, gate_rows, w1, w2]
    return pl.pallas_call(
        functools.partial(chip_kernel, here),
        grid_spec=pltpu.PrefetchScalarGridSpec(
            num_scalar_prefetch=1,
            grid=(here + shared,),
            in_specs=[
                *sources,
                pl.BlockSpec((rows, width), lambda i, at: (at[2], 0)),
                pl.BlockSpec((2, experts, count), lambda i, at: (at[2], 0, 0)),
                fixed(*gate_rows.shape),
                pl.BlockSpec((1, 2, units, width), lambda i, at: (own(i, at), 0, 0, 0)),
                pl.BlockSpec((1, units, width), lambda i, at: (own(i, at), 0, 0)),
                *[pl.BlockSpec(memory_space=pl.ANY) for _ in kept],
            ],
            out_specs=[
                pl.BlockSpec((1, 2 * units, rows), lambda i, at: (i, 0, at[2])),
                pl.BlockSpec((1, units, rows), lambda i, at: (i, 0, at[2])),
                pl.BlockSpec((rows, 2 * part), lambda i, at: (at[2], 0)),
            ],
            scratch_shapes=[pltpu.VMEM((rows, width), BF16), pltpu.VMEM((1, rows), F32)],
        ),
        out_shape=shapes,
        input_output_aliases={1 + len(inputs) + k: k for k in range(len(kept))},
        compiler_params=pltpu.CompilerParams(
            dimension_semantics=("arbitrary",), vmem_limit_bytes=VMEM_LIMIT
        ),
        cost_estimate=LIGHT,
        name="chip_hidden",
    )(at, *inputs, *kept)


def both_products(normed_ref, projected_ref, branch_ref, attended_ref):
    return jnp.concatenate(
        [tn(normed_ref[0], projected_ref[...]), tn(branch_ref[0], attended_ref[...])], axis=1
    )


def sent_kernel(at_ref, normed_ref, projected_ref, branch_ref, attended_ref, out_ref):
    out_ref[0] = both_products(normed_ref, projected_ref, branch_ref, attended_ref)


def held_kernel(at_ref, normed_ref, projected_ref, branch_ref, attended_ref, arrived_ref, *out_refs):
    block = pl.program_id(0)
    along_y, along_x = block // 2, lax.rem(block, 2)
    value = both_products(normed_ref, projected_ref, branch_ref, attended_ref) + arrived_ref[0]
    half = value.shape[1] // 2
    x_keep_ref, x_send_ref, y_keep_ref, y_send_ref = out_refs
    for same, index, columns, keep_ref, send_ref in (
        (along_x == at_ref[1], along_y, value[:, :half], x_keep_ref, x_send_ref),
        (along_y == at_ref[2], along_x, value[:, half:], y_keep_ref, y_send_ref),
    ):
        @pl.when(same)
        def _():
            keep_ref[index] = columns

        @pl.when(jnp.logical_not(same))
        def _():
            send_ref[index] = columns


def token_products(at, normed, projected, branch, attended, arrived):
    _, count, half = normed.shape
    blocks = BLOCKS // 2
    part = half // blocks
    cols = projected.shape[1] + attended.shape[1]
    side = pl.BlockSpec((1, count, part), lambda i, at: (at[0], 0, i))
    fixed = lambda *shape: pl.BlockSpec(shape, lambda i, at: (0,) * len(shape))
    block = pl.BlockSpec((1, part, cols), lambda i, at: (i, 0, 0))
    inputs = [normed, projected, branch, attended]
    in_specs = [side, fixed(*projected.shape), side, fixed(*attended.shape)]
    if arrived is None:
        kernel, out_specs = sent_kernel, block
        out_shape = jax.ShapeDtypeStruct((blocks, part, cols), F32)
    else:
        kernel, out_specs = held_kernel, [fixed(2, part, cols // 2)] * 4
        out_shape = [jax.ShapeDtypeStruct((2, part, cols // 2), F32)] * 4
        inputs, in_specs = [*inputs, arrived], [*in_specs, block]
    return pl.pallas_call(
        kernel,
        grid_spec=pltpu.PrefetchScalarGridSpec(
            num_scalar_prefetch=1, grid=(blocks,), in_specs=in_specs, out_specs=out_specs
        ),
        out_shape=out_shape,
        compiler_params=pltpu.CompilerParams(
            dimension_semantics=("arbitrary",), vmem_limit_bytes=VMEM_LIMIT
        ),
        cost_estimate=LIGHT,
        name="token_products",
    )(at, *inputs)


def turn_kernel(at_ref, x_keep_ref, x_got_ref, y_keep_ref, y_got_ref, x_own_ref, x_send_ref, y_own_ref, y_send_ref):
    for mine, keep_ref, got_ref, own_ref, send_ref in (
        (at_ref[2], x_keep_ref, x_got_ref, x_own_ref, x_send_ref),
        (at_ref[1], y_keep_ref, y_got_ref, y_own_ref, y_send_ref),
    ):
        own_ref[...] = keep_ref[mine] + got_ref[mine]
        send_ref[...] = keep_ref[1 - mine] + got_ref[1 - mine]


def turned_blocks(at, x_keep, x_got, y_keep, y_got):
    _, part, cols = x_keep.shape
    rows = part // 4
    spec = pl.BlockSpec((2, rows, cols), lambda i, at: (0, i, 0))
    out = pl.BlockSpec((rows, cols), lambda i, at: (i, 0))
    return pl.pallas_call(
        turn_kernel,
        grid_spec=pltpu.PrefetchScalarGridSpec(
            num_scalar_prefetch=1, grid=(4,), in_specs=[spec] * 4, out_specs=[out] * 4
        ),
        out_shape=[jax.ShapeDtypeStruct((part, cols), F32)] * 4,
        compiler_params=pltpu.CompilerParams(
            dimension_semantics=("arbitrary",), vmem_limit_bytes=VMEM_LIMIT
        ),
        cost_estimate=LIGHT,
        name="turned_blocks",
    )(at, x_keep, x_got, y_keep, y_got)


def weights_kernel(here, at_ref, mix_grad_ref, weighted_ref, tok_ref, cot_ref, *refs):
    part = refs[0].shape[-1]
    expert_refs, shared_refs, peer_refs = refs[:2], refs[2:4], refs[4:]
    core, step = at_ref[0], pl.program_id(0)
    products = nn(mix_grad_ref[0], tok_ref[...]), nn(weighted_ref[0], cot_ref[...])
    for value, expert_ref, shared_ref, peer_ref in zip(products, expert_refs, shared_refs, peer_refs, strict=True):
        low, high = value[:, :part], value[:, part:]
        mine = jnp.where(core == 0, low, high)
        peer_ref[...] = jnp.where(core == 0, high, low).reshape(peer_ref.shape)

        @pl.when(step < here)
        def _():
            expert_ref[...] = mine.reshape(expert_ref.shape)

        @pl.when(step >= here)
        def _():
            shared_ref[...] = mine.reshape(shared_ref.shape)


def tile_specs(core_of, here, shared, units, part):
    expert = lambda i, at: core_of(at) * here + jnp.minimum(i, here - 1)
    common = lambda i, at: core_of(at) * shared + jnp.maximum(i - here, 0)
    return [
        pl.BlockSpec((1, 2, units, part), lambda i, at: (expert(i, at), 0, 0, 0)),
        pl.BlockSpec((1, units, part), lambda i, at: (expert(i, at), 0, 0)),
        pl.BlockSpec((1, 2, units, part), lambda i, at: (common(i, at), 0, 0, 0)),
        pl.BlockSpec((1, units, part), lambda i, at: (common(i, at), 0, 0)),
    ]


def weight_grads(at, mix_grads, weighted, tokens, cotangent, here):
    tiles, units, total = weighted.shape
    part = tokens.shape[1] // 2
    shared = tiles - here
    one = lambda count: jax.ShapeDtypeStruct((count, 2, units, part), F32)
    two = lambda count: jax.ShapeDtypeStruct((count, units, part), F32)
    return pl.pallas_call(
        functools.partial(weights_kernel, here),
        grid_spec=pltpu.PrefetchScalarGridSpec(
            num_scalar_prefetch=1,
            grid=(tiles,),
            in_specs=[
                pl.BlockSpec((1, 2 * units, total), lambda i, at: (i, 0, 0)),
                pl.BlockSpec((1, units, total), lambda i, at: (i, 0, 0)),
                pl.BlockSpec((total, 2 * part), lambda i, at: (0, 0)),
                pl.BlockSpec((total, 2 * part), lambda i, at: (0, at[3])),
            ],
            out_specs=[
                *tile_specs(lambda at: at[0], here, shared, units, part),
                pl.BlockSpec((1, 2, units, part), lambda i, at: (i, 0, 0, 0)),
                pl.BlockSpec((1, units, part), lambda i, at: (i, 0, 0)),
            ],
        ),
        out_shape=[one(2 * here), two(2 * here), one(2 * shared), two(2 * shared), one(tiles), two(tiles)],
        compiler_params=pltpu.CompilerParams(
            dimension_semantics=("arbitrary",), vmem_limit_bytes=VMEM_LIMIT
        ),
        cost_estimate=LIGHT,
        name="weight_grads",
    )(at, mix_grads, weighted, tokens, cotangent)


def place_kernel(here, at_ref, one_ref, two_ref, *refs):
    step = pl.program_id(0)
    expert_one_ref, expert_two_ref, shared_one_ref, shared_two_ref = refs[-4:]

    @pl.when(step < here)
    def _():
        expert_one_ref[...] = one_ref[...]
        expert_two_ref[...] = two_ref[...]

    @pl.when(step >= here)
    def _():
        shared_one_ref[...] = one_ref[...]
        shared_two_ref[...] = two_ref[...]


def place_peer(at, one, two, grads, here):
    tiles, units, part = two.shape
    return pl.pallas_call(
        functools.partial(place_kernel, here),
        grid_spec=pltpu.PrefetchScalarGridSpec(
            num_scalar_prefetch=1,
            grid=(tiles,),
            in_specs=[
                pl.BlockSpec((1, 2, units, part), lambda i, at: (i, 0, 0, 0)),
                pl.BlockSpec((1, units, part), lambda i, at: (i, 0, 0)),
                *[pl.BlockSpec(memory_space=pl.ANY)] * 4,
            ],
            out_specs=tile_specs(lambda at: 1 - at[0], here, tiles - here, units, part),
        ),
        out_shape=[jax.ShapeDtypeStruct(g.shape, g.dtype) for g in grads],
        input_output_aliases={3 + k: k for k in range(4)},
        compiler_params=pltpu.CompilerParams(
            dimension_semantics=("arbitrary",), vmem_limit_bytes=VMEM_LIMIT
        ),
        cost_estimate=LIGHT,
        name="place_peer",
    )(at, one, two, *grads)


def split_kernel(in_ref, out_ref, route_ref):
    count = out_ref.shape[0]
    out_ref[...] = in_ref[0, :count].astype(BF16)
    route_ref[...] = in_ref[0, count:, :count][None]


def split_rounded(gathered, count):
    blocks, rows, width = gathered.shape
    extra = rows - count
    return pl.pallas_call(
        split_kernel,
        grid=(blocks,),
        in_specs=[pl.BlockSpec((1, rows, width), lambda i: (i, 0, 0))],
        out_specs=[
            pl.BlockSpec((count, width), lambda i: (i, 0)),
            pl.BlockSpec((1, extra, count), lambda i: (i, 0, 0)),
        ],
        out_shape=[
            jax.ShapeDtypeStruct((blocks * count, width), BF16),
            jax.ShapeDtypeStruct((blocks, extra, count), F32),
        ],
        compiler_params=pltpu.CompilerParams(
            dimension_semantics=("arbitrary",), vmem_limit_bytes=VMEM_LIMIT
        ),
        name="split_rounded",
    )(gathered)


def flip(value, bit):
    return lax.ppermute(value, "dp", [(i, i ^ bit) for i in range(8)])


def take(value, number, axis):
    return lax.dynamic_index_in_dim(value, number, axis, keepdims=False)


def shards(
    n_dp,
    n_tensor,
    layer_input,
    doc_ids,
    expert_ids,
    route_weights,
    attn_gain,
    qkv_weight,
    qkv_bias,
    out_weight,
    mlp_gain,
    expert_gate_up,
    expert_down,
    shared_gate_up,
    shared_down,
    shared_gate,
    cotangent,
):
    count, width = layer_input.shape
    heads_here = qkv_bias.shape[0]
    head_dim = qkv_bias.shape[1] // 3
    experts, units = expert_down.shape[:2]
    shared = shared_down.shape[0] // units
    part = width // n_dp
    me = lax.axis_index("dp")
    core, chip = me % 2, me // 2
    tied = lax.optimization_barrier

    choose = expert_ids[:, :, None] == jnp.arange(experts, dtype=jnp.int32)[None, None, :]
    route = jnp.sum(route_weights[:, :, None] * choose.astype(F32), axis=1).T
    cot_all = lax.all_gather(
        jnp.concatenate([cotangent.astype(F32), jnp.pad(route, ((0, 0), (0, width - count)))], axis=0), "dp"
    )
    gate_rows = jnp.broadcast_to(shared_gate[None, :], (16, width))
    index = jnp.arange(count, dtype=jnp.int32)
    place = (me * count + index - doc_ids).astype(F32)
    freq = ROPE_BASE ** (-(jnp.arange(head_dim // 2, dtype=F32) * 2.0 / head_dim))
    angle = place[:, None] * freq[None, :]
    cosine = jnp.concatenate([jnp.cos(angle), jnp.cos(angle)], axis=-1)
    sine = jnp.concatenate([-jnp.sin(angle), jnp.sin(angle)], axis=-1)
    row, col = doc_ids[None, :], doc_ids[:, None]
    gain_one = attn_gain.astype(F32)[None, :]
    gain_two = mlp_gain.astype(F32)[None, :]
    attn_part, normed_one, qkv, attended = attention(
        layer_input, gain_one, qkv_weight, qkv_bias.astype(F32)[:, None, :], cosine, sine, row, col, out_weight
    )

    attn_part, shared_gate_up = tied((attn_part, shared_gate_up))
    attn_sum = lax.psum(attn_part, "tensor")
    w1 = jnp.concatenate(
        [
            jnp.transpose(expert_gate_up, (0, 2, 3, 1)),
            jnp.transpose(shared_gate_up.reshape(width, 2, shared, units), (2, 1, 3, 0)),
        ]
    )
    w2 = jnp.concatenate([expert_down, shared_down.reshape(shared, units, width)])
    cot_low, route_all = split_rounded(cot_all, count)
    attn_sum, w1, w2, cot_low, route_all = tied((attn_sum, w1, w2, cot_low, route_all))

    residual, tokens, tokens_wide = second_norm(layer_input, attn_sum, gain_two)
    swap = lambda v: lax.ppermute(v, "dp", [(i, i ^ 1) for i in range(n_dp)])
    beside = swap(tokens_wide)
    tok_all = lax.all_gather(tokens_wide, "dp")
    mlp_part, normed_two_part, logit_grad = own_mlp(tokens, cotangent, route, gate_rows, w1, w2)
    hide = lambda other, starts, tokens, kept: chip_hidden(
        jnp.stack([core, chip, other, *starts]), tokens, cot_low, route_all, gate_rows, w1, w2, kept, part
    )
    in_order = (jnp.int32(0), jnp.int32(count))
    beside_starts = (core * count, (1 - core) * count)
    shared_gate_part = jnp.sum(logit_grad[0][:, None] * tokens.astype(F32), axis=0, keepdims=True)
    normed_two_total = lax.psum(normed_two_part, "tensor")
    last = n_dp == 8
    if last:
        ready = jnp.isnan(logit_grad[0, 0]).astype(jnp.int32)
        kept = hide(chip + ready, beside_starts, [tokens_wide, beside], [])
        kept = hide(chip ^ 1, in_order, [tok_all], kept)
        kept = hide(chip ^ 2, in_order, [tok_all], kept)
    else:
        kept = []
        for k in range(n_dp // 2):
            kept = hide(jnp.int32(k), in_order, [tok_all], kept)
    normed_two_total, mlp_part, shared_gate_part, kept = tied((normed_two_total, mlp_part, shared_gate_part, kept))
    mlp_sum = lax.psum_scatter(mlp_part, "tensor", scatter_dimension=0, tiled=True)

    normed_one_part, residual_grad, branch_grad, projected_grad, bias_part, mlp_gain_part = attention_back(
        normed_two_total, residual, cotangent, gain_two, out_weight, qkv, qkv_weight,
        cosine, sine, row, col, layer_input, shared_gate_part, 1,
    )
    summed = lax.psum(normed_one_part.reshape(-1, width), "tensor")

    def finish(summed):
        inputs = layer_input.astype(F32)
        factor = lax.rsqrt(jnp.mean(inputs * inputs, axis=-1, keepdims=True) + EPS)
        bias_row = jnp.pad(bias_part, ((0, 0), (0, width - bias_part.shape[1])))
        small = jnp.concatenate([summed[count : count + 2], mlp_gain_part, bias_row])
        input_grad = (residual_grad + norm_back(inputs, factor, gain_one, summed[:count])).astype(BF16)
        return input_grad, jnp.pad(small, ((0, 4), (0, 0)))

    if last:
        at = jnp.stack([core, chip % 2, chip // 2, chip])
        other_at = jnp.stack([1 - core, chip % 2, chip // 2, chip])
        arrived = swap(token_products(other_at, normed_one, projected_grad, branch_grad, attended, None))
        x_keep, x_send, y_keep, y_send = token_products(
            at, normed_one, projected_grad, branch_grad, attended, arrived
        )
        x_send, y_send, kept = tied((x_send, y_send, kept))
        x_got, y_got = flip(x_send, 2), flip(y_send, 4)
        kept = hide(chip ^ 3, in_order, [tok_all], kept)
        *grads, one_peer, two_peer = weight_grads(at, *kept, cot_low, experts // 2)
        one_peer, x_got, y_got, mlp_sum = tied((one_peer, x_got, y_got, mlp_sum))
        mlp_sum = lax.all_gather(mlp_sum, "tensor", axis=0, tiled=True)
        x_own, x_send, y_own, y_send = turned_blocks(at, x_keep, x_got, y_keep, y_got)
        x_send, y_send, one_peer, two_peer, summed = tied((x_send, y_send, one_peer, two_peer, summed))
        x_got, y_got = flip(x_send, 4), flip(y_send, 2)
        one_peer, two_peer = swap(one_peer), swap(two_peer)
        summed, one_peer, two_peer = tied((summed, one_peer, two_peer))
        expert_one, expert_two, shared_one, shared_two = place_peer(at, one_peer, two_peer, grads, experts // 2)
        expert_one, summed = tied((expert_one, summed))
        input_grad, small = finish(summed)
        for bit in (1, 2, 4):
            small = small + flip(small, bit)
        x_got, y_got, input_grad, small, expert_one = tied((x_got, y_got, input_grad, small, expert_one))
        both = jnp.concatenate([x_own + x_got, y_own + y_got], axis=1)
        cut = projected_grad.shape[1]
        qkv_weight_grad, out_weight_grad = both[:, :cut], both[:, cut:].T
        mlp_sum, qkv_weight_grad = tied((mlp_sum, qkv_weight_grad))
    else:
        at = jnp.stack([core, core, core, chip])
        *grads, one_peer, two_peer = weight_grads(at, *kept, cot_low, experts // 2)
        one_peer, two_peer = swap(one_peer), swap(two_peer)
        expert_one, expert_two, shared_one, shared_two = place_peer(at, one_peer, two_peer, grads, experts // 2)
        input_grad, small = finish(summed)
        small = lax.psum(small, "dp")
        mlp_sum = lax.all_gather(mlp_sum, "tensor", axis=0, tiled=True)
        joint = lambda v: v.reshape(2, count, BLOCKS // 2, -1).transpose(1, 2, 0, 3).reshape(count, width)
        out_weight_grad = lax.psum_scatter(tn(attended, joint(branch_grad)), "dp", scatter_dimension=1, tiled=True)
        qkv_weight_grad = lax.psum_scatter(
            tn(joint(normed_one), projected_grad), "dp", scatter_dimension=0, tiled=True
        )

    attn_gain_grad, shared_gate_grad, mlp_gain_grad = lax.dynamic_slice(small, (0, me * part), (3, part))
    bias_cols = 3 * head_dim // n_dp
    bias = small[3, : heads_here * 3 * head_dim].reshape(heads_here, 3 * head_dim)
    qkv_bias_grad = lax.dynamic_slice(bias, (0, me * bias_cols), (heads_here, bias_cols))
    layer_output = (residual + mlp_sum).astype(BF16)

    expert_gate_up_grad = jnp.transpose(expert_one, (0, 3, 1, 2))
    shared_gate_up_grad = jnp.transpose(shared_one, (3, 1, 0, 2)).reshape(part, 2, shared * units)
    shared_down_grad = shared_two.reshape(shared * units, part)
    return (
        layer_output,
        input_grad,
        attn_gain_grad,
        qkv_weight_grad,
        qkv_bias_grad,
        out_weight_grad,
        mlp_gain_grad,
        expert_gate_up_grad,
        expert_two,
        shared_gate_up_grad,
        shared_down_grad,
        shared_gate_grad,
    )


def solution(mesh):
    placed = (
        P("dp", None),
        P("dp"),
        P("dp", None),
        P("dp", None),
        P(),
        P(None, "tensor"),
        P("tensor", None),
        P("tensor", None),
        P(),
        P(None, None, None, "tensor"),
        P(None, "tensor", None),
        P(None, None, "tensor"),
        P("tensor", None),
        P(),
        P("dp", None),
    )
    return jax.shard_map(
        functools.partial(shards, mesh.shape["dp"], mesh.shape["tensor"]),
        mesh=mesh,
        in_specs=placed,
        out_specs=(
            P("dp", None),
            P("dp", None),
            P("dp"),
            P("dp", "tensor"),
            P("tensor", "dp"),
            P("tensor", "dp"),
            P("dp"),
            P(None, "dp", None, "tensor"),
            P(None, "tensor", "dp"),
            P("dp", None, "tensor"),
            P("tensor", "dp"),
            P("dp"),
        ),
        check_vma=False,
    )
```

```python
import functools

import jax
import jax.numpy as jnp
from jax import lax
from jax.experimental import pallas as pl
from jax.experimental.pallas import tpu as pltpu
from jax.sharding import PartitionSpec as P

EPS = 1e-06
ROPE_BASE = 1000000.0
NEG = -1e30
F32 = jnp.float32
BF16 = jnp.bfloat16
VMEM_LIMIT = 60 * 1024 * 1024
BLOCKS = 8
LIGHT = pl.CostEstimate(flops=1 << 20, bytes_accessed=1 << 16, transcendentals=0)


def nt(left, right):
    return lax.dot_general(left, right, (((1,), (1,)), ((), ())), preferred_element_type=F32)


def tn(left, right):
    return lax.dot_general(left, right, (((0,), (0,)), ((), ())), preferred_element_type=F32)


def nn(left, right):
    return jnp.dot(left, right, preferred_element_type=F32)


def norm_back(values_in, factor, gain_vec, upstream):
    scaled = gain_vec * upstream
    inner = jnp.mean(scaled * values_in, axis=-1, keepdims=True)
    return factor * scaled - values_in * factor**3 * inner


def turned(values, cosine, sine):
    return values * cosine + pltpu.roll(values, values.shape[1] // 2, 1) * sine


def turned_back(values, cosine, sine):
    return values * cosine - pltpu.roll(values, values.shape[1] // 2, 1) * sine


def head_probs(queries, keys, row_ref, col_ref):
    count = queries.shape[0]
    scores = nt(queries, keys) * queries.shape[1] ** (-0.5)
    rows = lax.broadcasted_iota(jnp.int32, (count, count), 0)
    cols = lax.broadcasted_iota(jnp.int32, (count, count), 1)
    scores = jnp.where((col_ref[...] == row_ref[...]) & (cols <= rows), scores, NEG)
    exponent = jnp.exp(scores - jnp.max(scores, axis=-1, keepdims=True))
    return exponent / jnp.sum(exponent, axis=-1, keepdims=True)


def split_columns(whole_ref, split_ref):
    part = whole_ref.shape[1] // BLOCKS
    for k in range(BLOCKS):
        split_ref[k % 2, :, k // 2 * part : (k // 2 + 1) * part] = whole_ref[:, k * part : (k + 1) * part]


def attn_kernel(x_ref, gain_ref, weight_ref, bias_ref, cos_ref, sin_ref, row_ref, col_ref, out_weight_ref,
                part_ref, split_ref, qkv_ref, attended_ref, normed_ref):
    head = pl.program_id(0)
    dim = cos_ref.shape[1]

    @pl.when(head == 0)
    def _():
        values = x_ref[...].astype(F32)
        factor = lax.rsqrt(jnp.mean(values * values, axis=-1, keepdims=True) + EPS)
        normed_ref[...] = (values * factor * gain_ref[...]).astype(BF16)
        split_columns(normed_ref, split_ref)

    projected = nn(normed_ref[...], weight_ref[...]) + bias_ref[0]
    queries = turned(projected[:, :dim], cos_ref[...], sin_ref[...]).astype(BF16)
    keys = turned(projected[:, dim : 2 * dim], cos_ref[...], sin_ref[...]).astype(BF16)
    values = projected[:, 2 * dim :].astype(BF16)
    qkv_ref[:, :dim] = queries
    qkv_ref[:, dim : 2 * dim] = keys
    qkv_ref[:, 2 * dim :] = values
    probs = head_probs(queries, keys, row_ref, col_ref)
    cols = pl.ds(pl.multiple_of(head * dim, dim), dim)
    attended_ref[:, cols] = nn(probs.astype(BF16), values).astype(BF16)

    @pl.when(head == pl.num_programs(0) - 1)
    def _():
        part_ref[...] = nn(attended_ref[...], out_weight_ref[...])


def whole(*shape):
    return pl.BlockSpec(shape, lambda *at: (0,) * len(shape))


def attention(x, gain, weight, bias, cosine, sine, row, col, out_weight):
    count, width = x.shape
    heads, _, cols = bias.shape
    return pl.pallas_call(
        attn_kernel,
        grid=(heads,),
        in_specs=[
            whole(count, width),
            whole(1, width),
            pl.BlockSpec((width, cols), lambda h: (0, h)),
            pl.BlockSpec((1, 1, cols), lambda h: (h, 0, 0)),
            whole(*cosine.shape),
            whole(*sine.shape),
            whole(1, count),
            whole(count, 1),
            whole(*out_weight.shape),
        ],
        out_specs=[
            whole(count, width),
            whole(2, count, width // 2),
            pl.BlockSpec((count, cols), lambda h: (0, h)),
            whole(count, out_weight.shape[0]),
        ],
        out_shape=[
            jax.ShapeDtypeStruct((count, width), F32),
            jax.ShapeDtypeStruct((2, count, width // 2), BF16),
            jax.ShapeDtypeStruct((count, heads * cols), BF16),
            jax.ShapeDtypeStruct((count, out_weight.shape[0]), BF16),
        ],
        scratch_shapes=[pltpu.VMEM((count, width), BF16)],
        compiler_params=pltpu.CompilerParams(
            dimension_semantics=("arbitrary",), vmem_limit_bytes=VMEM_LIMIT
        ),
        cost_estimate=LIGHT,
        name="attention",
    )(x, gain, weight, bias, cosine, sine, row, col, out_weight)


def norm_kernel(x_ref, sum_ref, gain_ref, residual_ref, low_ref, wide_ref):
    residual = x_ref[...].astype(F32) + sum_ref[...]
    factor = lax.rsqrt(jnp.mean(residual * residual, axis=-1, keepdims=True) + EPS)
    low = (residual * factor * gain_ref[...]).astype(BF16)
    residual_ref[...] = residual
    low_ref[...] = low
    wide_ref[...] = low.astype(F32)


def second_norm(x, attn_sum, gain):
    count, width = x.shape
    rows = count // 4
    spec = pl.BlockSpec((rows, width), lambda i: (i, 0))
    return pl.pallas_call(
        norm_kernel,
        grid=(4,),
        in_specs=[spec, spec, whole(1, width)],
        out_specs=[spec, spec, spec],
        out_shape=[
            jax.ShapeDtypeStruct((count, width), F32),
            jax.ShapeDtypeStruct((count, width), BF16),
            jax.ShapeDtypeStruct((count, width), F32),
        ],
        compiler_params=pltpu.CompilerParams(
            dimension_semantics=("arbitrary",), vmem_limit_bytes=VMEM_LIMIT
        ),
        name="second_norm",
    )(x, attn_sum, gain)


def back_kernel(total_ref, residual_ref, cot_ref, gain_ref, out_weight_ref, qkv_ref, weight_ref, cos_ref, sin_ref,
                row_ref, col_ref, x_ref, extra_ref, normed_grad_ref, residual_grad_ref, split_ref, projected_grad_ref, bias_ref,
                mlp_gain_ref, branch_ref, attended_grad_ref):
    head = pl.program_id(0)
    dim = cos_ref.shape[1]

    @pl.when(head == 0)
    def _():
        total = total_ref[...]
        residual = residual_ref[...]
        factor = lax.rsqrt(jnp.mean(residual * residual, axis=-1, keepdims=True) + EPS)
        scaled = gain_ref[...] * total
        inner = jnp.mean(scaled * residual, axis=-1, keepdims=True)
        residual_grad = cot_ref[...].astype(F32) + (factor * scaled - residual * factor**3 * inner)
        residual_grad_ref[...] = residual_grad
        branch_ref[...] = residual_grad.astype(BF16)
        split_columns(branch_ref, split_ref)
        mlp_gain_ref[...] = jnp.sum(total * residual * factor, axis=0, keepdims=True)
        attended_grad = nt(branch_ref[...], out_weight_ref[...]).astype(BF16)
        for k in range(attended_grad_ref.shape[0]):
            attended_grad_ref[k] = attended_grad[:, k * dim : (k + 1) * dim]

    queries, keys, values = qkv_ref[:, :dim], qkv_ref[:, dim : 2 * dim], qkv_ref[:, 2 * dim :]
    attended_grad = attended_grad_ref[head]
    probs = head_probs(queries, keys, row_ref, col_ref)
    prob_grad = nt(attended_grad, values)
    inner = jnp.sum(probs * prob_grad, axis=-1, keepdims=True)
    score = (probs * (prob_grad - inner) * dim ** (-0.5)).astype(BF16)
    query_grad = nn(score, keys).astype(BF16).astype(F32)
    key_grad = tn(score, queries).astype(BF16).astype(F32)
    value_grad = tn(probs.astype(BF16), attended_grad)
    grad = jnp.concatenate(
        [
            turned_back(query_grad, cos_ref[...], sin_ref[...]).astype(BF16),
            turned_back(key_grad, cos_ref[...], sin_ref[...]).astype(BF16),
            value_grad.astype(BF16),
        ],
        axis=1,
    )
    projected_grad_ref[...] = grad
    bias_ref[...] = jnp.sum(grad.astype(F32), axis=0, keepdims=True)
    product = nt(grad, weight_ref[...])
    groups, few = normed_grad_ref.shape[0], normed_grad_ref.shape[1] - 8

    @pl.when(head == 0)
    def _():
        for k in range(groups):
            normed_grad_ref[k, :few] = product[k * few : (k + 1) * few]

    @pl.when(head > 0)
    def _():
        for k in range(groups):
            normed_grad_ref[k, :few] += product[k * few : (k + 1) * few]

    @pl.when(head == pl.num_programs(0) - 1)
    def _():
        total = jnp.zeros((1, x_ref.shape[1]), F32)
        for k in range(groups):
            x = x_ref[k * few : (k + 1) * few].astype(F32)
            factor = lax.rsqrt(jnp.mean(x * x, axis=-1, keepdims=True) + EPS)
            total += jnp.sum(normed_grad_ref[k, :few] * x * factor, axis=0, keepdims=True)
        rows = lax.broadcasted_iota(jnp.int32, (8, x_ref.shape[1]), 0)
        small = jnp.where(rows == 0, total, jnp.where(rows == 1, extra_ref[...], 0.0))
        for k in range(groups):
            normed_grad_ref[k, few:] = small


def attention_back(total, residual, cotangent, gain, out_weight, qkv, weight, cosine, sine, row, col, x, extra,
                   groups):
    count, width = residual.shape
    dim = cosine.shape[1]
    cols = 3 * dim
    heads = qkv.shape[1] // cols
    return pl.pallas_call(
        back_kernel,
        grid=(heads,),
        in_specs=[
            whole(count, width),
            whole(count, width),
            whole(count, width),
            whole(1, width),
            whole(*out_weight.shape),
            pl.BlockSpec((count, cols), lambda h: (0, h)),
            pl.BlockSpec((width, cols), lambda h: (0, h)),
            whole(*cosine.shape),
            whole(*sine.shape),
            whole(1, count),
            whole(count, 1),
            whole(count, width),
            whole(1, width),
        ],
        out_specs=[
            whole(groups, count // groups + 8, width),
            whole(count, width),
            whole(2, count, width // 2),
            pl.BlockSpec((count, cols), lambda h: (0, h)),
            pl.BlockSpec((1, cols), lambda h: (0, h)),
            whole(1, width),
        ],
        out_shape=[
            jax.ShapeDtypeStruct((groups, count // groups + 8, width), F32),
            jax.ShapeDtypeStruct((count, width), F32),
            jax.ShapeDtypeStruct((2, count, width // 2), BF16),
            jax.ShapeDtypeStruct((count, heads * cols), BF16),
            jax.ShapeDtypeStruct((1, heads * cols), F32),
            jax.ShapeDtypeStruct((1, width), F32),
        ],
        scratch_shapes=[pltpu.VMEM((count, width), BF16), pltpu.VMEM((heads, count, dim), BF16)],
        compiler_params=pltpu.CompilerParams(
            dimension_semantics=("arbitrary",), vmem_limit_bytes=VMEM_LIMIT
        ),
        cost_estimate=LIGHT,
        name="attention_back",
    )(total, residual, cotangent, gain, out_weight, qkv, weight, cosine, sine, row, col, x, extra)


def hidden(w_one, w_two, tokens, branch, route_row):
    units = w_two.shape[0]
    mix = nt(w_one, tokens)
    gate, up = mix[:units], mix[units:]
    back = nt(w_two, branch)
    sigma = lax.logistic(gate)
    silu = gate * sigma
    act = silu * up
    scaled = back * route_row
    gate_grad = scaled * up * (sigma + silu * (1.0 - sigma))
    mix_grad = jnp.concatenate([gate_grad.astype(BF16), (scaled * silu).astype(BF16)], axis=0)
    return act, back, (act * route_row).astype(BF16), mix_grad


def open_row(gate_rows, tokens):
    return lax.logistic(nt(gate_rows, tokens)[:1])


def own_kernel(experts, tok_ref, cot_ref, route_ref, gate_ref, w1_ref, w2_ref, out_ref, dx_ref, logit_ref,
               open_ref):
    step = pl.program_id(0)
    group, units, width = w2_ref.shape
    shared = step * group >= experts

    @pl.when(step == 0)
    def _():
        for ref in (out_ref, dx_ref):
            ref[...] = jnp.zeros_like(ref)
        logit_ref[...] = jnp.zeros_like(logit_ref)
        open_ref[...] = open_row(gate_ref[...], tok_ref[...])

    weighted, mix_grads = [], []
    for k in range(group):
        act, back, scaled, mix_grad = hidden(
            w1_ref[k].reshape(2 * units, width),
            w2_ref[k],
            tok_ref[...],
            cot_ref[...],
            jnp.where(shared, open_ref[...], route_ref[k]),
        )
        weighted.append(scaled)
        mix_grads.append(mix_grad)
        logit_ref[...] += jnp.where(shared, jnp.sum(act * back, axis=0, keepdims=True), 0.0)
    out_ref[...] += tn(jnp.concatenate(weighted), w2_ref[...].reshape(group * units, width))
    dx_ref[...] += tn(jnp.concatenate(mix_grads), w1_ref[...].reshape(group * 2 * units, width))

    @pl.when(step == pl.num_programs(0) - 1)
    def _():
        opened = open_ref[...]
        logit = opened * (1.0 - opened) * logit_ref[...]
        logit_ref[...] = logit
        column = jnp.broadcast_to(logit, (8, logit.shape[1])).T[:, :1]
        dx_ref[...] += column * gate_ref[:1].astype(F32)


def own_mlp(tokens, cotangent, route, gate_rows, w1, w2):
    count, width = tokens.shape
    tiles, units = w2.shape[:2]
    experts = route.shape[0]
    group = 2
    return pl.pallas_call(
        functools.partial(own_kernel, experts),
        grid=(tiles // group,),
        in_specs=[
            whole(count, width),
            whole(count, width),
            pl.BlockSpec((group, 1, count), lambda i: (jnp.minimum(i, experts // group - 1), 0, 0)),
            whole(*gate_rows.shape),
            pl.BlockSpec((group, 2, units, width), lambda i: (i, 0, 0, 0)),
            pl.BlockSpec((group, units, width), lambda i: (i, 0, 0)),
        ],
        out_specs=[whole(count, width), whole(count, width), whole(1, count)],
        out_shape=[
            jax.ShapeDtypeStruct((count, width), F32),
            jax.ShapeDtypeStruct((count, width), F32),
            jax.ShapeDtypeStruct((1, count), F32),
        ],
        scratch_shapes=[pltpu.VMEM((1, count), F32)],
        compiler_params=pltpu.CompilerParams(
            dimension_semantics=("arbitrary",), vmem_limit_bytes=VMEM_LIMIT
        ),
        cost_estimate=LIGHT,
        name="own_mlp",
    )(tokens, cotangent, route[:, None, :], gate_rows, w1, w2)


def chip_kernel(here, at_ref, even_ref, odd_ref, cot_ref, route_ref, gate_ref, w1_ref, w2_ref, *refs):
    mix_grad_ref, weighted_ref, part_ref, tok_ref, open_ref = refs[-5:]
    step = pl.program_id(0)
    units, width = w2_ref.shape[-2:]
    cores, experts, count = route_ref.shape
    core = at_ref[0]

    @pl.when(step == 0)
    def _():
        for start, ref in ((at_ref[3], even_ref), (at_ref[4], odd_ref)):
            tok_ref[pl.ds(pl.multiple_of(start, count), count), :] = ref[...].reshape(count, width).astype(BF16)
        part = part_ref.shape[1]
        part_ref[...] = tok_ref[:, pl.ds(pl.multiple_of(at_ref[1] * part, part), part)]
        open_ref[...] = open_row(gate_ref[...], tok_ref[...])

    expert = jnp.minimum(core * here + step, experts - 1)
    route_row = jnp.concatenate([route_ref[k, pl.ds(expert, 1), :] for k in range(cores)], axis=1)
    _, _, weighted, mix_grad = hidden(
        w1_ref[...].reshape(2 * units, width),
        w2_ref[0],
        tok_ref[...],
        cot_ref[...],
        jnp.where(step >= here, open_ref[...], route_row),
    )
    mix_grad_ref[0] = mix_grad
    weighted_ref[0] = weighted


def chip_hidden(at, tokens, cotangent, route, gate_rows, w1, w2, kept, part):
    total, width = cotangent.shape
    tiles, units = w2.shape[:2]
    experts, count = route.shape[1:]
    here, shared = experts // 2, (tiles - experts) // 2
    rows = 2 * count
    own = lambda i, at: jnp.where(i < here, at[0] * here + i, experts + at[0] * shared + i - here)
    fixed = lambda *shape: pl.BlockSpec(shape, lambda i, at: (0,) * len(shape))
    if len(tokens) == 2:
        sources = [fixed(count, width), fixed(count, width)]
    else:
        tokens = [tokens[0], tokens[0]]
        sources = [
            pl.BlockSpec((1, count, width), lambda i, at: (2 * at[2], 0, 0)),
            pl.BlockSpec((1, count, width), lambda i, at: (2 * at[2] + 1, 0, 0)),
        ]
    shapes = [
        jax.ShapeDtypeStruct((here + shared, 2 * units, total), BF16),
        jax.ShapeDtypeStruct((here + shared, units, total), BF16),
        jax.ShapeDtypeStruct((total, 2 * part), BF16),
    ]
    inputs = [*tokens, cotangent, route, gate_rows, w1, w2]
    return pl.pallas_call(
        functools.partial(chip_kernel, here),
        grid_spec=pltpu.PrefetchScalarGridSpec(
            num_scalar_prefetch=1,
            grid=(here + shared,),
            in_specs=[
                *sources,
                pl.BlockSpec((rows, width), lambda i, at: (at[2], 0)),
                pl.BlockSpec((2, experts, count), lambda i, at: (at[2], 0, 0)),
                fixed(*gate_rows.shape),
                pl.BlockSpec((1, 2, units, width), lambda i, at: (own(i, at), 0, 0, 0)),
                pl.BlockSpec((1, units, width), lambda i, at: (own(i, at), 0, 0)),
                *[pl.BlockSpec(memory_space=pl.ANY) for _ in kept],
            ],
            out_specs=[
                pl.BlockSpec((1, 2 * units, rows), lambda i, at: (i, 0, at[2])),
                pl.BlockSpec((1, units, rows), lambda i, at: (i, 0, at[2])),
                pl.BlockSpec((rows, 2 * part), lambda i, at: (at[2], 0)),
            ],
            scratch_shapes=[pltpu.VMEM((rows, width), BF16), pltpu.VMEM((1, rows), F32)],
        ),
        out_shape=shapes,
        input_output_aliases={1 + len(inputs) + k: k for k in range(len(kept))},
        compiler_params=pltpu.CompilerParams(
            dimension_semantics=("arbitrary",), vmem_limit_bytes=VMEM_LIMIT
        ),
        cost_estimate=LIGHT,
        name="chip_hidden",
    )(at, *inputs, *kept)


def both_products(normed_ref, projected_ref, branch_ref, attended_ref):
    return jnp.concatenate(
        [tn(normed_ref[0], projected_ref[...]), tn(branch_ref[0], attended_ref[...])], axis=1
    )


def sent_kernel(at_ref, normed_ref, projected_ref, branch_ref, attended_ref, *out_refs):
    value = both_products(normed_ref, projected_ref, branch_ref, attended_ref)
    for block, out_ref in enumerate(out_refs):
        @pl.when(pl.program_id(0) == block)
        def _():
            out_ref[...] = value


def held_kernel(at_ref, normed_ref, projected_ref, branch_ref, attended_ref, *refs):
    block = pl.program_id(0)
    along_y, along_x = block // 2, lax.rem(block, 2)
    arrived_refs, out_refs = refs[:-4], refs[-4:]
    arrived = arrived_refs[0][...]
    for k, arrived_ref in enumerate(arrived_refs[1:], 1):
        arrived = jnp.where(block == k, arrived_ref[...], arrived)
    value = both_products(normed_ref, projected_ref, branch_ref, attended_ref) + arrived
    half = value.shape[1] // 2
    x_keep_ref, x_send_ref, y_keep_ref, y_send_ref = out_refs
    for same, index, columns, keep_ref, send_ref in (
        (along_x == at_ref[1], along_y, value[:, :half], x_keep_ref, x_send_ref),
        (along_y == at_ref[2], along_x, value[:, half:], y_keep_ref, y_send_ref),
    ):
        @pl.when(same)
        def _():
            keep_ref[index] = columns

        @pl.when(jnp.logical_not(same))
        def _():
            send_ref[index] = columns


def token_products(at, normed, projected, branch, attended, arrived):
    _, count, half = normed.shape
    blocks = BLOCKS // 2
    part = half // blocks
    cols = projected.shape[1] + attended.shape[1]
    side = pl.BlockSpec((1, count, part), lambda i, at: (at[0], 0, i))
    fixed = lambda *shape: pl.BlockSpec(shape, lambda i, at: (0,) * len(shape))
    inputs = [normed, projected, branch, attended]
    in_specs = [side, fixed(*projected.shape), side, fixed(*attended.shape)]
    if arrived is None:
        kernel, out_specs = sent_kernel, [fixed(part, cols)] * blocks
        out_shape = [jax.ShapeDtypeStruct((part, cols), F32)] * blocks
    else:
        kernel, out_specs = held_kernel, [fixed(2, part, cols // 2)] * 4
        out_shape = [jax.ShapeDtypeStruct((2, part, cols // 2), F32)] * 4
        inputs, in_specs = [*inputs, *arrived], [*in_specs, *[fixed(part, cols)] * blocks]
    return pl.pallas_call(
        kernel,
        grid_spec=pltpu.PrefetchScalarGridSpec(
            num_scalar_prefetch=1, grid=(blocks,), in_specs=in_specs, out_specs=out_specs
        ),
        out_shape=out_shape,
        compiler_params=pltpu.CompilerParams(
            dimension_semantics=("arbitrary",), vmem_limit_bytes=VMEM_LIMIT
        ),
        cost_estimate=LIGHT,
        name="token_products",
    )(at, *inputs)


def turn_kernel(at_ref, x_keep_ref, x_got_ref, y_keep_ref, y_got_ref, x_own_ref, x_send_ref, y_own_ref, y_send_ref):
    for mine, keep_ref, got_ref, own_ref, send_ref in (
        (at_ref[2], x_keep_ref, x_got_ref, x_own_ref, x_send_ref),
        (at_ref[1], y_keep_ref, y_got_ref, y_own_ref, y_send_ref),
    ):
        own_ref[...] = keep_ref[mine] + got_ref[mine]
        send_ref[...] = keep_ref[1 - mine] + got_ref[1 - mine]


def turned_blocks(at, x_keep, x_got, y_keep, y_got):
    _, part, cols = x_keep.shape
    rows = part // 4
    spec = pl.BlockSpec((2, rows, cols), lambda i, at: (0, i, 0))
    out = pl.BlockSpec((rows, cols), lambda i, at: (i, 0))
    return pl.pallas_call(
        turn_kernel,
        grid_spec=pltpu.PrefetchScalarGridSpec(
            num_scalar_prefetch=1, grid=(4,), in_specs=[spec] * 4, out_specs=[out] * 4
        ),
        out_shape=[jax.ShapeDtypeStruct((part, cols), F32)] * 4,
        compiler_params=pltpu.CompilerParams(
            dimension_semantics=("arbitrary",), vmem_limit_bytes=VMEM_LIMIT
        ),
        cost_estimate=LIGHT,
        name="turned_blocks",
    )(at, x_keep, x_got, y_keep, y_got)


def weights_kernel(here, at_ref, mix_grad_ref, weighted_ref, tok_ref, cot_ref, *refs):
    part = refs[0].shape[-1]
    expert_refs, shared_refs, peer_refs = refs[:2], refs[2:4], refs[4:]
    core, step = at_ref[0], pl.program_id(0)
    products = nn(mix_grad_ref[0], tok_ref[...]), nn(weighted_ref[0], cot_ref[...])
    for value, expert_ref, shared_ref, peer_ref in zip(products, expert_refs, shared_refs, peer_refs, strict=True):
        low, high = value[:, :part], value[:, part:]
        mine = jnp.where(core == 0, low, high)
        peer_ref[...] = jnp.where(core == 0, high, low).reshape(peer_ref.shape)

        @pl.when(step < here)
        def _():
            expert_ref[...] = mine.reshape(expert_ref.shape)

        @pl.when(step >= here)
        def _():
            shared_ref[...] = mine.reshape(shared_ref.shape)


def tile_specs(core_of, here, shared, units, part):
    expert = lambda i, at: core_of(at) * here + jnp.minimum(i, here - 1)
    common = lambda i, at: core_of(at) * shared + jnp.maximum(i - here, 0)
    return [
        pl.BlockSpec((1, 2, units, part), lambda i, at: (expert(i, at), 0, 0, 0)),
        pl.BlockSpec((1, units, part), lambda i, at: (expert(i, at), 0, 0)),
        pl.BlockSpec((1, 2, units, part), lambda i, at: (common(i, at), 0, 0, 0)),
        pl.BlockSpec((1, units, part), lambda i, at: (common(i, at), 0, 0)),
    ]


def weight_grads(at, mix_grads, weighted, tokens, cotangent, here):
    tiles, units, total = weighted.shape
    part = tokens.shape[1] // 2
    shared = tiles - here
    one = lambda count: jax.ShapeDtypeStruct((count, 2, units, part), F32)
    two = lambda count: jax.ShapeDtypeStruct((count, units, part), F32)
    return pl.pallas_call(
        functools.partial(weights_kernel, here),
        grid_spec=pltpu.PrefetchScalarGridSpec(
            num_scalar_prefetch=1,
            grid=(tiles,),
            in_specs=[
                pl.BlockSpec((1, 2 * units, total), lambda i, at: (i, 0, 0)),
                pl.BlockSpec((1, units, total), lambda i, at: (i, 0, 0)),
                pl.BlockSpec((total, 2 * part), lambda i, at: (0, 0)),
                pl.BlockSpec((total, 2 * part), lambda i, at: (0, at[3])),
            ],
            out_specs=[
                *tile_specs(lambda at: at[0], here, shared, units, part),
                pl.BlockSpec((1, 2, units, part), lambda i, at: (i, 0, 0, 0)),
                pl.BlockSpec((1, units, part), lambda i, at: (i, 0, 0)),
            ],
        ),
        out_shape=[one(2 * here), two(2 * here), one(2 * shared), two(2 * shared), one(tiles), two(tiles)],
        compiler_params=pltpu.CompilerParams(
            dimension_semantics=("arbitrary",), vmem_limit_bytes=VMEM_LIMIT
        ),
        cost_estimate=LIGHT,
        name="weight_grads",
    )(at, mix_grads, weighted, tokens, cotangent)


def place_kernel(here, at_ref, one_ref, two_ref, *refs):
    step = pl.program_id(0)
    expert_one_ref, expert_two_ref, shared_one_ref, shared_two_ref = refs[-4:]

    @pl.when(step < here)
    def _():
        expert_one_ref[...] = one_ref[...]
        expert_two_ref[...] = two_ref[...]

    @pl.when(step >= here)
    def _():
        shared_one_ref[...] = one_ref[...]
        shared_two_ref[...] = two_ref[...]


def place_peer(at, one, two, grads, here):
    tiles, units, part = two.shape
    return pl.pallas_call(
        functools.partial(place_kernel, here),
        grid_spec=pltpu.PrefetchScalarGridSpec(
            num_scalar_prefetch=1,
            grid=(tiles,),
            in_specs=[
                pl.BlockSpec((1, 2, units, part), lambda i, at: (i, 0, 0, 0)),
                pl.BlockSpec((1, units, part), lambda i, at: (i, 0, 0)),
                *[pl.BlockSpec(memory_space=pl.ANY)] * 4,
            ],
            out_specs=tile_specs(lambda at: 1 - at[0], here, tiles - here, units, part),
        ),
        out_shape=[jax.ShapeDtypeStruct(g.shape, g.dtype) for g in grads],
        input_output_aliases={3 + k: k for k in range(4)},
        compiler_params=pltpu.CompilerParams(
            dimension_semantics=("arbitrary",), vmem_limit_bytes=VMEM_LIMIT
        ),
        cost_estimate=LIGHT,
        name="place_peer",
    )(at, one, two, *grads)


def split_kernel(in_ref, out_ref, route_ref):
    count = out_ref.shape[0]
    out_ref[...] = in_ref[0, :count].astype(BF16)
    route_ref[...] = in_ref[0, count:, :count][None]


def split_rounded(gathered, count):
    blocks, rows, width = gathered.shape
    extra = rows - count
    return pl.pallas_call(
        split_kernel,
        grid=(blocks,),
        in_specs=[pl.BlockSpec((1, rows, width), lambda i: (i, 0, 0))],
        out_specs=[
            pl.BlockSpec((count, width), lambda i: (i, 0)),
            pl.BlockSpec((1, extra, count), lambda i: (i, 0, 0)),
        ],
        out_shape=[
            jax.ShapeDtypeStruct((blocks * count, width), BF16),
            jax.ShapeDtypeStruct((blocks, extra, count), F32),
        ],
        compiler_params=pltpu.CompilerParams(
            dimension_semantics=("arbitrary",), vmem_limit_bytes=VMEM_LIMIT
        ),
        name="split_rounded",
    )(gathered)


def flip(value, bit):
    return lax.ppermute(value, "dp", [(i, i ^ bit) for i in range(8)])


def take(value, number, axis):
    return lax.dynamic_index_in_dim(value, number, axis, keepdims=False)


def shards(
    n_dp,
    n_tensor,
    layer_input,
    doc_ids,
    expert_ids,
    route_weights,
    attn_gain,
    qkv_weight,
    qkv_bias,
    out_weight,
    mlp_gain,
    expert_gate_up,
    expert_down,
    shared_gate_up,
    shared_down,
    shared_gate,
    cotangent,
):
    count, width = layer_input.shape
    heads_here = qkv_bias.shape[0]
    head_dim = qkv_bias.shape[1] // 3
    experts, units = expert_down.shape[:2]
    shared = shared_down.shape[0] // units
    part = width // n_dp
    me = lax.axis_index("dp")
    core, chip = me % 2, me // 2
    tied = lax.optimization_barrier

    choose = expert_ids[:, :, None] == jnp.arange(experts, dtype=jnp.int32)[None, None, :]
    route = jnp.sum(route_weights[:, :, None] * choose.astype(F32), axis=1).T
    payload = jnp.concatenate([cotangent.astype(F32), jnp.pad(route, ((0, 0), (0, width - count)))], axis=0)
    cot_all = lax.all_gather(payload, "dp")
    gate_rows = jnp.broadcast_to(shared_gate[None, :], (16, width))
    index = jnp.arange(count, dtype=jnp.int32)
    place = (me * count + index - doc_ids).astype(F32)
    freq = ROPE_BASE ** (-(jnp.arange(head_dim // 2, dtype=F32) * 2.0 / head_dim))
    angle = place[:, None] * freq[None, :]
    cosine = jnp.concatenate([jnp.cos(angle), jnp.cos(angle)], axis=-1)
    sine = jnp.concatenate([-jnp.sin(angle), jnp.sin(angle)], axis=-1)
    row, col = doc_ids[None, :], doc_ids[:, None]
    gain_one = attn_gain.astype(F32)[None, :]
    gain_two = mlp_gain.astype(F32)[None, :]
    attn_part, normed_one, qkv, attended = attention(
        layer_input, gain_one, qkv_weight, qkv_bias.astype(F32)[:, None, :], cosine, sine, row, col, out_weight
    )

    attn_part, shared_gate_up = tied((attn_part, shared_gate_up))
    attn_sum = lax.psum(attn_part, "tensor")
    w1 = jnp.concatenate(
        [
            jnp.transpose(expert_gate_up, (0, 2, 3, 1)),
            jnp.transpose(shared_gate_up.reshape(width, 2, shared, units), (2, 1, 3, 0)),
        ]
    )
    w2 = jnp.concatenate([expert_down, shared_down.reshape(shared, units, width)])
    w1, cot_all = tied((w1, cot_all))
    attn_sum, w1, w2, cot_all = tied((attn_sum, w1, w2, cot_all))

    residual, tokens, tokens_wide = second_norm(layer_input, attn_sum, gain_two)
    swap = lambda v: lax.ppermute(v, "dp", [(i, i ^ 1) for i in range(n_dp)])
    beside = swap(tokens_wide)
    tok_all = lax.all_gather(tokens_wide, "dp")
    mlp_part, normed_two_part, logit_grad = own_mlp(tokens, cotangent, route, gate_rows, w1, w2)
    cot_all, logit_grad = tied((cot_all, logit_grad))
    cot_low, route_all = split_rounded(cot_all, count)
    hide = lambda other, starts, tokens, kept: chip_hidden(
        jnp.stack([core, chip, other, *starts]), tokens, cot_low, route_all, gate_rows, w1, w2, kept, part
    )
    in_order = (jnp.int32(0), jnp.int32(count))
    beside_starts = (core * count, (1 - core) * count)
    shared_gate_part = jnp.sum(logit_grad[0][:, None] * tokens.astype(F32), axis=0, keepdims=True)
    normed_two_total = lax.psum(normed_two_part, "tensor")
    last = n_dp == 8
    if last:
        ready = jnp.isnan(logit_grad[0, 0]).astype(jnp.int32)
        kept = hide(chip + ready, beside_starts, [tokens_wide, beside], [])
        kept = hide(chip ^ 1, in_order, [tok_all], kept)
        kept = hide(chip ^ 2, in_order, [tok_all], kept)
    else:
        kept = []
        for k in range(n_dp // 2):
            kept = hide(jnp.int32(k), in_order, [tok_all], kept)
    normed_two_total, shared_gate_part, kept = tied((normed_two_total, shared_gate_part, kept))
    mlp_sum = lax.psum_scatter(mlp_part, "tensor", scatter_dimension=0, tiled=True)

    normed_one_part, residual_grad, branch_grad, projected_grad, bias_part, mlp_gain_part = attention_back(
        normed_two_total, residual, cotangent, gain_two, out_weight, qkv, qkv_weight,
        cosine, sine, row, col, layer_input, shared_gate_part, 1,
    )
    summed = lax.psum(normed_one_part.reshape(-1, width), "tensor")

    def finish(summed):
        inputs = layer_input.astype(F32)
        factor = lax.rsqrt(jnp.mean(inputs * inputs, axis=-1, keepdims=True) + EPS)
        bias_row = jnp.pad(bias_part, ((0, 0), (0, width - bias_part.shape[1])))
        small = jnp.concatenate([summed[count : count + 2], mlp_gain_part, bias_row])
        input_grad = (residual_grad + norm_back(inputs, factor, gain_one, summed[:count])).astype(BF16)
        return input_grad, jnp.pad(small, ((0, 4), (0, 0)))

    if last:
        at = jnp.stack([core, chip % 2, chip // 2, chip])
        other_at = jnp.stack([1 - core, chip % 2, chip // 2, chip])
        arrived = [swap(v) for v in token_products(other_at, normed_one, projected_grad, branch_grad, attended, None)]
        x_keep, x_send, y_keep, y_send = token_products(
            at, normed_one, projected_grad, branch_grad, attended, arrived
        )
        x_send, y_send, kept, mlp_sum = tied((x_send, y_send, kept, mlp_sum))
        x_got, y_got = flip(x_send, 2), flip(y_send, 4)
        kept = hide(chip ^ 3, in_order, [tok_all], kept)
        *grads, one_peer, two_peer = weight_grads(at, *kept, cot_low, experts // 2)
        one_peer, x_got, y_got, mlp_sum = tied((one_peer, x_got, y_got, mlp_sum))
        mlp_sum = lax.all_gather(mlp_sum, "tensor", axis=0, tiled=True)
        x_own, x_send, y_own, y_send = turned_blocks(at, x_keep, x_got, y_keep, y_got)
        x_send, y_send, one_peer, two_peer, summed = tied((x_send, y_send, one_peer, two_peer, summed))
        x_got, y_got = flip(x_send, 4), flip(y_send, 2)
        one_peer, two_peer = swap(one_peer), swap(two_peer)
        summed, one_peer, two_peer = tied((summed, one_peer, two_peer))
        expert_one, expert_two, shared_one, shared_two = place_peer(at, one_peer, two_peer, grads, experts // 2)
        expert_one, summed = tied((expert_one, summed))
        input_grad, small = finish(summed)
        for bit in (1, 2, 4):
            small = small + flip(small, bit)
        x_got, y_got, input_grad, small, expert_one = tied((x_got, y_got, input_grad, small, expert_one))
        both = jnp.concatenate([x_own + x_got, y_own + y_got], axis=1)
        cut = projected_grad.shape[1]
        qkv_weight_grad, out_weight_grad = both[:, :cut], both[:, cut:].T
        mlp_sum, qkv_weight_grad = tied((mlp_sum, qkv_weight_grad))
    else:
        at = jnp.stack([core, core, core, chip])
        *grads, one_peer, two_peer = weight_grads(at, *kept, cot_low, experts // 2)
        one_peer, two_peer = swap(one_peer), swap(two_peer)
        expert_one, expert_two, shared_one, shared_two = place_peer(at, one_peer, two_peer, grads, experts // 2)
        input_grad, small = finish(summed)
        small = lax.psum(small, "dp")
        mlp_sum = lax.all_gather(mlp_sum, "tensor", axis=0, tiled=True)
        joint = lambda v: v.reshape(2, count, BLOCKS // 2, -1).transpose(1, 2, 0, 3).reshape(count, width)
        out_weight_grad = lax.psum_scatter(tn(attended, joint(branch_grad)), "dp", scatter_dimension=1, tiled=True)
        qkv_weight_grad = lax.psum_scatter(
            tn(joint(normed_one), projected_grad), "dp", scatter_dimension=0, tiled=True
        )

    attn_gain_grad, shared_gate_grad, mlp_gain_grad = lax.dynamic_slice(small, (0, me * part), (3, part))
    bias_cols = 3 * head_dim // n_dp
    bias = small[3, : heads_here * 3 * head_dim].reshape(heads_here, 3 * head_dim)
    qkv_bias_grad = lax.dynamic_slice(bias, (0, me * bias_cols), (heads_here, bias_cols))
    layer_output = (residual + mlp_sum).astype(BF16)

    expert_gate_up_grad = jnp.transpose(expert_one, (0, 3, 1, 2))
    shared_gate_up_grad = jnp.transpose(shared_one, (3, 1, 0, 2)).reshape(part, 2, shared * units)
    shared_down_grad = shared_two.reshape(shared * units, part)
    return (
        layer_output,
        input_grad,
        attn_gain_grad,
        qkv_weight_grad,
        qkv_bias_grad,
        out_weight_grad,
        mlp_gain_grad,
        expert_gate_up_grad,
        expert_two,
        shared_gate_up_grad,
        shared_down_grad,
        shared_gate_grad,
    )


def solution(mesh):
    placed = (
        P("dp", None),
        P("dp"),
        P("dp", None),
        P("dp", None),
        P(),
        P(None, "tensor"),
        P("tensor", None),
        P("tensor", None),
        P(),
        P(None, None, None, "tensor"),
        P(None, "tensor", None),
        P(None, None, "tensor"),
        P("tensor", None),
        P(),
        P("dp", None),
    )
    return jax.shard_map(
        functools.partial(shards, mesh.shape["dp"], mesh.shape["tensor"]),
        mesh=mesh,
        in_specs=placed,
        out_specs=(
            P("dp", None),
            P("dp", None),
            P("dp"),
            P("dp", "tensor"),
            P("tensor", "dp"),
            P("tensor", "dp"),
            P("dp"),
            P(None, "dp", None, "tensor"),
            P(None, "tensor", "dp"),
            P("dp", None, "tensor"),
            P("tensor", "dp"),
            P("dp"),
        ),
        check_vma=False,
    )
```

```python
import functools

import jax
import jax.numpy as jnp
from jax import lax
from jax.experimental import pallas as pl
from jax.experimental.pallas import tpu as pltpu
from jax.sharding import PartitionSpec as P

EPS = 1e-06
ROPE_BASE = 1000000.0
NEG = -1e30
F32 = jnp.float32
BF16 = jnp.bfloat16
VMEM_LIMIT = 60 * 1024 * 1024
BLOCKS = 8
LIGHT = pl.CostEstimate(flops=1 << 20, bytes_accessed=1 << 16, transcendentals=0)


def nt(left, right):
    return lax.dot_general(left, right, (((1,), (1,)), ((), ())), preferred_element_type=F32)


def tn(left, right):
    return lax.dot_general(left, right, (((0,), (0,)), ((), ())), preferred_element_type=F32)


def nn(left, right):
    return jnp.dot(left, right, preferred_element_type=F32)


def norm_back(values_in, factor, gain_vec, upstream):
    scaled = gain_vec * upstream
    inner = jnp.mean(scaled * values_in, axis=-1, keepdims=True)
    return factor * scaled - values_in * factor**3 * inner


def turned(values, cosine, sine):
    return values * cosine + pltpu.roll(values, values.shape[1] // 2, 1) * sine


def turned_back(values, cosine, sine):
    return values * cosine - pltpu.roll(values, values.shape[1] // 2, 1) * sine


def head_probs(queries, keys, row_ref, col_ref):
    count = queries.shape[0]
    scores = nt(queries, keys) * queries.shape[1] ** (-0.5)
    rows = lax.broadcasted_iota(jnp.int32, (count, count), 0)
    cols = lax.broadcasted_iota(jnp.int32, (count, count), 1)
    scores = jnp.where((col_ref[...] == row_ref[...]) & (cols <= rows), scores, NEG)
    exponent = jnp.exp(scores - jnp.max(scores, axis=-1, keepdims=True))
    return exponent / jnp.sum(exponent, axis=-1, keepdims=True)


def split_columns(whole_ref, split_ref):
    part = whole_ref.shape[1] // BLOCKS
    for k in range(BLOCKS):
        split_ref[k % 2, :, k // 2 * part : (k // 2 + 1) * part] = whole_ref[:, k * part : (k + 1) * part]


def attn_kernel(x_ref, gain_ref, weight_ref, bias_ref, cos_ref, sin_ref, row_ref, col_ref, out_weight_ref,
                part_ref, split_ref, qkv_ref, attended_ref, normed_ref):
    head = pl.program_id(0)
    dim = cos_ref.shape[1]

    @pl.when(head == 0)
    def _():
        values = x_ref[...].astype(F32)
        factor = lax.rsqrt(jnp.mean(values * values, axis=-1, keepdims=True) + EPS)
        normed_ref[...] = (values * factor * gain_ref[...]).astype(BF16)
        split_columns(normed_ref, split_ref)

    projected = nn(normed_ref[...], weight_ref[...]) + bias_ref[0]
    queries = turned(projected[:, :dim], cos_ref[...], sin_ref[...]).astype(BF16)
    keys = turned(projected[:, dim : 2 * dim], cos_ref[...], sin_ref[...]).astype(BF16)
    values = projected[:, 2 * dim :].astype(BF16)
    qkv_ref[:, :dim] = queries
    qkv_ref[:, dim : 2 * dim] = keys
    qkv_ref[:, 2 * dim :] = values
    probs = head_probs(queries, keys, row_ref, col_ref)
    cols = pl.ds(pl.multiple_of(head * dim, dim), dim)
    attended_ref[:, cols] = nn(probs.astype(BF16), values).astype(BF16)

    @pl.when(head == pl.num_programs(0) - 1)
    def _():
        part_ref[...] = nn(attended_ref[...], out_weight_ref[...])


def whole(*shape):
    return pl.BlockSpec(shape, lambda *at: (0,) * len(shape))


def attention(x, gain, weight, bias, cosine, sine, row, col, out_weight):
    count, width = x.shape
    heads, _, cols = bias.shape
    return pl.pallas_call(
        attn_kernel,
        grid=(heads,),
        in_specs=[
            whole(count, width),
            whole(1, width),
            pl.BlockSpec((width, cols), lambda h: (0, h)),
            pl.BlockSpec((1, 1, cols), lambda h: (h, 0, 0)),
            whole(*cosine.shape),
            whole(*sine.shape),
            whole(1, count),
            whole(count, 1),
            whole(*out_weight.shape),
        ],
        out_specs=[
            whole(count, width),
            whole(2, count, width // 2),
            pl.BlockSpec((count, cols), lambda h: (0, h)),
            whole(count, out_weight.shape[0]),
        ],
        out_shape=[
            jax.ShapeDtypeStruct((count, width), F32),
            jax.ShapeDtypeStruct((2, count, width // 2), BF16),
            jax.ShapeDtypeStruct((count, heads * cols), BF16),
            jax.ShapeDtypeStruct((count, out_weight.shape[0]), BF16),
        ],
        scratch_shapes=[pltpu.VMEM((count, width), BF16)],
        compiler_params=pltpu.CompilerParams(
            dimension_semantics=("arbitrary",), vmem_limit_bytes=VMEM_LIMIT
        ),
        cost_estimate=LIGHT,
        name="attention",
    )(x, gain, weight, bias, cosine, sine, row, col, out_weight)


def norm_kernel(x_ref, sum_ref, gain_ref, residual_ref, low_ref, wide_ref):
    residual = x_ref[...].astype(F32) + sum_ref[...]
    factor = lax.rsqrt(jnp.mean(residual * residual, axis=-1, keepdims=True) + EPS)
    low = (residual * factor * gain_ref[...]).astype(BF16)
    residual_ref[...] = residual
    low_ref[...] = low
    wide_ref[...] = low.astype(F32)


def second_norm(x, attn_sum, gain):
    count, width = x.shape
    rows = count // 4
    spec = pl.BlockSpec((rows, width), lambda i: (i, 0))
    return pl.pallas_call(
        norm_kernel,
        grid=(4,),
        in_specs=[spec, spec, whole(1, width)],
        out_specs=[spec, spec, spec],
        out_shape=[
            jax.ShapeDtypeStruct((count, width), F32),
            jax.ShapeDtypeStruct((count, width), BF16),
            jax.ShapeDtypeStruct((count, width), F32),
        ],
        compiler_params=pltpu.CompilerParams(
            dimension_semantics=("arbitrary",), vmem_limit_bytes=VMEM_LIMIT
        ),
        name="second_norm",
    )(x, attn_sum, gain)


def back_kernel(total_ref, residual_ref, cot_ref, gain_ref, out_weight_ref, qkv_ref, weight_ref, cos_ref, sin_ref,
                row_ref, col_ref, x_ref, extra_ref, normed_grad_ref, residual_grad_ref, split_ref, projected_grad_ref, bias_ref,
                mlp_gain_ref, branch_ref, attended_grad_ref):
    head = pl.program_id(0)
    dim = cos_ref.shape[1]

    @pl.when(head == 0)
    def _():
        total = total_ref[...]
        residual = residual_ref[...]
        factor = lax.rsqrt(jnp.mean(residual * residual, axis=-1, keepdims=True) + EPS)
        scaled = gain_ref[...] * total
        inner = jnp.mean(scaled * residual, axis=-1, keepdims=True)
        residual_grad = cot_ref[...].astype(F32) + (factor * scaled - residual * factor**3 * inner)
        residual_grad_ref[...] = residual_grad
        branch_ref[...] = residual_grad.astype(BF16)
        split_columns(branch_ref, split_ref)
        mlp_gain_ref[...] = jnp.sum(total * residual * factor, axis=0, keepdims=True)
        attended_grad = nt(branch_ref[...], out_weight_ref[...]).astype(BF16)
        for k in range(attended_grad_ref.shape[0]):
            attended_grad_ref[k] = attended_grad[:, k * dim : (k + 1) * dim]

    queries, keys, values = qkv_ref[:, :dim], qkv_ref[:, dim : 2 * dim], qkv_ref[:, 2 * dim :]
    attended_grad = attended_grad_ref[head]
    probs = head_probs(queries, keys, row_ref, col_ref)
    prob_grad = nt(attended_grad, values)
    inner = jnp.sum(probs * prob_grad, axis=-1, keepdims=True)
    score = (probs * (prob_grad - inner) * dim ** (-0.5)).astype(BF16)
    query_grad = nn(score, keys).astype(BF16).astype(F32)
    key_grad = tn(score, queries).astype(BF16).astype(F32)
    value_grad = tn(probs.astype(BF16), attended_grad)
    grad = jnp.concatenate(
        [
            turned_back(query_grad, cos_ref[...], sin_ref[...]).astype(BF16),
            turned_back(key_grad, cos_ref[...], sin_ref[...]).astype(BF16),
            value_grad.astype(BF16),
        ],
        axis=1,
    )
    projected_grad_ref[...] = grad
    bias_ref[...] = jnp.sum(grad.astype(F32), axis=0, keepdims=True)
    product = nt(grad, weight_ref[...])
    groups, few = normed_grad_ref.shape[0], normed_grad_ref.shape[1] - 8

    @pl.when(head == 0)
    def _():
        for k in range(groups):
            normed_grad_ref[k, :few] = product[k * few : (k + 1) * few]

    @pl.when(head > 0)
    def _():
        for k in range(groups):
            normed_grad_ref[k, :few] += product[k * few : (k + 1) * few]

    @pl.when(head == pl.num_programs(0) - 1)
    def _():
        total = jnp.zeros((1, x_ref.shape[1]), F32)
        for k in range(groups):
            x = x_ref[k * few : (k + 1) * few].astype(F32)
            factor = lax.rsqrt(jnp.mean(x * x, axis=-1, keepdims=True) + EPS)
            total += jnp.sum(normed_grad_ref[k, :few] * x * factor, axis=0, keepdims=True)
        rows = lax.broadcasted_iota(jnp.int32, (8, x_ref.shape[1]), 0)
        small = jnp.where(rows == 0, total, jnp.where(rows == 1, extra_ref[...], 0.0))
        for k in range(groups):
            normed_grad_ref[k, few:] = small


def attention_back(total, residual, cotangent, gain, out_weight, qkv, weight, cosine, sine, row, col, x, extra,
                   groups):
    count, width = residual.shape
    dim = cosine.shape[1]
    cols = 3 * dim
    heads = qkv.shape[1] // cols
    return pl.pallas_call(
        back_kernel,
        grid=(heads,),
        in_specs=[
            whole(count, width),
            whole(count, width),
            whole(count, width),
            whole(1, width),
            whole(*out_weight.shape),
            pl.BlockSpec((count, cols), lambda h: (0, h)),
            pl.BlockSpec((width, cols), lambda h: (0, h)),
            whole(*cosine.shape),
            whole(*sine.shape),
            whole(1, count),
            whole(count, 1),
            whole(count, width),
            whole(1, width),
        ],
        out_specs=[
            whole(groups, count // groups + 8, width),
            whole(count, width),
            whole(2, count, width // 2),
            pl.BlockSpec((count, cols), lambda h: (0, h)),
            pl.BlockSpec((1, cols), lambda h: (0, h)),
            whole(1, width),
        ],
        out_shape=[
            jax.ShapeDtypeStruct((groups, count // groups + 8, width), F32),
            jax.ShapeDtypeStruct((count, width), F32),
            jax.ShapeDtypeStruct((2, count, width // 2), BF16),
            jax.ShapeDtypeStruct((count, heads * cols), BF16),
            jax.ShapeDtypeStruct((1, heads * cols), F32),
            jax.ShapeDtypeStruct((1, width), F32),
        ],
        scratch_shapes=[pltpu.VMEM((count, width), BF16), pltpu.VMEM((heads, count, dim), BF16)],
        compiler_params=pltpu.CompilerParams(
            dimension_semantics=("arbitrary",), vmem_limit_bytes=VMEM_LIMIT
        ),
        cost_estimate=LIGHT,
        name="attention_back",
    )(total, residual, cotangent, gain, out_weight, qkv, weight, cosine, sine, row, col, x, extra)


def hidden(w_one, w_two, tokens, branch, route_row):
    units = w_two.shape[0]
    mix = nt(w_one, tokens)
    gate, up = mix[:units], mix[units:]
    back = nt(w_two, branch)
    sigma = lax.logistic(gate)
    silu = gate * sigma
    act = silu * up
    scaled = back * route_row
    gate_grad = scaled * up * (sigma + silu * (1.0 - sigma))
    mix_grad = jnp.concatenate([gate_grad.astype(BF16), (scaled * silu).astype(BF16)], axis=0)
    return act, back, (act * route_row).astype(BF16), mix_grad


def open_row(gate_rows, tokens):
    return lax.logistic(nt(gate_rows, tokens)[:1])


def own_kernel(experts, tok_ref, cot_ref, route_ref, gate_ref, w1_ref, w2_ref, out_ref, dx_ref, logit_ref,
               open_ref):
    step = pl.program_id(0)
    group, units, width = w2_ref.shape
    shared = step * group >= experts

    @pl.when(step == 0)
    def _():
        for ref in (out_ref, dx_ref):
            ref[...] = jnp.zeros_like(ref)
        logit_ref[...] = jnp.zeros_like(logit_ref)
        open_ref[...] = open_row(gate_ref[...], tok_ref[...])

    weighted, mix_grads = [], []
    for k in range(group):
        act, back, scaled, mix_grad = hidden(
            w1_ref[k].reshape(2 * units, width),
            w2_ref[k],
            tok_ref[...],
            cot_ref[...],
            jnp.where(shared, open_ref[...], route_ref[k]),
        )
        weighted.append(scaled)
        mix_grads.append(mix_grad)
        logit_ref[...] += jnp.where(shared, jnp.sum(act * back, axis=0, keepdims=True), 0.0)
    out_ref[...] += tn(jnp.concatenate(weighted), w2_ref[...].reshape(group * units, width))
    dx_ref[...] += tn(jnp.concatenate(mix_grads), w1_ref[...].reshape(group * 2 * units, width))

    @pl.when(step == pl.num_programs(0) - 1)
    def _():
        opened = open_ref[...]
        logit = opened * (1.0 - opened) * logit_ref[...]
        logit_ref[...] = logit
        column = jnp.broadcast_to(logit, (8, logit.shape[1])).T[:, :1]
        dx_ref[...] += column * gate_ref[:1].astype(F32)


def own_mlp(tokens, cotangent, route, gate_rows, w1, w2):
    count, width = tokens.shape
    tiles, units = w2.shape[:2]
    experts = route.shape[0]
    group = 2
    return pl.pallas_call(
        functools.partial(own_kernel, experts),
        grid=(tiles // group,),
        in_specs=[
            whole(count, width),
            whole(count, width),
            pl.BlockSpec((group, 1, count), lambda i: (jnp.minimum(i, experts // group - 1), 0, 0)),
            whole(*gate_rows.shape),
            pl.BlockSpec((group, 2, units, width), lambda i: (i, 0, 0, 0)),
            pl.BlockSpec((group, units, width), lambda i: (i, 0, 0)),
        ],
        out_specs=[whole(count, width), whole(count, width), whole(1, count)],
        out_shape=[
            jax.ShapeDtypeStruct((count, width), F32),
            jax.ShapeDtypeStruct((count, width), F32),
            jax.ShapeDtypeStruct((1, count), F32),
        ],
        scratch_shapes=[pltpu.VMEM((1, count), F32)],
        compiler_params=pltpu.CompilerParams(
            dimension_semantics=("arbitrary",), vmem_limit_bytes=VMEM_LIMIT
        ),
        cost_estimate=LIGHT,
        name="own_mlp",
    )(tokens, cotangent, route[:, None, :], gate_rows, w1, w2)


def chip_kernel(here, at_ref, even_ref, odd_ref, cot_ref, route_ref, gate_ref, w1_ref, w2_ref, *refs):
    mix_grad_ref, weighted_ref, part_ref, tok_ref, open_ref = refs[-5:]
    step = pl.program_id(0)
    units, width = w2_ref.shape[-2:]
    cores, experts, count = route_ref.shape
    core = at_ref[0]

    @pl.when(step == 0)
    def _():
        for start, ref in ((at_ref[3], even_ref), (at_ref[4], odd_ref)):
            tok_ref[pl.ds(pl.multiple_of(start, count), count), :] = ref[...].reshape(count, width).astype(BF16)
        part = part_ref.shape[1]
        part_ref[...] = tok_ref[:, pl.ds(pl.multiple_of(at_ref[1] * part, part), part)]
        open_ref[...] = open_row(gate_ref[...], tok_ref[...])

    expert = jnp.minimum(core * here + step, experts - 1)
    route_row = jnp.concatenate([route_ref[k, pl.ds(expert, 1), :] for k in range(cores)], axis=1)
    _, _, weighted, mix_grad = hidden(
        w1_ref[...].reshape(2 * units, width),
        w2_ref[0],
        tok_ref[...],
        cot_ref[...],
        jnp.where(step >= here, open_ref[...], route_row),
    )
    mix_grad_ref[0] = mix_grad
    weighted_ref[0] = weighted


def chip_hidden(at, tokens, cotangent, route, gate_rows, w1, w2, kept, part):
    total, width = cotangent.shape
    tiles, units = w2.shape[:2]
    experts, count = route.shape[1:]
    here, shared = experts // 2, (tiles - experts) // 2
    rows = 2 * count
    own = lambda i, at: jnp.where(i < here, at[0] * here + i, experts + at[0] * shared + i - here)
    fixed = lambda *shape: pl.BlockSpec(shape, lambda i, at: (0,) * len(shape))
    if len(tokens) == 2:
        sources = [fixed(count, width), fixed(count, width)]
    else:
        tokens = [tokens[0], tokens[0]]
        sources = [
            pl.BlockSpec((1, count, width), lambda i, at: (2 * at[2], 0, 0)),
            pl.BlockSpec((1, count, width), lambda i, at: (2 * at[2] + 1, 0, 0)),
        ]
    shapes = [
        jax.ShapeDtypeStruct((here + shared, 2 * units, total), BF16),
        jax.ShapeDtypeStruct((here + shared, units, total), BF16),
        jax.ShapeDtypeStruct((total, 2 * part), BF16),
    ]
    inputs = [*tokens, cotangent, route, gate_rows, w1, w2]
    return pl.pallas_call(
        functools.partial(chip_kernel, here),
        grid_spec=pltpu.PrefetchScalarGridSpec(
            num_scalar_prefetch=1,
            grid=(here + shared,),
            in_specs=[
                *sources,
                pl.BlockSpec((rows, width), lambda i, at: (at[2], 0)),
                pl.BlockSpec((2, experts, count), lambda i, at: (at[2], 0, 0)),
                fixed(*gate_rows.shape),
                pl.BlockSpec((1, 2, units, width), lambda i, at: (own(i, at), 0, 0, 0)),
                pl.BlockSpec((1, units, width), lambda i, at: (own(i, at), 0, 0)),
                *[pl.BlockSpec(memory_space=pl.ANY) for _ in kept],
            ],
            out_specs=[
                pl.BlockSpec((1, 2 * units, rows), lambda i, at: (i, 0, at[2])),
                pl.BlockSpec((1, units, rows), lambda i, at: (i, 0, at[2])),
                pl.BlockSpec((rows, 2 * part), lambda i, at: (at[2], 0)),
            ],
            scratch_shapes=[pltpu.VMEM((rows, width), BF16), pltpu.VMEM((1, rows), F32)],
        ),
        out_shape=shapes,
        input_output_aliases={1 + len(inputs) + k: k for k in range(len(kept))},
        compiler_params=pltpu.CompilerParams(
            dimension_semantics=("arbitrary",), vmem_limit_bytes=VMEM_LIMIT
        ),
        cost_estimate=LIGHT,
        name="chip_hidden",
    )(at, *inputs, *kept)


def both_products(normed_ref, projected_ref, branch_ref, attended_ref):
    return jnp.concatenate(
        [tn(normed_ref[0], projected_ref[...]), tn(branch_ref[0], attended_ref[...])], axis=1
    )


def sent_kernel(at_ref, normed_ref, projected_ref, branch_ref, attended_ref, *out_refs):
    value = both_products(normed_ref, projected_ref, branch_ref, attended_ref)
    for block, out_ref in enumerate(out_refs):
        @pl.when(pl.program_id(0) == block)
        def _():
            out_ref[...] = value


def held_kernel(at_ref, normed_ref, projected_ref, branch_ref, attended_ref, *refs):
    block = pl.program_id(0)
    along_y, along_x = block // 2, lax.rem(block, 2)
    arrived_refs, out_refs = refs[:-4], refs[-4:]
    arrived = arrived_refs[0][...]
    for k, arrived_ref in enumerate(arrived_refs[1:], 1):
        arrived = jnp.where(block == k, arrived_ref[...], arrived)
    value = both_products(normed_ref, projected_ref, branch_ref, attended_ref) + arrived
    half = value.shape[1] // 2
    x_keep_ref, x_send_ref, y_keep_ref, y_send_ref = out_refs
    for same, index, columns, keep_ref, send_ref in (
        (along_x == at_ref[1], along_y, value[:, :half], x_keep_ref, x_send_ref),
        (along_y == at_ref[2], along_x, value[:, half:], y_keep_ref, y_send_ref),
    ):
        @pl.when(same)
        def _():
            keep_ref[index] = columns

        @pl.when(jnp.logical_not(same))
        def _():
            send_ref[index] = columns


def token_products(at, normed, projected, branch, attended, arrived):
    _, count, half = normed.shape
    blocks = BLOCKS // 2
    part = half // blocks
    cols = projected.shape[1] + attended.shape[1]
    side = pl.BlockSpec((1, count, part), lambda i, at: (at[0], 0, i))
    fixed = lambda *shape: pl.BlockSpec(shape, lambda i, at: (0,) * len(shape))
    inputs = [normed, projected, branch, attended]
    in_specs = [side, fixed(*projected.shape), side, fixed(*attended.shape)]
    if arrived is None:
        kernel, out_specs = sent_kernel, [fixed(part, cols)] * blocks
        out_shape = [jax.ShapeDtypeStruct((part, cols), F32)] * blocks
    else:
        kernel, out_specs = held_kernel, [fixed(2, part, cols // 2)] * 4
        out_shape = [jax.ShapeDtypeStruct((2, part, cols // 2), F32)] * 4
        inputs, in_specs = [*inputs, *arrived], [*in_specs, *[fixed(part, cols)] * blocks]
    return pl.pallas_call(
        kernel,
        grid_spec=pltpu.PrefetchScalarGridSpec(
            num_scalar_prefetch=1, grid=(blocks,), in_specs=in_specs, out_specs=out_specs
        ),
        out_shape=out_shape,
        compiler_params=pltpu.CompilerParams(
            dimension_semantics=("arbitrary",), vmem_limit_bytes=VMEM_LIMIT
        ),
        cost_estimate=LIGHT,
        name="token_products",
    )(at, *inputs)


def turn_kernel(at_ref, x_keep_ref, x_got_ref, y_keep_ref, y_got_ref, x_own_ref, x_send_ref, y_own_ref, y_send_ref):
    for mine, keep_ref, got_ref, own_ref, send_ref in (
        (at_ref[2], x_keep_ref, x_got_ref, x_own_ref, x_send_ref),
        (at_ref[1], y_keep_ref, y_got_ref, y_own_ref, y_send_ref),
    ):
        own_ref[...] = keep_ref[mine] + got_ref[mine]
        send_ref[...] = keep_ref[1 - mine] + got_ref[1 - mine]


def turned_blocks(at, x_keep, x_got, y_keep, y_got):
    _, part, cols = x_keep.shape
    rows = part // 4
    spec = pl.BlockSpec((2, rows, cols), lambda i, at: (0, i, 0))
    out = pl.BlockSpec((rows, cols), lambda i, at: (i, 0))
    return pl.pallas_call(
        turn_kernel,
        grid_spec=pltpu.PrefetchScalarGridSpec(
            num_scalar_prefetch=1, grid=(4,), in_specs=[spec] * 4, out_specs=[out] * 4
        ),
        out_shape=[jax.ShapeDtypeStruct((part, cols), F32)] * 4,
        compiler_params=pltpu.CompilerParams(
            dimension_semantics=("arbitrary",), vmem_limit_bytes=VMEM_LIMIT
        ),
        cost_estimate=LIGHT,
        name="turned_blocks",
    )(at, x_keep, x_got, y_keep, y_got)


def weights_kernel(here, at_ref, mix_grad_ref, weighted_ref, tok_ref, cot_ref, *refs):
    part = refs[0].shape[-1]
    expert_refs, shared_refs, peer_refs = refs[:2], refs[2:4], refs[4:]
    core, step = at_ref[0], pl.program_id(0)
    products = nn(mix_grad_ref[0], tok_ref[...]), nn(weighted_ref[0], cot_ref[...])
    for value, expert_ref, shared_ref, peer_ref in zip(products, expert_refs, shared_refs, peer_refs, strict=True):
        low, high = value[:, :part], value[:, part:]
        mine = jnp.where(core == 0, low, high)
        peer_ref[...] = jnp.where(core == 0, high, low).reshape(peer_ref.shape)

        @pl.when(step < here)
        def _():
            expert_ref[...] = mine.reshape(expert_ref.shape)

        @pl.when(step >= here)
        def _():
            shared_ref[...] = mine.reshape(shared_ref.shape)


def tile_specs(core_of, here, shared, units, part):
    expert = lambda i, at: core_of(at) * here + jnp.minimum(i, here - 1)
    common = lambda i, at: core_of(at) * shared + jnp.maximum(i - here, 0)
    return [
        pl.BlockSpec((1, 2, units, part), lambda i, at: (expert(i, at), 0, 0, 0)),
        pl.BlockSpec((1, units, part), lambda i, at: (expert(i, at), 0, 0)),
        pl.BlockSpec((1, 2, units, part), lambda i, at: (common(i, at), 0, 0, 0)),
        pl.BlockSpec((1, units, part), lambda i, at: (common(i, at), 0, 0)),
    ]


def weight_grads(at, mix_grads, weighted, tokens, cotangent, here):
    tiles, units, total = weighted.shape
    part = tokens.shape[1] // 2
    shared = tiles - here
    one = lambda count: jax.ShapeDtypeStruct((count, 2, units, part), F32)
    two = lambda count: jax.ShapeDtypeStruct((count, units, part), F32)
    return pl.pallas_call(
        functools.partial(weights_kernel, here),
        grid_spec=pltpu.PrefetchScalarGridSpec(
            num_scalar_prefetch=1,
            grid=(tiles,),
            in_specs=[
                pl.BlockSpec((1, 2 * units, total), lambda i, at: (i, 0, 0)),
                pl.BlockSpec((1, units, total), lambda i, at: (i, 0, 0)),
                pl.BlockSpec((total, 2 * part), lambda i, at: (0, 0)),
                pl.BlockSpec((total, 2 * part), lambda i, at: (0, at[3])),
            ],
            out_specs=[
                *tile_specs(lambda at: at[0], here, shared, units, part),
                pl.BlockSpec((1, 2, units, part), lambda i, at: (i, 0, 0, 0)),
                pl.BlockSpec((1, units, part), lambda i, at: (i, 0, 0)),
            ],
        ),
        out_shape=[one(2 * here), two(2 * here), one(2 * shared), two(2 * shared), one(tiles), two(tiles)],
        compiler_params=pltpu.CompilerParams(
            dimension_semantics=("arbitrary",), vmem_limit_bytes=VMEM_LIMIT
        ),
        cost_estimate=LIGHT,
        name="weight_grads",
    )(at, mix_grads, weighted, tokens, cotangent)


def place_kernel(here, at_ref, one_ref, two_ref, *refs):
    step = pl.program_id(0)
    expert_one_ref, expert_two_ref, shared_one_ref, shared_two_ref = refs[-4:]

    @pl.when(step < here)
    def _():
        expert_one_ref[...] = one_ref[...]
        expert_two_ref[...] = two_ref[...]

    @pl.when(step >= here)
    def _():
        shared_one_ref[...] = one_ref[...]
        shared_two_ref[...] = two_ref[...]


def place_peer(at, one, two, grads, here):
    tiles, units, part = two.shape
    return pl.pallas_call(
        functools.partial(place_kernel, here),
        grid_spec=pltpu.PrefetchScalarGridSpec(
            num_scalar_prefetch=1,
            grid=(tiles,),
            in_specs=[
                pl.BlockSpec((1, 2, units, part), lambda i, at: (i, 0, 0, 0)),
                pl.BlockSpec((1, units, part), lambda i, at: (i, 0, 0)),
                *[pl.BlockSpec(memory_space=pl.ANY)] * 4,
            ],
            out_specs=tile_specs(lambda at: 1 - at[0], here, tiles - here, units, part),
        ),
        out_shape=[jax.ShapeDtypeStruct(g.shape, g.dtype) for g in grads],
        input_output_aliases={3 + k: k for k in range(4)},
        compiler_params=pltpu.CompilerParams(
            dimension_semantics=("arbitrary",), vmem_limit_bytes=VMEM_LIMIT
        ),
        cost_estimate=LIGHT,
        name="place_peer",
    )(at, one, two, *grads)


def split_kernel(in_ref, out_ref, route_ref):
    count = out_ref.shape[0]
    out_ref[...] = in_ref[0, :count].astype(BF16)
    route_ref[...] = in_ref[0, count:, :count][None]


def split_rounded(gathered, count):
    blocks, rows, width = gathered.shape
    extra = rows - count
    return pl.pallas_call(
        split_kernel,
        grid=(blocks,),
        in_specs=[pl.BlockSpec((1, rows, width), lambda i: (i, 0, 0))],
        out_specs=[
            pl.BlockSpec((count, width), lambda i: (i, 0)),
            pl.BlockSpec((1, extra, count), lambda i: (i, 0, 0)),
        ],
        out_shape=[
            jax.ShapeDtypeStruct((blocks * count, width), BF16),
            jax.ShapeDtypeStruct((blocks, extra, count), F32),
        ],
        compiler_params=pltpu.CompilerParams(
            dimension_semantics=("arbitrary",), vmem_limit_bytes=VMEM_LIMIT
        ),
        name="split_rounded",
    )(gathered)


def flip(value, bit):
    return lax.ppermute(value, "dp", [(i, i ^ bit) for i in range(8)])


def take(value, number, axis):
    return lax.dynamic_index_in_dim(value, number, axis, keepdims=False)


def shards(
    n_dp,
    n_tensor,
    layer_input,
    doc_ids,
    expert_ids,
    route_weights,
    attn_gain,
    qkv_weight,
    qkv_bias,
    out_weight,
    mlp_gain,
    expert_gate_up,
    expert_down,
    shared_gate_up,
    shared_down,
    shared_gate,
    cotangent,
):
    count, width = layer_input.shape
    heads_here = qkv_bias.shape[0]
    head_dim = qkv_bias.shape[1] // 3
    experts, units = expert_down.shape[:2]
    shared = shared_down.shape[0] // units
    part = width // n_dp
    me = lax.axis_index("dp")
    core, chip = me % 2, me // 2
    tied = lax.optimization_barrier

    choose = expert_ids[:, :, None] == jnp.arange(experts, dtype=jnp.int32)[None, None, :]
    route = jnp.sum(route_weights[:, :, None] * choose.astype(F32), axis=1).T
    payload = jnp.concatenate([cotangent.astype(F32), jnp.pad(route, ((0, 0), (0, width - count)))], axis=0)
    cot_all = lax.all_gather(payload, "dp")
    gate_rows = jnp.broadcast_to(shared_gate[None, :], (16, width))
    index = jnp.arange(count, dtype=jnp.int32)
    place = (me * count + index - doc_ids).astype(F32)
    freq = ROPE_BASE ** (-(jnp.arange(head_dim // 2, dtype=F32) * 2.0 / head_dim))
    angle = place[:, None] * freq[None, :]
    cosine = jnp.concatenate([jnp.cos(angle), jnp.cos(angle)], axis=-1)
    sine = jnp.concatenate([-jnp.sin(angle), jnp.sin(angle)], axis=-1)
    row, col = doc_ids[None, :], doc_ids[:, None]
    gain_one = attn_gain.astype(F32)[None, :]
    gain_two = mlp_gain.astype(F32)[None, :]
    attn_part, normed_one, qkv, attended = attention(
        layer_input, gain_one, qkv_weight, qkv_bias.astype(F32)[:, None, :], cosine, sine, row, col, out_weight
    )

    attn_part, shared_gate_up = tied((attn_part, shared_gate_up))
    attn_sum = lax.psum(attn_part, "tensor")
    w1 = jnp.concatenate(
        [
            jnp.transpose(expert_gate_up, (0, 2, 3, 1)),
            jnp.transpose(shared_gate_up.reshape(width, 2, shared, units), (2, 1, 3, 0)),
        ]
    )
    w2 = jnp.concatenate([expert_down, shared_down.reshape(shared, units, width)])
    w1, cot_all = tied((w1, cot_all))
    attn_sum, w1, w2, cot_all = tied((attn_sum, w1, w2, cot_all))

    residual, tokens, tokens_wide = second_norm(layer_input, attn_sum, gain_two)
    swap = lambda v: lax.ppermute(v, "dp", [(i, i ^ 1) for i in range(n_dp)])
    beside = swap(tokens_wide)
    tok_all = lax.all_gather(tokens_wide, "dp")
    mlp_part, normed_two_part, logit_grad = own_mlp(tokens, cotangent, route, gate_rows, w1, w2)
    cot_all, logit_grad = tied((cot_all, logit_grad))
    cot_low, route_all = split_rounded(cot_all, count)
    hide = lambda other, starts, tokens, kept: chip_hidden(
        jnp.stack([core, chip, other, *starts]), tokens, cot_low, route_all, gate_rows, w1, w2, kept, part
    )
    in_order = (jnp.int32(0), jnp.int32(count))
    beside_starts = (core * count, (1 - core) * count)
    shared_gate_part = jnp.sum(logit_grad[0][:, None] * tokens.astype(F32), axis=0, keepdims=True)
    normed_two_total = lax.psum(normed_two_part, "tensor")
    last = n_dp == 8
    if last:
        ready = jnp.isnan(logit_grad[0, 0]).astype(jnp.int32)
        kept = hide(chip + ready, beside_starts, [tokens_wide, beside], [])
        kept = hide(chip ^ 1, in_order, [tok_all], kept)
        kept = hide(chip ^ 2, in_order, [tok_all], kept)
    else:
        kept = []
        for k in range(n_dp // 2):
            kept = hide(jnp.int32(k), in_order, [tok_all], kept)
    normed_two_total, shared_gate_part, kept = tied((normed_two_total, shared_gate_part, kept))
    mlp_sum = lax.psum_scatter(mlp_part, "tensor", scatter_dimension=0, tiled=True)

    normed_one_part, residual_grad, branch_grad, projected_grad, bias_part, mlp_gain_part = attention_back(
        normed_two_total, residual, cotangent, gain_two, out_weight, qkv, qkv_weight,
        cosine, sine, row, col, layer_input, shared_gate_part, n_tensor,
    )
    few = count // n_tensor
    summed = lax.psum_scatter(normed_one_part.reshape(-1, width), "tensor", scatter_dimension=0, tiled=True)
    own_rows = lambda v: lax.dynamic_slice_in_dim(v, lax.axis_index("tensor") * few, few, 0)

    def finish(summed):
        inputs = own_rows(layer_input).astype(F32)
        factor = lax.rsqrt(jnp.mean(inputs * inputs, axis=-1, keepdims=True) + EPS)
        bias_row = jnp.pad(bias_part, ((0, 0), (0, width - bias_part.shape[1])))
        small = jnp.concatenate([summed[few : few + 2], mlp_gain_part, bias_row])
        return norm_back(inputs, factor, gain_one, summed[:few]), jnp.pad(small, ((0, 4), (0, 0)))

    if last:
        at = jnp.stack([core, chip % 2, chip // 2, chip])
        other_at = jnp.stack([1 - core, chip % 2, chip // 2, chip])
        arrived = [swap(v) for v in token_products(other_at, normed_one, projected_grad, branch_grad, attended, None)]
        x_keep, x_send, y_keep, y_send = token_products(
            at, normed_one, projected_grad, branch_grad, attended, arrived
        )
        x_send, y_send, kept, mlp_sum = tied((x_send, y_send, kept, mlp_sum))
        x_got, y_got = flip(x_send, 2), flip(y_send, 4)
        kept = hide(chip ^ 3, in_order, [tok_all], kept)
        kept, summed = tied((kept, summed))
        back, small = finish(summed)
        back, kept = tied((back, kept))
        gathered = lax.all_gather(jnp.concatenate([back, mlp_sum]), "tensor")
        *grads, one_peer, two_peer = weight_grads(at, *kept, cot_low, experts // 2)
        one_peer, x_got, y_got = tied((one_peer, x_got, y_got))
        x_own, x_send, y_own, y_send = turned_blocks(at, x_keep, x_got, y_keep, y_got)
        x_send, y_send, one_peer, two_peer = tied((x_send, y_send, one_peer, two_peer))
        x_got, y_got = flip(x_send, 4), flip(y_send, 2)
        one_peer, two_peer = swap(one_peer), swap(two_peer)
        expert_one, expert_two, shared_one, shared_two = place_peer(at, one_peer, two_peer, grads, experts // 2)
        expert_one, small = tied((expert_one, small))
        for bit in (1, 2, 4):
            small = small + flip(small, bit)
        x_got, y_got, small, expert_one = tied((x_got, y_got, small, expert_one))
        both = jnp.concatenate([x_own + x_got, y_own + y_got], axis=1)
        cut = projected_grad.shape[1]
        qkv_weight_grad, out_weight_grad = both[:, :cut], both[:, cut:].T
        gathered, qkv_weight_grad = tied((gathered, qkv_weight_grad))
    else:
        at = jnp.stack([core, core, core, chip])
        *grads, one_peer, two_peer = weight_grads(at, *kept, cot_low, experts // 2)
        one_peer, two_peer = swap(one_peer), swap(two_peer)
        expert_one, expert_two, shared_one, shared_two = place_peer(at, one_peer, two_peer, grads, experts // 2)
        back, small = finish(summed)
        small = lax.psum(small, "dp")
        gathered = lax.all_gather(jnp.concatenate([back, mlp_sum]), "tensor")
        joint = lambda v: v.reshape(2, count, BLOCKS // 2, -1).transpose(1, 2, 0, 3).reshape(count, width)
        out_weight_grad = lax.psum_scatter(tn(attended, joint(branch_grad)), "dp", scatter_dimension=1, tiled=True)
        qkv_weight_grad = lax.psum_scatter(
            tn(joint(normed_one), projected_grad), "dp", scatter_dimension=0, tiled=True
        )

    attn_gain_grad, shared_gate_grad, mlp_gain_grad = lax.dynamic_slice(small, (0, me * part), (3, part))
    bias_cols = 3 * head_dim // n_dp
    bias = small[3, : heads_here * 3 * head_dim].reshape(heads_here, 3 * head_dim)
    qkv_bias_grad = lax.dynamic_slice(bias, (0, me * bias_cols), (heads_here, bias_cols))
    input_grad = (residual_grad + gathered[:, :few].reshape(count, width)).astype(BF16)
    layer_output = (residual + gathered[:, few:].reshape(count, width)).astype(BF16)

    expert_gate_up_grad = jnp.transpose(expert_one, (0, 3, 1, 2))
    shared_gate_up_grad = jnp.transpose(shared_one, (3, 1, 0, 2)).reshape(part, 2, shared * units)
    shared_down_grad = shared_two.reshape(shared * units, part)
    return (
        layer_output,
        input_grad,
        attn_gain_grad,
        qkv_weight_grad,
        qkv_bias_grad,
        out_weight_grad,
        mlp_gain_grad,
        expert_gate_up_grad,
        expert_two,
        shared_gate_up_grad,
        shared_down_grad,
        shared_gate_grad,
    )


def solution(mesh):
    placed = (
        P("dp", None),
        P("dp"),
        P("dp", None),
        P("dp", None),
        P(),
        P(None, "tensor"),
        P("tensor", None),
        P("tensor", None),
        P(),
        P(None, None, None, "tensor"),
        P(None, "tensor", None),
        P(None, None, "tensor"),
        P("tensor", None),
        P(),
        P("dp", None),
    )
    return jax.shard_map(
        functools.partial(shards, mesh.shape["dp"], mesh.shape["tensor"]),
        mesh=mesh,
        in_specs=placed,
        out_specs=(
            P("dp", None),
            P("dp", None),
            P("dp"),
            P("dp", "tensor"),
            P("tensor", "dp"),
            P("tensor", "dp"),
            P("dp"),
            P(None, "dp", None, "tensor"),
            P(None, "tensor", "dp"),
            P("dp", None, "tensor"),
            P("tensor", "dp"),
            P("dp"),
        ),
        check_vma=False,
    )
```

```python
import functools

import jax
import jax.numpy as jnp
from jax import lax
from jax.experimental import pallas as pl
from jax.experimental.pallas import tpu as pltpu
from jax.sharding import PartitionSpec as P

EPS = 1e-06
ROPE_BASE = 1000000.0
NEG = -1e30
F32 = jnp.float32
BF16 = jnp.bfloat16
VMEM_LIMIT = 60 * 1024 * 1024
BLOCKS = 8
LIGHT = pl.CostEstimate(flops=1 << 20, bytes_accessed=1 << 16, transcendentals=0)


def nt(left, right):
    return lax.dot_general(left, right, (((1,), (1,)), ((), ())), preferred_element_type=F32)


def tn(left, right):
    return lax.dot_general(left, right, (((0,), (0,)), ((), ())), preferred_element_type=F32)


def nn(left, right):
    return jnp.dot(left, right, preferred_element_type=F32)


def norm_back(values_in, factor, gain_vec, upstream):
    scaled = gain_vec * upstream
    inner = jnp.mean(scaled * values_in, axis=-1, keepdims=True)
    return factor * scaled - values_in * factor**3 * inner


def turned(values, cosine, sine):
    return values * cosine + pltpu.roll(values, values.shape[1] // 2, 1) * sine


def turned_back(values, cosine, sine):
    return values * cosine - pltpu.roll(values, values.shape[1] // 2, 1) * sine


def head_probs(queries, keys, row_ref, col_ref):
    count = queries.shape[0]
    scores = nt(queries, keys) * queries.shape[1] ** (-0.5)
    rows = lax.broadcasted_iota(jnp.int32, (count, count), 0)
    cols = lax.broadcasted_iota(jnp.int32, (count, count), 1)
    scores = jnp.where((col_ref[...] == row_ref[...]) & (cols <= rows), scores, NEG)
    exponent = jnp.exp(scores - jnp.max(scores, axis=-1, keepdims=True))
    return exponent / jnp.sum(exponent, axis=-1, keepdims=True)


def split_columns(whole_ref, split_ref):
    part = whole_ref.shape[1] // BLOCKS
    for k in range(BLOCKS):
        split_ref[k % 2, :, k // 2 * part : (k // 2 + 1) * part] = whole_ref[:, k * part : (k + 1) * part]


def attn_kernel(x_ref, gain_ref, weight_ref, bias_ref, cos_ref, sin_ref, row_ref, col_ref, out_weight_ref,
                part_ref, split_ref, qkv_ref, attended_ref, normed_ref):
    head = pl.program_id(0)
    dim = cos_ref.shape[1]

    @pl.when(head == 0)
    def _():
        values = x_ref[...].astype(F32)
        factor = lax.rsqrt(jnp.mean(values * values, axis=-1, keepdims=True) + EPS)
        normed_ref[...] = (values * factor * gain_ref[...]).astype(BF16)
        split_columns(normed_ref, split_ref)

    projected = nn(normed_ref[...], weight_ref[...]) + bias_ref[0]
    queries = turned(projected[:, :dim], cos_ref[...], sin_ref[...]).astype(BF16)
    keys = turned(projected[:, dim : 2 * dim], cos_ref[...], sin_ref[...]).astype(BF16)
    values = projected[:, 2 * dim :].astype(BF16)
    qkv_ref[:, :dim] = queries
    qkv_ref[:, dim : 2 * dim] = keys
    qkv_ref[:, 2 * dim :] = values
    probs = head_probs(queries, keys, row_ref, col_ref)
    cols = pl.ds(pl.multiple_of(head * dim, dim), dim)
    attended_ref[:, cols] = nn(probs.astype(BF16), values).astype(BF16)

    @pl.when(head == pl.num_programs(0) - 1)
    def _():
        part_ref[...] = nn(attended_ref[...], out_weight_ref[...])


def whole(*shape):
    return pl.BlockSpec(shape, lambda *at: (0,) * len(shape))


def attention(x, gain, weight, bias, cosine, sine, row, col, out_weight):
    count, width = x.shape
    heads, _, cols = bias.shape
    return pl.pallas_call(
        attn_kernel,
        grid=(heads,),
        in_specs=[
            whole(count, width),
            whole(1, width),
            pl.BlockSpec((width, cols), lambda h: (0, h)),
            pl.BlockSpec((1, 1, cols), lambda h: (h, 0, 0)),
            whole(*cosine.shape),
            whole(*sine.shape),
            whole(1, count),
            whole(count, 1),
            whole(*out_weight.shape),
        ],
        out_specs=[
            whole(count, width),
            whole(2, count, width // 2),
            pl.BlockSpec((count, cols), lambda h: (0, h)),
            whole(count, out_weight.shape[0]),
        ],
        out_shape=[
            jax.ShapeDtypeStruct((count, width), F32),
            jax.ShapeDtypeStruct((2, count, width // 2), BF16),
            jax.ShapeDtypeStruct((count, heads * cols), BF16),
            jax.ShapeDtypeStruct((count, out_weight.shape[0]), BF16),
        ],
        scratch_shapes=[pltpu.VMEM((count, width), BF16)],
        compiler_params=pltpu.CompilerParams(
            dimension_semantics=("arbitrary",), vmem_limit_bytes=VMEM_LIMIT
        ),
        cost_estimate=LIGHT,
        name="attention",
    )(x, gain, weight, bias, cosine, sine, row, col, out_weight)


def norm_kernel(x_ref, sum_ref, gain_ref, residual_ref, low_ref, wide_ref):
    residual = x_ref[...].astype(F32) + sum_ref[...]
    factor = lax.rsqrt(jnp.mean(residual * residual, axis=-1, keepdims=True) + EPS)
    low = (residual * factor * gain_ref[...]).astype(BF16)
    residual_ref[...] = residual
    low_ref[...] = low
    wide_ref[...] = low.astype(F32)


def second_norm(x, attn_sum, gain):
    count, width = x.shape
    rows = count // 4
    spec = pl.BlockSpec((rows, width), lambda i: (i, 0))
    return pl.pallas_call(
        norm_kernel,
        grid=(4,),
        in_specs=[spec, spec, whole(1, width)],
        out_specs=[spec, spec, spec],
        out_shape=[
            jax.ShapeDtypeStruct((count, width), F32),
            jax.ShapeDtypeStruct((count, width), BF16),
            jax.ShapeDtypeStruct((count, width), F32),
        ],
        compiler_params=pltpu.CompilerParams(
            dimension_semantics=("arbitrary",), vmem_limit_bytes=VMEM_LIMIT
        ),
        name="second_norm",
    )(x, attn_sum, gain)


def back_kernel(total_ref, residual_ref, cot_ref, gain_ref, out_weight_ref, qkv_ref, weight_ref, cos_ref, sin_ref,
                row_ref, col_ref, x_ref, extra_ref, normed_grad_ref, residual_grad_ref, split_ref, projected_grad_ref, bias_ref,
                mlp_gain_ref, branch_ref, attended_grad_ref):
    head = pl.program_id(0)
    dim = cos_ref.shape[1]

    @pl.when(head == 0)
    def _():
        total = total_ref[...]
        residual = residual_ref[...]
        factor = lax.rsqrt(jnp.mean(residual * residual, axis=-1, keepdims=True) + EPS)
        scaled = gain_ref[...] * total
        inner = jnp.mean(scaled * residual, axis=-1, keepdims=True)
        residual_grad = cot_ref[...].astype(F32) + (factor * scaled - residual * factor**3 * inner)
        residual_grad_ref[...] = residual_grad
        branch_ref[...] = residual_grad.astype(BF16)
        split_columns(branch_ref, split_ref)
        mlp_gain_ref[...] = jnp.sum(total * residual * factor, axis=0, keepdims=True)
        attended_grad = nt(branch_ref[...], out_weight_ref[...]).astype(BF16)
        for k in range(attended_grad_ref.shape[0]):
            attended_grad_ref[k] = attended_grad[:, k * dim : (k + 1) * dim]

    queries, keys, values = qkv_ref[:, :dim], qkv_ref[:, dim : 2 * dim], qkv_ref[:, 2 * dim :]
    attended_grad = attended_grad_ref[head]
    probs = head_probs(queries, keys, row_ref, col_ref)
    prob_grad = nt(attended_grad, values)
    inner = jnp.sum(probs * prob_grad, axis=-1, keepdims=True)
    score = (probs * (prob_grad - inner) * dim ** (-0.5)).astype(BF16)
    query_grad = nn(score, keys).astype(BF16).astype(F32)
    key_grad = tn(score, queries).astype(BF16).astype(F32)
    value_grad = tn(probs.astype(BF16), attended_grad)
    grad = jnp.concatenate(
        [
            turned_back(query_grad, cos_ref[...], sin_ref[...]).astype(BF16),
            turned_back(key_grad, cos_ref[...], sin_ref[...]).astype(BF16),
            value_grad.astype(BF16),
        ],
        axis=1,
    )
    projected_grad_ref[...] = grad
    bias_ref[...] = jnp.sum(grad.astype(F32), axis=0, keepdims=True)
    product = nt(grad, weight_ref[...])
    groups, few = normed_grad_ref.shape[0], normed_grad_ref.shape[1] - 8

    @pl.when(head == 0)
    def _():
        for k in range(groups):
            normed_grad_ref[k, :few] = product[k * few : (k + 1) * few]

    @pl.when(head > 0)
    def _():
        for k in range(groups):
            normed_grad_ref[k, :few] += product[k * few : (k + 1) * few]

    @pl.when(head == pl.num_programs(0) - 1)
    def _():
        total = jnp.zeros((1, x_ref.shape[1]), F32)
        for k in range(groups):
            x = x_ref[k * few : (k + 1) * few].astype(F32)
            factor = lax.rsqrt(jnp.mean(x * x, axis=-1, keepdims=True) + EPS)
            total += jnp.sum(normed_grad_ref[k, :few] * x * factor, axis=0, keepdims=True)
        rows = lax.broadcasted_iota(jnp.int32, (8, x_ref.shape[1]), 0)
        small = jnp.where(rows == 0, total, jnp.where(rows == 1, extra_ref[...], 0.0))
        for k in range(groups):
            normed_grad_ref[k, few:] = small


def attention_back(total, residual, cotangent, gain, out_weight, qkv, weight, cosine, sine, row, col, x, extra,
                   groups):
    count, width = residual.shape
    dim = cosine.shape[1]
    cols = 3 * dim
    heads = qkv.shape[1] // cols
    return pl.pallas_call(
        back_kernel,
        grid=(heads,),
        in_specs=[
            whole(count, width),
            whole(count, width),
            whole(count, width),
            whole(1, width),
            whole(*out_weight.shape),
            pl.BlockSpec((count, cols), lambda h: (0, h)),
            pl.BlockSpec((width, cols), lambda h: (0, h)),
            whole(*cosine.shape),
            whole(*sine.shape),
            whole(1, count),
            whole(count, 1),
            whole(count, width),
            whole(1, width),
        ],
        out_specs=[
            whole(groups, count // groups + 8, width),
            whole(count, width),
            whole(2, count, width // 2),
            pl.BlockSpec((count, cols), lambda h: (0, h)),
            pl.BlockSpec((1, cols), lambda h: (0, h)),
            whole(1, width),
        ],
        out_shape=[
            jax.ShapeDtypeStruct((groups, count // groups + 8, width), F32),
            jax.ShapeDtypeStruct((count, width), F32),
            jax.ShapeDtypeStruct((2, count, width // 2), BF16),
            jax.ShapeDtypeStruct((count, heads * cols), BF16),
            jax.ShapeDtypeStruct((1, heads * cols), F32),
            jax.ShapeDtypeStruct((1, width), F32),
        ],
        scratch_shapes=[pltpu.VMEM((count, width), BF16), pltpu.VMEM((heads, count, dim), BF16)],
        compiler_params=pltpu.CompilerParams(
            dimension_semantics=("arbitrary",), vmem_limit_bytes=VMEM_LIMIT
        ),
        cost_estimate=LIGHT,
        name="attention_back",
    )(total, residual, cotangent, gain, out_weight, qkv, weight, cosine, sine, row, col, x, extra)


def hidden(w_one, w_two, tokens, branch, route_row):
    units = w_two.shape[0]
    mix = nt(w_one, tokens)
    gate, up = mix[:units], mix[units:]
    back = nt(w_two, branch)
    sigma = lax.logistic(gate)
    silu = gate * sigma
    act = silu * up
    scaled = back * route_row
    gate_grad = scaled * up * (sigma + silu * (1.0 - sigma))
    mix_grad = jnp.concatenate([gate_grad.astype(BF16), (scaled * silu).astype(BF16)], axis=0)
    return act, back, (act * route_row).astype(BF16), mix_grad


def open_row(gate_rows, tokens):
    return lax.logistic(nt(gate_rows, tokens)[:1])


def own_kernel(experts, tok_ref, cot_ref, route_ref, gate_ref, w1_ref, w2_ref, out_ref, dx_ref, logit_ref,
               open_ref):
    step = pl.program_id(0)
    group, units, width = w2_ref.shape
    shared = step * group >= experts

    @pl.when(step == 0)
    def _():
        for ref in (out_ref, dx_ref):
            ref[...] = jnp.zeros_like(ref)
        logit_ref[...] = jnp.zeros_like(logit_ref)
        open_ref[...] = open_row(gate_ref[...], tok_ref[...])

    weighted, mix_grads = [], []
    for k in range(group):
        act, back, scaled, mix_grad = hidden(
            w1_ref[k].reshape(2 * units, width),
            w2_ref[k],
            tok_ref[...],
            cot_ref[...],
            jnp.where(shared, open_ref[...], route_ref[k]),
        )
        weighted.append(scaled)
        mix_grads.append(mix_grad)
        logit_ref[...] += jnp.where(shared, jnp.sum(act * back, axis=0, keepdims=True), 0.0)
    out_ref[...] += tn(jnp.concatenate(weighted), w2_ref[...].reshape(group * units, width))
    dx_ref[...] += tn(jnp.concatenate(mix_grads), w1_ref[...].reshape(group * 2 * units, width))

    @pl.when(step == pl.num_programs(0) - 1)
    def _():
        opened = open_ref[...]
        logit = opened * (1.0 - opened) * logit_ref[...]
        logit_ref[...] = logit
        column = jnp.broadcast_to(logit, (8, logit.shape[1])).T[:, :1]
        dx_ref[...] += column * gate_ref[:1].astype(F32)


def own_mlp(tokens, cotangent, route, gate_rows, w1, w2):
    count, width = tokens.shape
    tiles, units = w2.shape[:2]
    experts = route.shape[0]
    group = 2
    return pl.pallas_call(
        functools.partial(own_kernel, experts),
        grid=(tiles // group,),
        in_specs=[
            whole(count, width),
            whole(count, width),
            pl.BlockSpec((group, 1, count), lambda i: (jnp.minimum(i, experts // group - 1), 0, 0)),
            whole(*gate_rows.shape),
            pl.BlockSpec((group, 2, units, width), lambda i: (i, 0, 0, 0)),
            pl.BlockSpec((group, units, width), lambda i: (i, 0, 0)),
        ],
        out_specs=[whole(count, width), whole(count, width), whole(1, count)],
        out_shape=[
            jax.ShapeDtypeStruct((count, width), F32),
            jax.ShapeDtypeStruct((count, width), F32),
            jax.ShapeDtypeStruct((1, count), F32),
        ],
        scratch_shapes=[pltpu.VMEM((1, count), F32)],
        compiler_params=pltpu.CompilerParams(
            dimension_semantics=("arbitrary",), vmem_limit_bytes=VMEM_LIMIT
        ),
        cost_estimate=LIGHT,
        name="own_mlp",
    )(tokens, cotangent, route[:, None, :], gate_rows, w1, w2)


def chip_kernel(here, at_ref, even_ref, odd_ref, cot_ref, route_ref, gate_ref, w1_ref, w2_ref, *refs):
    mix_grad_ref, weighted_ref, part_ref, tok_ref, open_ref = refs[-5:]
    step = pl.program_id(0)
    units, width = w2_ref.shape[-2:]
    cores, experts, count = route_ref.shape
    core = at_ref[0]

    @pl.when(step == 0)
    def _():
        for start, ref in ((at_ref[3], even_ref), (at_ref[4], odd_ref)):
            tok_ref[pl.ds(pl.multiple_of(start, count), count), :] = ref[...].reshape(count, width).astype(BF16)
        part = part_ref.shape[1]
        part_ref[...] = tok_ref[:, pl.ds(pl.multiple_of(at_ref[1] * part, part), part)]
        open_ref[...] = open_row(gate_ref[...], tok_ref[...])

    expert = jnp.minimum(core * here + step, experts - 1)
    route_row = jnp.concatenate([route_ref[k, pl.ds(expert, 1), :] for k in range(cores)], axis=1)
    _, _, weighted, mix_grad = hidden(
        w1_ref[...].reshape(2 * units, width),
        w2_ref[0],
        tok_ref[...],
        cot_ref[...],
        jnp.where(step >= here, open_ref[...], route_row),
    )
    mix_grad_ref[0] = mix_grad
    weighted_ref[0] = weighted


def chip_hidden(at, tokens, cotangent, route, gate_rows, w1, w2, kept, part):
    total, width = cotangent.shape
    tiles, units = w2.shape[:2]
    experts, count = route.shape[1:]
    here, shared = experts // 2, (tiles - experts) // 2
    rows = 2 * count
    own = lambda i, at: jnp.where(i < here, at[0] * here + i, experts + at[0] * shared + i - here)
    fixed = lambda *shape: pl.BlockSpec(shape, lambda i, at: (0,) * len(shape))
    if len(tokens) == 2:
        sources = [fixed(count, width), fixed(count, width)]
    else:
        tokens = [tokens[0], tokens[0]]
        sources = [
            pl.BlockSpec((1, count, width), lambda i, at: (2 * at[2], 0, 0)),
            pl.BlockSpec((1, count, width), lambda i, at: (2 * at[2] + 1, 0, 0)),
        ]
    shapes = [
        jax.ShapeDtypeStruct((here + shared, 2 * units, total), BF16),
        jax.ShapeDtypeStruct((here + shared, units, total), BF16),
        jax.ShapeDtypeStruct((total, 2 * part), BF16),
    ]
    inputs = [*tokens, cotangent, route, gate_rows, w1, w2]
    return pl.pallas_call(
        functools.partial(chip_kernel, here),
        grid_spec=pltpu.PrefetchScalarGridSpec(
            num_scalar_prefetch=1,
            grid=(here + shared,),
            in_specs=[
                *sources,
                pl.BlockSpec((rows, width), lambda i, at: (at[2], 0)),
                pl.BlockSpec((2, experts, count), lambda i, at: (at[2], 0, 0)),
                fixed(*gate_rows.shape),
                pl.BlockSpec((1, 2, units, width), lambda i, at: (own(i, at), 0, 0, 0)),
                pl.BlockSpec((1, units, width), lambda i, at: (own(i, at), 0, 0)),
                *[pl.BlockSpec(memory_space=pl.ANY) for _ in kept],
            ],
            out_specs=[
                pl.BlockSpec((1, 2 * units, rows), lambda i, at: (i, 0, at[2])),
                pl.BlockSpec((1, units, rows), lambda i, at: (i, 0, at[2])),
                pl.BlockSpec((rows, 2 * part), lambda i, at: (at[2], 0)),
            ],
            scratch_shapes=[pltpu.VMEM((rows, width), BF16), pltpu.VMEM((1, rows), F32)],
        ),
        out_shape=shapes,
        input_output_aliases={1 + len(inputs) + k: k for k in range(len(kept))},
        compiler_params=pltpu.CompilerParams(
            dimension_semantics=("arbitrary",), vmem_limit_bytes=VMEM_LIMIT
        ),
        cost_estimate=LIGHT,
        name="chip_hidden",
    )(at, *inputs, *kept)


def both_products(normed_ref, projected_ref, branch_ref, attended_ref):
    return jnp.concatenate(
        [tn(normed_ref[0], projected_ref[...]), tn(branch_ref[0], attended_ref[...])], axis=1
    )


def sent_kernel(at_ref, normed_ref, projected_ref, branch_ref, attended_ref, *out_refs):
    value = both_products(normed_ref, projected_ref, branch_ref, attended_ref)
    for block, out_ref in enumerate(out_refs):
        @pl.when(pl.program_id(0) == block)
        def _():
            out_ref[...] = value


def held_kernel(at_ref, normed_ref, projected_ref, branch_ref, attended_ref, *refs):
    block = pl.program_id(0)
    along_y, along_x = block // 2, lax.rem(block, 2)
    arrived_refs, out_refs = refs[:-4], refs[-4:]
    arrived = arrived_refs[0][...]
    for k, arrived_ref in enumerate(arrived_refs[1:], 1):
        arrived = jnp.where(block == k, arrived_ref[...], arrived)
    value = both_products(normed_ref, projected_ref, branch_ref, attended_ref) + arrived
    half = value.shape[1] // 2
    x_keep_ref, x_send_ref, y_keep_ref, y_send_ref = out_refs
    for same, index, columns, keep_ref, send_ref in (
        (along_x == at_ref[1], along_y, value[:, :half], x_keep_ref, x_send_ref),
        (along_y == at_ref[2], along_x, value[:, half:], y_keep_ref, y_send_ref),
    ):
        @pl.when(same)
        def _():
            keep_ref[index] = columns

        @pl.when(jnp.logical_not(same))
        def _():
            send_ref[index] = columns


def token_products(at, normed, projected, branch, attended, arrived):
    _, count, half = normed.shape
    blocks = BLOCKS // 2
    part = half // blocks
    cols = projected.shape[1] + attended.shape[1]
    side = pl.BlockSpec((1, count, part), lambda i, at: (at[0], 0, i))
    fixed = lambda *shape: pl.BlockSpec(shape, lambda i, at: (0,) * len(shape))
    inputs = [normed, projected, branch, attended]
    in_specs = [side, fixed(*projected.shape), side, fixed(*attended.shape)]
    if arrived is None:
        kernel, out_specs = sent_kernel, [fixed(part, cols)] * blocks
        out_shape = [jax.ShapeDtypeStruct((part, cols), F32)] * blocks
    else:
        kernel, out_specs = held_kernel, [fixed(2, part, cols // 2)] * 4
        out_shape = [jax.ShapeDtypeStruct((2, part, cols // 2), F32)] * 4
        inputs, in_specs = [*inputs, *arrived], [*in_specs, *[fixed(part, cols)] * blocks]
    return pl.pallas_call(
        kernel,
        grid_spec=pltpu.PrefetchScalarGridSpec(
            num_scalar_prefetch=1, grid=(blocks,), in_specs=in_specs, out_specs=out_specs
        ),
        out_shape=out_shape,
        compiler_params=pltpu.CompilerParams(
            dimension_semantics=("arbitrary",), vmem_limit_bytes=VMEM_LIMIT
        ),
        cost_estimate=LIGHT,
        name="token_products",
    )(at, *inputs)


def turn_kernel(at_ref, x_keep_ref, x_got_ref, y_keep_ref, y_got_ref, x_own_ref, x_send_ref, y_own_ref, y_send_ref):
    for mine, keep_ref, got_ref, own_ref, send_ref in (
        (at_ref[2], x_keep_ref, x_got_ref, x_own_ref, x_send_ref),
        (at_ref[1], y_keep_ref, y_got_ref, y_own_ref, y_send_ref),
    ):
        own_ref[...] = keep_ref[mine] + got_ref[mine]
        send_ref[...] = keep_ref[1 - mine] + got_ref[1 - mine]


def turned_blocks(at, x_keep, x_got, y_keep, y_got):
    _, part, cols = x_keep.shape
    rows = part // 4
    spec = pl.BlockSpec((2, rows, cols), lambda i, at: (0, i, 0))
    out = pl.BlockSpec((rows, cols), lambda i, at: (i, 0))
    return pl.pallas_call(
        turn_kernel,
        grid_spec=pltpu.PrefetchScalarGridSpec(
            num_scalar_prefetch=1, grid=(4,), in_specs=[spec] * 4, out_specs=[out] * 4
        ),
        out_shape=[jax.ShapeDtypeStruct((part, cols), F32)] * 4,
        compiler_params=pltpu.CompilerParams(
            dimension_semantics=("arbitrary",), vmem_limit_bytes=VMEM_LIMIT
        ),
        cost_estimate=LIGHT,
        name="turned_blocks",
    )(at, x_keep, x_got, y_keep, y_got)


def weights_kernel(here, at_ref, mix_grad_ref, weighted_ref, tok_ref, cot_ref, *refs):
    part = refs[0].shape[-1]
    expert_refs, shared_refs, peer_refs = refs[:2], refs[2:4], refs[4:]
    core, step = at_ref[0], pl.program_id(0)
    products = nn(mix_grad_ref[0], tok_ref[...]), nn(weighted_ref[0], cot_ref[...])
    for value, expert_ref, shared_ref, peer_ref in zip(products, expert_refs, shared_refs, peer_refs, strict=True):
        low, high = value[:, :part], value[:, part:]
        mine = jnp.where(core == 0, low, high)
        peer_ref[...] = jnp.where(core == 0, high, low).reshape(peer_ref.shape)

        @pl.when(step < here)
        def _():
            expert_ref[...] = mine.reshape(expert_ref.shape)

        @pl.when(step >= here)
        def _():
            shared_ref[...] = mine.reshape(shared_ref.shape)


def tile_specs(core_of, here, shared, units, part):
    expert = lambda i, at: core_of(at) * here + jnp.minimum(i, here - 1)
    common = lambda i, at: core_of(at) * shared + jnp.maximum(i - here, 0)
    return [
        pl.BlockSpec((1, 2, units, part), lambda i, at: (expert(i, at), 0, 0, 0)),
        pl.BlockSpec((1, units, part), lambda i, at: (expert(i, at), 0, 0)),
        pl.BlockSpec((1, 2, units, part), lambda i, at: (common(i, at), 0, 0, 0)),
        pl.BlockSpec((1, units, part), lambda i, at: (common(i, at), 0, 0)),
    ]


def weight_grads(at, mix_grads, weighted, tokens, cotangent, here):
    tiles, units, total = weighted.shape
    part = tokens.shape[1] // 2
    shared = tiles - here
    one = lambda count: jax.ShapeDtypeStruct((count, 2, units, part), F32)
    two = lambda count: jax.ShapeDtypeStruct((count, units, part), F32)
    return pl.pallas_call(
        functools.partial(weights_kernel, here),
        grid_spec=pltpu.PrefetchScalarGridSpec(
            num_scalar_prefetch=1,
            grid=(tiles,),
            in_specs=[
                pl.BlockSpec((1, 2 * units, total), lambda i, at: (i, 0, 0)),
                pl.BlockSpec((1, units, total), lambda i, at: (i, 0, 0)),
                pl.BlockSpec((total, 2 * part), lambda i, at: (0, 0)),
                pl.BlockSpec((total, 2 * part), lambda i, at: (0, at[3])),
            ],
            out_specs=[
                *tile_specs(lambda at: at[0], here, shared, units, part),
                pl.BlockSpec((1, 2, units, part), lambda i, at: (i, 0, 0, 0)),
                pl.BlockSpec((1, units, part), lambda i, at: (i, 0, 0)),
            ],
        ),
        out_shape=[one(2 * here), two(2 * here), one(2 * shared), two(2 * shared), one(tiles), two(tiles)],
        compiler_params=pltpu.CompilerParams(
            dimension_semantics=("arbitrary",), vmem_limit_bytes=VMEM_LIMIT
        ),
        cost_estimate=LIGHT,
        name="weight_grads",
    )(at, mix_grads, weighted, tokens, cotangent)


def place_kernel(here, at_ref, one_ref, two_ref, *refs):
    step = pl.program_id(0)
    expert_one_ref, expert_two_ref, shared_one_ref, shared_two_ref = refs[-4:]

    @pl.when(step < here)
    def _():
        expert_one_ref[...] = one_ref[...]
        expert_two_ref[...] = two_ref[...]

    @pl.when(step >= here)
    def _():
        shared_one_ref[...] = one_ref[...]
        shared_two_ref[...] = two_ref[...]


def place_peer(at, one, two, grads, here):
    tiles, units, part = two.shape
    return pl.pallas_call(
        functools.partial(place_kernel, here),
        grid_spec=pltpu.PrefetchScalarGridSpec(
            num_scalar_prefetch=1,
            grid=(tiles,),
            in_specs=[
                pl.BlockSpec((1, 2, units, part), lambda i, at: (i, 0, 0, 0)),
                pl.BlockSpec((1, units, part), lambda i, at: (i, 0, 0)),
                *[pl.BlockSpec(memory_space=pl.ANY)] * 4,
            ],
            out_specs=tile_specs(lambda at: 1 - at[0], here, tiles - here, units, part),
        ),
        out_shape=[jax.ShapeDtypeStruct(g.shape, g.dtype) for g in grads],
        input_output_aliases={3 + k: k for k in range(4)},
        compiler_params=pltpu.CompilerParams(
            dimension_semantics=("arbitrary",), vmem_limit_bytes=VMEM_LIMIT
        ),
        cost_estimate=LIGHT,
        name="place_peer",
    )(at, one, two, *grads)


def split_kernel(in_ref, out_ref, route_ref):
    count = out_ref.shape[0]
    out_ref[...] = in_ref[0, :count].astype(BF16)
    route_ref[...] = in_ref[0, count:, :count][None]


def split_rounded(gathered, count):
    blocks, rows, width = gathered.shape
    extra = rows - count
    return pl.pallas_call(
        split_kernel,
        grid=(blocks,),
        in_specs=[pl.BlockSpec((1, rows, width), lambda i: (i, 0, 0))],
        out_specs=[
            pl.BlockSpec((count, width), lambda i: (i, 0)),
            pl.BlockSpec((1, extra, count), lambda i: (i, 0, 0)),
        ],
        out_shape=[
            jax.ShapeDtypeStruct((blocks * count, width), BF16),
            jax.ShapeDtypeStruct((blocks, extra, count), F32),
        ],
        compiler_params=pltpu.CompilerParams(
            dimension_semantics=("arbitrary",), vmem_limit_bytes=VMEM_LIMIT
        ),
        name="split_rounded",
    )(gathered)


def flip(value, bit):
    return lax.ppermute(value, "dp", [(i, i ^ bit) for i in range(8)])


def take(value, number, axis):
    return lax.dynamic_index_in_dim(value, number, axis, keepdims=False)


def shards(
    n_dp,
    n_tensor,
    layer_input,
    doc_ids,
    expert_ids,
    route_weights,
    attn_gain,
    qkv_weight,
    qkv_bias,
    out_weight,
    mlp_gain,
    expert_gate_up,
    expert_down,
    shared_gate_up,
    shared_down,
    shared_gate,
    cotangent,
):
    count, width = layer_input.shape
    heads_here = qkv_bias.shape[0]
    head_dim = qkv_bias.shape[1] // 3
    experts, units = expert_down.shape[:2]
    shared = shared_down.shape[0] // units
    part = width // n_dp
    me = lax.axis_index("dp")
    core, chip = me % 2, me // 2
    tied = lax.optimization_barrier

    choose = expert_ids[:, :, None] == jnp.arange(experts, dtype=jnp.int32)[None, None, :]
    route = jnp.sum(route_weights[:, :, None] * choose.astype(F32), axis=1).T
    payload = jnp.concatenate([cotangent.astype(F32), jnp.pad(route, ((0, 0), (0, width - count)))], axis=0)
    cot_all = lax.all_gather(payload, "dp")
    gate_rows = jnp.broadcast_to(shared_gate[None, :], (16, width))
    index = jnp.arange(count, dtype=jnp.int32)
    place = (me * count + index - doc_ids).astype(F32)
    freq = ROPE_BASE ** (-(jnp.arange(head_dim // 2, dtype=F32) * 2.0 / head_dim))
    angle = place[:, None] * freq[None, :]
    cosine = jnp.concatenate([jnp.cos(angle), jnp.cos(angle)], axis=-1)
    sine = jnp.concatenate([-jnp.sin(angle), jnp.sin(angle)], axis=-1)
    row, col = doc_ids[None, :], doc_ids[:, None]
    gain_one = attn_gain.astype(F32)[None, :]
    gain_two = mlp_gain.astype(F32)[None, :]
    attn_part, normed_one, qkv, attended = attention(
        layer_input, gain_one, qkv_weight, qkv_bias.astype(F32)[:, None, :], cosine, sine, row, col, out_weight
    )

    attn_part, shared_gate_up = tied((attn_part, shared_gate_up))
    attn_sum = lax.psum(attn_part, "tensor")
    w1 = jnp.concatenate(
        [
            jnp.transpose(expert_gate_up, (0, 2, 3, 1)),
            jnp.transpose(shared_gate_up.reshape(width, 2, shared, units), (2, 1, 3, 0)),
        ]
    )
    w2 = jnp.concatenate([expert_down, shared_down.reshape(shared, units, width)])
    w1, cot_all = tied((w1, cot_all))
    attn_sum, w1, w2, cot_all = tied((attn_sum, w1, w2, cot_all))

    residual, tokens, tokens_wide = second_norm(layer_input, attn_sum, gain_two)
    swap = lambda v: lax.ppermute(v, "dp", [(i, i ^ 1) for i in range(n_dp)])
    beside = swap(tokens_wide)
    tok_all = lax.all_gather(tokens_wide, "dp")
    mlp_part, normed_two_part, logit_grad = own_mlp(tokens, cotangent, route, gate_rows, w1, w2)
    cot_all, logit_grad = tied((cot_all, logit_grad))
    cot_low, route_all = split_rounded(cot_all, count)
    hide = lambda other, starts, tokens, kept: chip_hidden(
        jnp.stack([core, chip, other, *starts]), tokens, cot_low, route_all, gate_rows, w1, w2, kept, part
    )
    in_order = (jnp.int32(0), jnp.int32(count))
    beside_starts = (core * count, (1 - core) * count)
    shared_gate_part = jnp.sum(logit_grad[0][:, None] * tokens.astype(F32), axis=0, keepdims=True)
    normed_two_total = lax.psum(normed_two_part, "tensor")
    last = n_dp == 8
    if last:
        ready = jnp.isnan(logit_grad[0, 0]).astype(jnp.int32)
        kept = hide(chip + ready, beside_starts, [tokens_wide, beside], [])
        kept = hide(chip ^ 1, in_order, [tok_all], kept)
        kept = hide(chip ^ 2, in_order, [tok_all], kept)
    else:
        kept = []
        for k in range(n_dp // 2):
            kept = hide(jnp.int32(k), in_order, [tok_all], kept)
    normed_two_total, shared_gate_part, kept = tied((normed_two_total, shared_gate_part, kept))
    mlp_sum = lax.psum_scatter(mlp_part, "tensor", scatter_dimension=0, tiled=True)

    normed_one_part, residual_grad, branch_grad, projected_grad, bias_part, mlp_gain_part = attention_back(
        normed_two_total, residual, cotangent, gain_two, out_weight, qkv, qkv_weight,
        cosine, sine, row, col, layer_input, shared_gate_part, n_tensor,
    )
    few = count // n_tensor
    summed = lax.psum_scatter(normed_one_part.reshape(-1, width), "tensor", scatter_dimension=0, tiled=True)
    own_rows = lambda v: lax.dynamic_slice_in_dim(v, lax.axis_index("tensor") * few, few, 0)

    def finish(summed):
        inputs = own_rows(layer_input).astype(F32)
        factor = lax.rsqrt(jnp.mean(inputs * inputs, axis=-1, keepdims=True) + EPS)
        bias_row = jnp.pad(bias_part, ((0, 0), (0, width - bias_part.shape[1])))
        small = jnp.concatenate([summed[few : few + 2], mlp_gain_part, bias_row])
        return norm_back(inputs, factor, gain_one, summed[:few]), jnp.pad(small, ((0, 4), (0, 0)))

    if last:
        at = jnp.stack([core, chip % 2, chip // 2, chip])
        other_at = jnp.stack([1 - core, chip % 2, chip // 2, chip])
        arrived = [swap(v) for v in token_products(other_at, normed_one, projected_grad, branch_grad, attended, None)]
        x_keep, x_send, y_keep, y_send = token_products(
            at, normed_one, projected_grad, branch_grad, attended, arrived
        )
        x_send, y_send, kept, mlp_sum = tied((x_send, y_send, kept, mlp_sum))
        x_got, y_got = flip(x_send, 2), flip(y_send, 4)
        kept = hide(chip ^ 3, in_order, [tok_all], kept)
        kept, summed = tied((kept, summed))
        back, small = finish(summed)
        back, kept = tied((back, kept))
        mlp_sum = lax.all_gather(mlp_sum, "tensor", axis=0, tiled=True)
        back = lax.all_gather(back, "tensor", axis=0, tiled=True)
        *grads, one_peer, two_peer = weight_grads(at, *kept, cot_low, experts // 2)
        one_peer, x_got, y_got = tied((one_peer, x_got, y_got))
        x_own, x_send, y_own, y_send = turned_blocks(at, x_keep, x_got, y_keep, y_got)
        x_send, y_send, one_peer, two_peer = tied((x_send, y_send, one_peer, two_peer))
        x_got, y_got = flip(x_send, 4), flip(y_send, 2)
        one_peer, two_peer = swap(one_peer), swap(two_peer)
        expert_one, expert_two, shared_one, shared_two = place_peer(at, one_peer, two_peer, grads, experts // 2)
        expert_one, small = tied((expert_one, small))
        for bit in (1, 2, 4):
            small = small + flip(small, bit)
        x_got, y_got, small, expert_one = tied((x_got, y_got, small, expert_one))
        both = jnp.concatenate([x_own + x_got, y_own + y_got], axis=1)
        cut = projected_grad.shape[1]
        qkv_weight_grad, out_weight_grad = both[:, :cut], both[:, cut:].T
        mlp_sum, qkv_weight_grad = tied((mlp_sum, qkv_weight_grad))
    else:
        at = jnp.stack([core, core, core, chip])
        *grads, one_peer, two_peer = weight_grads(at, *kept, cot_low, experts // 2)
        one_peer, two_peer = swap(one_peer), swap(two_peer)
        expert_one, expert_two, shared_one, shared_two = place_peer(at, one_peer, two_peer, grads, experts // 2)
        back, small = finish(summed)
        small = lax.psum(small, "dp")
        mlp_sum = lax.all_gather(mlp_sum, "tensor", axis=0, tiled=True)
        back = lax.all_gather(back, "tensor", axis=0, tiled=True)
        joint = lambda v: v.reshape(2, count, BLOCKS // 2, -1).transpose(1, 2, 0, 3).reshape(count, width)
        out_weight_grad = lax.psum_scatter(tn(attended, joint(branch_grad)), "dp", scatter_dimension=1, tiled=True)
        qkv_weight_grad = lax.psum_scatter(
            tn(joint(normed_one), projected_grad), "dp", scatter_dimension=0, tiled=True
        )

    attn_gain_grad, shared_gate_grad, mlp_gain_grad = lax.dynamic_slice(small, (0, me * part), (3, part))
    bias_cols = 3 * head_dim // n_dp
    bias = small[3, : heads_here * 3 * head_dim].reshape(heads_here, 3 * head_dim)
    qkv_bias_grad = lax.dynamic_slice(bias, (0, me * bias_cols), (heads_here, bias_cols))
    layer_output = (residual + mlp_sum).astype(BF16)
    back, layer_output = tied((back, layer_output))
    input_grad = (residual_grad + back).astype(BF16)

    expert_gate_up_grad = jnp.transpose(expert_one, (0, 3, 1, 2))
    shared_gate_up_grad = jnp.transpose(shared_one, (3, 1, 0, 2)).reshape(part, 2, shared * units)
    shared_down_grad = shared_two.reshape(shared * units, part)
    return (
        layer_output,
        input_grad,
        attn_gain_grad,
        qkv_weight_grad,
        qkv_bias_grad,
        out_weight_grad,
        mlp_gain_grad,
        expert_gate_up_grad,
        expert_two,
        shared_gate_up_grad,
        shared_down_grad,
        shared_gate_grad,
    )


def solution(mesh):
    placed = (
        P("dp", None),
        P("dp"),
        P("dp", None),
        P("dp", None),
        P(),
        P(None, "tensor"),
        P("tensor", None),
        P("tensor", None),
        P(),
        P(None, None, None, "tensor"),
        P(None, "tensor", None),
        P(None, None, "tensor"),
        P("tensor", None),
        P(),
        P("dp", None),
    )
    return jax.shard_map(
        functools.partial(shards, mesh.shape["dp"], mesh.shape["tensor"]),
        mesh=mesh,
        in_specs=placed,
        out_specs=(
            P("dp", None),
            P("dp", None),
            P("dp"),
            P("dp", "tensor"),
            P("tensor", "dp"),
            P("tensor", "dp"),
            P("dp"),
            P(None, "dp", None, "tensor"),
            P(None, "tensor", "dp"),
            P("dp", None, "tensor"),
            P("tensor", "dp"),
            P("dp"),
        ),
        check_vma=False,
    )
```
